32 devices in a mesh: lat: 4 (over x, core), lon: 8 (over z, y).
Axes of the slice: x: 2, y: 2, z: 4, core: 2. Of those that a mesh axis runs over, the one named last changes fastest.
Arguments:
- queries: bfloat16 [32, 128, 512], P('lat', 'lon'), may hold values from -180 to 180
- key_cells: bfloat16 [32, 128, 512], P('lat', 'lon'), may hold values from -15 to 15
- value_cells: bfloat16 [32, 128, 512], P('lat', 'lon'), may hold values from -5 to 5
- grad_output: bfloat16 [32, 128, 512], P('lat', 'lon'), may hold values from -5 to 5
- rel_bias: float32 [8, 169], replicated, may hold values from -4 to 4
Outputs:
- output: bfloat16 [32, 128, 512], P('lat', 'lon')
- grad_query: bfloat16 [32, 128, 512], P('lat', 'lon')
- grad_key: bfloat16 [32, 128, 512], P('lat', 'lon')
- grad_value: bfloat16 [32, 128, 512], P('lat', 'lon')
The draws below stay inside these ranges and needn't reach their ends.
All inputs are finite; a program needn't handle non-finite values.
Results may differ from the reference program's by a relative error of at most 0.009.
Values may be sent and summed in bfloat16 or wider, within the bound.
No kernel may reach another device: no remote copies, remote signals or barrier semaphores. Data moves between devices by JAX's collectives and lax.ppermute only.
A program may use at most 64 MiB of HBM per device.

```python
import jax
import jax.numpy as jnp
from jax import lax

HEADS = 8
HEAD_DIM = 64
TILE = 8
RADIUS = 6
FEAT = 512
SPAN = 13
NLAT = 32
NLON = 128


def pair_fields(key):
    shape_all = (NLAT, NLON, HEADS * HEAD_DIM)
    query_draw = jnp.clip(jax.random.normal(jax.random.fold_in(key, 101), shape_all, jnp.float32), -5.0, 5.0)
    key_draw = jnp.clip(jax.random.normal(jax.random.fold_in(key, 102), shape_all, jnp.float32), -5.0, 5.0)
    return (query_draw, key_draw)


def draw_queries(key, part):
    return pair_fields(key)[0].astype(jnp.bfloat16)


def draw_key_cells(key, part):
    return pair_fields(key)[1].astype(jnp.bfloat16)


def levels(rng, shape, shards, least, largest):
    loudness, own = 1.0, jax.random.fold_in(rng, 6)
    for axis_at, blocks in shards:
        heights = jnp.exp(jax.random.uniform(jax.random.fold_in(own, axis_at), (blocks,), jnp.float32, least / len(shards), largest / len(shards)))
        loudness = loudness * jnp.repeat(heights, shape[axis_at] // blocks).reshape([-1 if axis == axis_at else 1 for axis in range(len(shape))])
    return loudness


def bell_draw(own_key, shape, spread, limit, split=(), held_as=jnp.bfloat16):
    entries = spread * jax.random.normal(own_key, shape, jnp.float32)
    if split:
        entries = entries * levels(own_key, shape, split, -0.22, 0.18)
    return jnp.clip(entries, -limit, limit).astype(held_as)


def setup_inputs(seed: int = 0) -> dict:
    streams_of = jax.random.split(jax.random.key(seed), 6)
    queries = draw_queries(jax.random.fold_in(streams_of[5], 71), 0)
    key_cells = draw_key_cells(jax.random.fold_in(streams_of[5], 71), 0)
    value_cells = bell_draw(streams_of[2], (NLAT, NLON, FEAT), 1.0, 5.0, ((0, 4), (1, 8)))
    grad_output = bell_draw(streams_of[3], (NLAT, NLON, FEAT), 1.0, 5.0, ((0, 4), (1, 8)))
    rel_bias = bell_draw(streams_of[4], (HEADS, SPAN * SPAN), 1.0, 4.0, (), jnp.float32)
    return {"queries": queries, "key_cells": key_cells, "value_cells": value_cells, "grad_output": grad_output, "rel_bias": rel_bias}


HIGH = lax.Precision.HIGHEST


def offset_onehot(inner_len, outer_len, span_len, direction, offset):
    shape_all = (inner_len, outer_len, span_len)
    offset_index = lax.broadcasted_iota(jnp.int32, shape_all, 2)
    inner_index = lax.broadcasted_iota(jnp.int32, shape_all, 0)
    outer_index = lax.broadcasted_iota(jnp.int32, shape_all, 1)
    return (offset_index == direction * (outer_index - inner_index) + offset).astype(jnp.float32)


def expand_bias(rel_bias, direction, offset):
    span_len = 2 * RADIUS + 1
    extent = TILE + 2 * RADIUS
    head_count = rel_bias.shape[0]
    offsets_table = rel_bias.reshape(head_count, span_len, span_len)
    onehot = offset_onehot(TILE, extent, span_len, direction, offset)
    partial_sum = jnp.einsum("hab,jcb->hajc", offsets_table, onehot, precision=HIGH)
    expanded = jnp.einsum("ira,hajc->hijrc", onehot, partial_sum, precision=HIGH)
    inside = jnp.einsum("ira,jcb->ijrc", onehot, onehot, precision=HIGH) > 0.5
    return expanded.reshape(head_count, TILE * TILE, extent * extent), inside.reshape(TILE * TILE, extent * extent)


def wrap_pad(values):
    widened = jnp.concatenate([values[:, -RADIUS:], values, values[:, :RADIUS]], axis=1)
    return jnp.pad(widened, ((RADIUS, RADIUS), (0, 0), (0, 0)))


def strip_blocks(padded, first_row):
    extent = TILE + 2 * RADIUS
    strip = lax.dynamic_slice_in_dim(padded, first_row, extent, 0)
    starts = jnp.arange(NLON // TILE, dtype=jnp.int32) * TILE
    columns = starts[:, None] + jnp.arange(extent, dtype=jnp.int32)[None, :]
    picked = strip[:, columns]
    return picked.transpose(1, 0, 2, 3).reshape(NLON // TILE, extent * extent, padded.shape[-1])


def row_tiles(values, first_row):
    band = lax.dynamic_slice_in_dim(values, first_row, TILE, 0)
    arranged = band.reshape(TILE, NLON // TILE, TILE, values.shape[-1]).transpose(1, 0, 2, 3)
    return arranged.reshape(NLON // TILE, TILE * TILE, values.shape[-1])


def untile(stacked):
    channels = stacked.shape[-1]
    arranged = stacked.reshape(NLAT // TILE, NLON // TILE, TILE, TILE, channels).transpose(0, 2, 1, 3, 4)
    return arranged.reshape(NLAT, NLON, channels)


def rounded(values):
    return lax.optimization_barrier(values.astype(jnp.bfloat16)).astype(jnp.float32)


def split_heads(values):
    return values.astype(jnp.float32).reshape(values.shape[0], values.shape[1], HEADS, HEAD_DIM)


def band_inside(first_row):
    extent = TILE + 2 * RADIUS
    global_row = first_row - RADIUS + jnp.arange(extent, dtype=jnp.int32)
    inside = (global_row >= 0) & (global_row < NLAT)
    return jnp.broadcast_to(inside[:, None], (extent, extent)).reshape(extent * extent)


def reference(queries, key_cells, value_cells, grad_output, rel_bias):
    factor = HEAD_DIM ** -0.5
    bias_query, inside_query = expand_bias(rel_bias, 1, 0)
    bias_key, inside_key = expand_bias(rel_bias, -1, 2 * RADIUS)
    key_pad = wrap_pad(key_cells)
    value_pad = wrap_pad(value_cells)
    starts = jnp.arange(NLAT // TILE, dtype=jnp.int32) * TILE

    def query_band(first_row):
        query_heads = split_heads(row_tiles(queries, first_row))
        grad_heads = split_heads(row_tiles(grad_output, first_row))
        key_heads = split_heads(strip_blocks(key_pad, first_row))
        value_heads = split_heads(strip_blocks(value_pad, first_row))
        allowed = inside_query & band_inside(first_row)[None, :]
        scores = jnp.einsum("tqhd,tkhd->thqk", query_heads, key_heads) * factor + bias_query[None]
        scores = jnp.where(allowed[None, None], scores, -jnp.inf)
        row_max = jnp.max(scores, axis=-1, keepdims=True)
        log_total = row_max + jnp.log(jnp.sum(jnp.exp(scores - row_max), axis=-1, keepdims=True))
        probability = jnp.exp(scores - log_total)
        weights = rounded(probability)
        attended = jnp.einsum("thqk,tkhd->tqhd", weights, value_heads)
        row_dot = jnp.sum(grad_heads * attended, axis=-1)
        grad_prob = jnp.einsum("tqhd,tkhd->thqk", grad_heads, value_heads)
        dscore = rounded(probability * (grad_prob - jnp.transpose(row_dot, (0, 2, 1))[..., None]))
        grad_q = jnp.einsum("thqk,tkhd->tqhd", dscore, key_heads) * factor
        tile_count = attended.shape[0]
        return (attended.reshape(tile_count, TILE * TILE, HEADS * HEAD_DIM).astype(jnp.bfloat16),
                grad_q.reshape(tile_count, TILE * TILE, HEADS * HEAD_DIM).astype(jnp.bfloat16),
                jnp.transpose(log_total[..., 0], (0, 2, 1)), row_dot)

    out_tiles, grad_q_tiles, total_tiles, dot_tiles = lax.map(query_band, starts)
    summary = jnp.concatenate([untile(total_tiles), untile(dot_tiles)], axis=-1)
    query_pad = wrap_pad(queries)
    grad_pad = wrap_pad(grad_output)
    summary_pad = wrap_pad(summary)

    def key_band(first_row):
        key_heads = split_heads(row_tiles(key_cells, first_row))
        value_heads = split_heads(row_tiles(value_cells, first_row))
        query_heads = split_heads(strip_blocks(query_pad, first_row))
        grad_heads = split_heads(strip_blocks(grad_pad, first_row))
        nearby = strip_blocks(summary_pad, first_row)
        totals = jnp.transpose(nearby[..., :HEADS], (0, 2, 1))[:, :, None, :]
        dots = jnp.transpose(nearby[..., HEADS:], (0, 2, 1))[:, :, None, :]
        allowed = inside_key & band_inside(first_row)[None, :]
        scores = jnp.einsum("tkhd,tqhd->thkq", key_heads, query_heads) * factor + bias_key[None]
        scores = jnp.where(allowed[None, None], scores, -jnp.inf)
        probability = jnp.exp(scores - totals)
        weights = rounded(probability)
        grad_prob = jnp.einsum("tkhd,tqhd->thkq", value_heads, grad_heads)
        dscore = rounded(probability * (grad_prob - dots))
        grad_k = jnp.einsum("thkq,tqhd->tkhd", dscore, query_heads) * factor
        grad_v = jnp.einsum("thkq,tqhd->tkhd", weights, grad_heads)
        tile_count = grad_k.shape[0]
        return (grad_k.reshape(tile_count, TILE * TILE, HEADS * HEAD_DIM).astype(jnp.bfloat16),
                grad_v.reshape(tile_count, TILE * TILE, HEADS * HEAD_DIM).astype(jnp.bfloat16))

    grad_k_tiles, grad_v_tiles = lax.map(key_band, starts)
    return (untile(out_tiles), untile(grad_q_tiles), untile(grad_k_tiles), untile(grad_v_tiles))
```

```python
import functools

import jax
import jax.numpy as jnp
from jax import lax
from jax.experimental import pallas as pl
from jax.experimental.pallas import tpu as pltpu
from jax.sharding import PartitionSpec as P

HEAD_DIM = 64
RADIUS = 6
SPAN = 2 * RADIUS + 1
ROWS = 8
COLS = 16
CELLS = ROWS * COLS
SIDE = ROWS * RADIUS
BAND = RADIUS * COLS
BACK = BAND + 2 * SIDE
PAIR = 2 * HEAD_DIM
BASE = 336
TABLE = 512
MASKED = -1e30

OWN_AT = 0
LON_AT = CELLS
LAT_AT = LON_AT + 2 * SIDE
CORNER_AT = LAT_AT + 2 * BAND
KEYS = CORNER_AT + 4 * SIDE

F32 = jnp.float32
BF16 = jnp.bfloat16


def pair_exchange(value, axis, odd, wrap):
    count = lax.axis_size(axis)
    pairs = []
    for first in range(odd, count, 2):
        second = first + 1
        if second >= count and not wrap:
            continue
        second %= count
        pairs += [(first, second), (second, first)]
    return lax.ppermute(value, axis, pairs)


def is_odd(axis):
    return lax.axis_index(axis) % 2 == 1


def pick_matrix(first_col):
    shape = (SIDE, CELLS)
    place = lax.broadcasted_iota(jnp.int32, shape, 0)
    cell = lax.broadcasted_iota(jnp.int32, shape, 1)
    source = (place % ROWS) * COLS + first_col + place // ROWS
    return (cell == source).astype(BF16)


def pack_kernel(k_ref, v_ref, bias_ref, lon_odd_ref, lon_even_ref, lat_even_ref, lat_odd_ref, line_ref):
    lon_odd = is_odd("lon")
    lat_odd = is_odd("lat")
    pick_odd = pick_matrix(jnp.where(lon_odd, COLS - RADIUS, 0))
    pick_even = pick_matrix(jnp.where(lon_odd, 0, COLS - RADIUS))
    low, high = 0, CELLS - BAND
    start_even = pl.multiple_of(jnp.where(lat_odd, low, high), 32)
    start_odd = pl.multiple_of(jnp.where(lat_odd, high, low), 32)
    for slot, source in ((0, k_ref), (1, v_ref)):
        whole = source[...]
        lon_odd_ref[slot] = jnp.dot(pick_odd, whole, preferred_element_type=F32).astype(BF16)
        lon_even_ref[slot] = jnp.dot(pick_even, whole, preferred_element_type=F32).astype(BF16)
        lat_even_ref[slot] = source[pl.ds(start_even, BAND), :]
        lat_odd_ref[slot] = source[pl.ds(start_odd, BAND), :]
    shape = (SPAN * SPAN, TABLE)
    entry = lax.broadcasted_iota(jnp.int32, shape, 0)
    offset = BASE - lax.broadcasted_iota(jnp.int32, shape, 1)
    chosen = (offset == (entry // SPAN) * COLS + entry % SPAN).astype(F32)
    line = jnp.dot(bias_ref[...], chosen, preferred_element_type=F32, precision=lax.Precision.HIGHEST)
    offset = BASE - lax.broadcasted_iota(jnp.int32, (1, TABLE), 1)
    valid = (offset >= 0) & (offset < SPAN * COLS) & (offset % COLS < SPAN)
    line_ref[...] = jnp.where(valid, line, MASKED)


def bias_kernel(line_ref, table_ref):
    lon_odd = is_odd("lon")
    lat_odd = is_odd("lat")
    has_north = lax.axis_index("lat") > 0
    has_south = lax.axis_index("lat") < lax.axis_size("lat") - 1
    head = pl.program_id(0)
    line = jnp.broadcast_to(line_ref[pl.ds(head, 1), :], (8, TABLE))
    by_one = pltpu.roll(line, 0, 1, stride=1, stride_axis=0)
    by_row = pltpu.roll(line, 0, 1, stride=COLS, stride_axis=0)
    query_col = lax.broadcasted_iota(jnp.int32, (8, CELLS), 1) % COLS
    sub = lax.broadcasted_iota(jnp.int32, (8, CELLS), 0)

    def window(source, row, col):
        first = BASE - (COLS * row + col)
        return source[:, first : first + CELLS]

    def near(delta):
        return (delta >= 0) & (delta < SPAN)

    def put(at, values):
        table_ref[0, pl.ds(pl.multiple_of(at, 8), 8), :] = values

    def cells(at, row, row_count, there):
        for half in range(COLS // 8):
            allowed = near(RADIUS + 8 * half + sub - query_col)
            if there is not None:
                allowed = allowed & there
            for step in range(row_count):
                values = window(by_one, row + step, RADIUS + 8 * half)
                put(at + step * COLS + 8 * half, jnp.where(allowed, values, MASKED))

    def sides(at, row, first_col, there):
        for step in range(RADIUS):
            allowed = near(first_col + step - query_col)
            if there is not None:
                allowed = allowed & there
            values = window(by_row, row, first_col + step)
            put(at + step * ROWS, jnp.where(allowed, values, MASKED))

    west, east = 0, COLS + RADIUS
    west_slot = jnp.where(lon_odd, SIDE, 0)
    east_slot = SIDE - west_slot
    cells(OWN_AT, RADIUS, ROWS, None)
    sides(LON_AT + west_slot, RADIUS, west, None)
    sides(LON_AT + east_slot, RADIUS, east, None)
    north_slot = jnp.where(lat_odd, 0, 1)
    south_slot = 1 - north_slot
    for slot, row, there in ((north_slot, 0, has_north), (south_slot, ROWS + RADIUS, has_south)):
        cells(LAT_AT + slot * BAND, row, RADIUS, there)
        first = row if row else row - (ROWS - RADIUS)
        sides(CORNER_AT + slot * 2 * SIDE + west_slot, first, west, there)
        sides(CORNER_AT + slot * 2 * SIDE + east_slot, first, east, there)


def main_kernel(
    q_ref, do_ref, k_ref, v_ref, lon_odd_ref, lon_even_ref, lat_even_ref, lat_odd_ref,
    c0_ref, c1_ref, c2_ref, c3_ref, table_ref,
    out_ref, dq_ref, own_ref, dlon_odd_ref, dlon_even_ref, back_even_ref, back_odd_ref,
):
    parts = (lon_odd_ref, lon_even_ref, lat_even_ref, lat_odd_ref, c0_ref, c1_ref, c2_ref, c3_ref)
    keys = jnp.concatenate([k_ref[...]] + [part[0] for part in parts], axis=0)
    values = jnp.concatenate([v_ref[...]] + [part[1] for part in parts], axis=0)
    first_head = lax.broadcasted_iota(jnp.int32, (CELLS, PAIR), 1) < HEAD_DIM
    factor = HEAD_DIM ** (-0.5)

    def both_heads(block):
        zero = jnp.zeros_like(block)
        return jnp.concatenate([jnp.where(first_head, block, zero), jnp.where(first_head, zero, block)], axis=0)

    queries = both_heads(q_ref[...] * jnp.asarray(factor, BF16))
    grads = both_heads(do_ref[...])
    last = (((1,), (1,)), ((), ()))
    scores = lax.dot_general(keys, queries, last, preferred_element_type=F32)
    scores = scores + jnp.concatenate([table_ref[0], table_ref[1]], axis=1)
    grad_prob = lax.dot_general(values, grads, last, preferred_element_type=F32)
    largest = jnp.max(scores, axis=0, keepdims=True)
    raised = jnp.exp(scores - largest)
    total = jnp.sum(raised, axis=0, keepdims=True)
    inverse = 1.0 / total
    row_dot = jnp.sum(raised * grad_prob, axis=0, keepdims=True) * inverse
    probability = raised * inverse
    weights = probability.astype(BF16)
    dscore = (probability * (grad_prob - row_dot)).astype(BF16)

    def per_query(cells, coefficients):
        turned = jnp.dot(cells.T, coefficients, preferred_element_type=F32)
        mine = jnp.concatenate([turned[:HEAD_DIM, :CELLS], turned[HEAD_DIM:, CELLS:]], axis=0)
        return mine.T

    out_ref[...] = per_query(values, weights).astype(BF16)
    dq_ref[...] = (per_query(keys, dscore) * factor).astype(BF16)
    for slot, coefficients, other in ((0, dscore, queries), (1, weights, grads)):
        grad = jnp.dot(coefficients, other, preferred_element_type=F32)
        own_ref[slot] = grad[:CELLS]
        dlon_odd_ref[slot] = grad[LON_AT : LON_AT + SIDE]
        dlon_even_ref[slot] = grad[LON_AT + SIDE : LAT_AT]
        for index, back in ((0, back_even_ref), (1, back_odd_ref)):
            at = LAT_AT + index * BAND
            back[slot, :BAND] = grad[at : at + BAND].astype(BF16)
            at = CORNER_AT + index * 2 * SIDE
            back[slot, BAND:] = grad[at : at + 2 * SIDE].astype(BF16)


def middle_kernel(dlon_odd_ref, dlon_even_ref, back_even_ref, back_odd_ref, send_odd_ref, send_even_ref):
    for index, (mine, send) in enumerate(((dlon_odd_ref, send_odd_ref), (dlon_even_ref, send_even_ref))):
        at = BAND + index * SIDE
        from_even = back_even_ref[:, at : at + SIDE].astype(F32)
        from_odd = back_odd_ref[:, at : at + SIDE].astype(F32)
        send[...] = (mine[...] + from_even + from_odd).astype(BF16)


def final_kernel(own_ref, back_even_ref, back_odd_ref, side_odd_ref, side_even_ref, dk_ref, dv_ref, sum_ref):
    lon_odd = is_odd("lon")
    lat_odd = is_odd("lat")
    start_even = pl.multiple_of(jnp.where(lat_odd, 0, CELLS - BAND), 32)
    start_odd = pl.multiple_of(jnp.where(lat_odd, CELLS - BAND, 0), 32)
    shape = (CELLS, SIDE)
    cell = lax.broadcasted_iota(jnp.int32, shape, 0)
    place = lax.broadcasted_iota(jnp.int32, shape, 1)

    def spread(first_col):
        return (cell == (place % ROWS) * COLS + first_col + place // ROWS).astype(BF16)

    spread_odd = spread(jnp.where(lon_odd, COLS - RADIUS, 0))
    spread_even = spread(jnp.where(lon_odd, 0, COLS - RADIUS))
    for slot, out in ((0, dk_ref), (1, dv_ref)):
        sum_ref[...] = (
            own_ref[slot]
            + jnp.dot(spread_odd, side_odd_ref[slot], preferred_element_type=F32)
            + jnp.dot(spread_even, side_even_ref[slot], preferred_element_type=F32)
        )
        sum_ref[pl.ds(start_even, BAND), :] += back_even_ref[slot, :BAND].astype(F32)
        sum_ref[pl.ds(start_odd, BAND), :] += back_odd_ref[slot, :BAND].astype(F32)
        out[...] = sum_ref[...].astype(BF16)


def arr(shape, dtype):
    return jax.ShapeDtypeStruct(shape, dtype)


PARAMS = pltpu.CompilerParams(vmem_limit_bytes=48 * 1024 * 1024)


def shards(queries, key_cells, value_cells, grad_output, rel_bias):
    block = queries.shape
    heads = rel_bias.shape[0]
    feat = block[-1]
    q, k, v, g = (x.reshape(CELLS, feat) for x in (queries, key_cells, value_cells, grad_output))
    side, band, back = (2, SIDE, feat), (2, BAND, feat), (2, BACK, feat)

    lon_odd, lon_even, lat_even, lat_odd, line = pl.pallas_call(
        pack_kernel,
        out_shape=[arr(side, BF16), arr(side, BF16), arr(band, BF16), arr(band, BF16), arr((heads, TABLE), F32)],
        compiler_params=PARAMS,
        name="pack",
    )(k, v, rel_bias)

    lon_odd = pair_exchange(lon_odd, "lon", 1, True)
    lon_even = pair_exchange(lon_even, "lon", 0, True)
    lat_even = pair_exchange(lat_even, "lat", 0, False)
    lat_odd = pair_exchange(lat_odd, "lat", 1, False)

    table = pl.pallas_call(
        bias_kernel,
        out_shape=arr((heads, KEYS, CELLS), F32),
        grid=(heads,),
        in_specs=[pl.BlockSpec((heads, TABLE), lambda i: (0, 0))],
        out_specs=pl.BlockSpec((1, KEYS, CELLS), lambda i: (i, 0, 0)),
        compiler_params=PARAMS,
        cost_estimate=pl.CostEstimate(flops=4 * heads * KEYS * CELLS, bytes_accessed=4 * heads * KEYS * CELLS, transcendentals=0),
        name="bias_table",
    )(line)

    corners = [
        pair_exchange(piece, "lat", odd, False) for odd in (0, 1) for piece in (lon_odd, lon_even)
    ]

    def cut(shape):
        if len(shape) == 2:
            return pl.BlockSpec((shape[0], PAIR), lambda i: (0, i))
        return pl.BlockSpec((shape[0], shape[1], PAIR), lambda i: (0, 0, i))

    inputs = (q, g, k, v, lon_odd, lon_even, lat_even, lat_odd, *corners)
    outs = [
        arr((CELLS, feat), BF16), arr((CELLS, feat), BF16), arr((2, CELLS, feat), F32),
        arr(side, F32), arr(side, F32), arr(back, BF16), arr(back, BF16),
    ]
    out, dq, own, dlon_odd, dlon_even, back_even, back_odd = pl.pallas_call(
        main_kernel,
        out_shape=outs,
        grid=(feat // PAIR,),
        in_specs=[cut(x.shape) for x in inputs] + [pl.BlockSpec((2, KEYS, CELLS), lambda i: (i, 0, 0))],
        out_specs=[cut(x.shape) for x in outs],
        compiler_params=PARAMS,
        name="attention",
    )(*inputs, table)

    back_even = pair_exchange(back_even, "lat", 0, False)
    back_odd = pair_exchange(back_odd, "lat", 1, False)
    send_odd, send_even = pl.pallas_call(
        middle_kernel,
        out_shape=[arr(side, BF16), arr(side, BF16)],
        compiler_params=PARAMS,
        name="middle",
    )(dlon_odd, dlon_even, back_even, back_odd)
    side_odd = pair_exchange(send_odd, "lon", 1, True)
    side_even = pair_exchange(send_even, "lon", 0, True)
    dk, dv = pl.pallas_call(
        final_kernel,
        out_shape=[arr((CELLS, feat), BF16), arr((CELLS, feat), BF16)],
        scratch_shapes=[pltpu.VMEM((CELLS, feat), F32)],
        compiler_params=PARAMS,
        name="final",
    )(own, back_even, back_odd, side_odd, side_even)
    return tuple(x.reshape(block) for x in (out, dq, dk, dv))


def solution(mesh):
    spec = P("lat", "lon", None)
    return jax.shard_map(
        shards, mesh=mesh, in_specs=(spec, spec, spec, spec, P()), out_specs=(spec,) * 4, check_vma=False
    )
```

```python
import functools

import jax
import jax.numpy as jnp
from jax import lax
from jax.experimental import pallas as pl
from jax.experimental.pallas import tpu as pltpu
from jax.sharding import PartitionSpec as P

HEAD_DIM = 64
RADIUS = 6
SPAN = 2 * RADIUS + 1
ROWS = 8
COLS = 16
CELLS = ROWS * COLS
SIDE = ROWS * RADIUS
BAND = RADIUS * COLS
PAIR = 2 * HEAD_DIM
BASE = 336
TABLE = 512
MASKED = -1e30

OWN_AT = 0
LON_AT = CELLS
LAT_AT = LON_AT + 2 * SIDE
NEAR = LAT_AT + 2 * BAND
CORNERS = 4 * SIDE

F32 = jnp.float32
BF16 = jnp.bfloat16


def pair_exchange(value, axis, odd, wrap):
    count = lax.axis_size(axis)
    pairs = []
    for first in range(odd, count, 2):
        second = first + 1
        if second >= count and not wrap:
            continue
        second %= count
        pairs += [(first, second), (second, first)]
    return lax.ppermute(value, axis, pairs)


def is_odd(axis):
    return lax.axis_index(axis) % 2 == 1


def pick_matrix(first_col):
    shape = (SIDE, CELLS)
    place = lax.broadcasted_iota(jnp.int32, shape, 0)
    cell = lax.broadcasted_iota(jnp.int32, shape, 1)
    source = (place % ROWS) * COLS + first_col + place // ROWS
    return (cell == source).astype(BF16)


def pack_kernel(
    k_hbm, v_hbm, bias_hbm, lon_odd_ref, lon_even_ref, lat_even_ref, lat_odd_ref, line_ref, k_ref, v_ref, bias_ref, sems
):
    copies = [
        pltpu.make_async_copy(source, target, sems.at[index])
        for index, (source, target) in enumerate(((k_hbm, k_ref), (v_hbm, v_ref), (bias_hbm, bias_ref)))
    ]
    for copy in copies:
        copy.start()
    lon_odd = is_odd("lon")
    lat_odd = is_odd("lat")
    pick_odd = pick_matrix(jnp.where(lon_odd, COLS - RADIUS, 0))
    pick_even = pick_matrix(jnp.where(lon_odd, 0, COLS - RADIUS))
    low, high = 0, CELLS - BAND
    start_even = pl.multiple_of(jnp.where(lat_odd, low, high), 32)
    start_odd = pl.multiple_of(jnp.where(lat_odd, high, low), 32)
    shape = (SPAN * SPAN, TABLE)
    entry = lax.broadcasted_iota(jnp.int32, shape, 0)
    offset = BASE - lax.broadcasted_iota(jnp.int32, shape, 1)
    chosen = (offset == (entry // SPAN) * COLS + entry % SPAN).astype(F32)
    for slot, source in ((0, k_ref), (1, v_ref)):
        copies[slot].wait()
        whole = source[...]
        lon_odd_ref[slot] = jnp.dot(pick_odd, whole, preferred_element_type=F32).astype(BF16)
        lon_even_ref[slot] = jnp.dot(pick_even, whole, preferred_element_type=F32).astype(BF16)
        lat_even_ref[slot] = source[pl.ds(start_even, BAND), :]
        lat_odd_ref[slot] = source[pl.ds(start_odd, BAND), :]
    copies[2].wait()
    line = jnp.dot(bias_ref[...], chosen, preferred_element_type=F32, precision=lax.Precision.HIGHEST)
    offset = BASE - lax.broadcasted_iota(jnp.int32, (1, TABLE), 1)
    valid = (offset >= 0) & (offset < SPAN * COLS) & (offset % COLS < SPAN)
    line_ref[...] = jnp.where(valid, line, MASKED)


def bias_kernel(line_ref, table_ref, corner_ref):
    lon_odd = is_odd("lon")
    lat_odd = is_odd("lat")
    has_north = lax.axis_index("lat") > 0
    has_south = lax.axis_index("lat") < lax.axis_size("lat") - 1
    head = pl.program_id(0)
    line = jnp.broadcast_to(line_ref[pl.ds(head, 1), :], (8, TABLE))
    by_one = pltpu.roll(line, 0, 1, stride=1, stride_axis=0)
    by_row = pltpu.roll(line, 0, 1, stride=COLS, stride_axis=0)
    query_col = lax.broadcasted_iota(jnp.int32, (8, CELLS), 1) % COLS
    sub = lax.broadcasted_iota(jnp.int32, (8, CELLS), 0)

    def window(source, row, col):
        first = BASE - (COLS * row + col)
        return source[:, first : first + CELLS]

    def near(delta):
        return (delta >= 0) & (delta < SPAN)

    def put(at, values, target=table_ref):
        target[0, pl.ds(pl.multiple_of(at, 8), 8), :] = values

    def cells(at, row, row_count, there):
        for half in range(COLS // 8):
            allowed = near(RADIUS + 8 * half + sub - query_col)
            if there is not None:
                allowed = allowed & there
            for step in range(row_count):
                values = window(by_one, row + step, RADIUS + 8 * half)
                put(at + step * COLS + 8 * half, jnp.where(allowed, values, MASKED))

    def sides(at, row, first_col, there, target=table_ref):
        for step in range(RADIUS):
            allowed = near(first_col + step - query_col)
            if there is not None:
                allowed = allowed & there
            values = window(by_row, row, first_col + step)
            put(at + step * ROWS, jnp.where(allowed, values, MASKED), target)

    west, east = 0, COLS + RADIUS
    west_slot = jnp.where(lon_odd, SIDE, 0)
    east_slot = SIDE - west_slot
    cells(OWN_AT, RADIUS, ROWS, None)
    sides(LON_AT + west_slot, RADIUS, west, None)
    sides(LON_AT + east_slot, RADIUS, east, None)
    north_slot = jnp.where(lat_odd, 0, 1)
    south_slot = 1 - north_slot
    for slot, row, there in ((north_slot, 0, has_north), (south_slot, ROWS + RADIUS, has_south)):
        cells(LAT_AT + slot * BAND, row, RADIUS, there)
        first = row if row else row - (ROWS - RADIUS)
        sides(slot * 2 * SIDE + west_slot, first, west, there, corner_ref)
        sides(slot * 2 * SIDE + east_slot, first, east, there, corner_ref)


LAST = (((1,), (1,)), ((), ()))
FACTOR = HEAD_DIM ** (-0.5)


def both_heads(block):
    first_head = lax.broadcasted_iota(jnp.int32, block.shape, 1) < HEAD_DIM
    zero = jnp.zeros_like(block)
    return jnp.concatenate([jnp.where(first_head, block, zero), jnp.where(first_head, zero, block)], axis=0)


def scaled_queries(q_ref):
    return both_heads(q_ref[...] * jnp.asarray(FACTOR, BF16))


def pair_scores(keys, values, queries, grads, table_ref):
    scores = lax.dot_general(keys, queries, LAST, preferred_element_type=F32)
    scores = scores + jnp.concatenate([table_ref[0], table_ref[1]], axis=1)
    grad_prob = lax.dot_general(values, grads, LAST, preferred_element_type=F32)
    return scores, grad_prob


def column_sum(x):
    return jnp.sum(x, axis=0, keepdims=True)


def score_gradient(probability, grad_prob, row_dot):
    return probability.astype(BF16), (probability * (grad_prob - row_dot)).astype(BF16)


def near_kernel(
    q_ref, g_ref, k_ref, v_ref, lon_odd_ref, lon_even_ref, lat_even_ref, lat_odd_ref, table_ref,
    own_raised_ref, own_prob_ref, lon_raised_ref, lon_prob_ref, lat_raised_ref, lat_prob_ref, stats_ref,
):
    parts = (lon_odd_ref, lon_even_ref, lat_even_ref, lat_odd_ref)
    keys = jnp.concatenate([k_ref[...]] + [part[0] for part in parts], axis=0)
    values = jnp.concatenate([v_ref[...]] + [part[1] for part in parts], axis=0)
    scores, grad_prob = pair_scores(keys, values, scaled_queries(q_ref), both_heads(g_ref[...]), table_ref)
    largest = jnp.max(scores, axis=0, keepdims=True)
    raised = jnp.exp(scores - largest)
    stats_ref[0, 0:1] = largest
    stats_ref[0, 1:2] = column_sum(raised)
    stats_ref[0, 2:3] = column_sum(raised * grad_prob)
    for at, end, raised_ref, prob_ref in (
        (OWN_AT, LON_AT, own_raised_ref, own_prob_ref),
        (LON_AT, LAT_AT, lon_raised_ref, lon_prob_ref),
        (LAT_AT, NEAR, lat_raised_ref, lat_prob_ref),
    ):
        raised_ref[0] = raised[at:end]
        prob_ref[0] = grad_prob[at:end]


def corner_kernel(
    q_ref, g_ref, c0_ref, c1_ref, c2_ref, c3_ref, table_ref, lon_raised_ref, lon_prob_ref, near_stats_ref,
    back_even_ref, back_odd_ref, dlon_odd_ref, dlon_even_ref, weights_ref, dscore_ref, stats_ref,
):
    parts = (c0_ref, c1_ref, c2_ref, c3_ref)
    keys = jnp.concatenate([part[0] for part in parts], axis=0)
    values = jnp.concatenate([part[1] for part in parts], axis=0)
    queries, grads = scaled_queries(q_ref), both_heads(g_ref[...])
    scores, grad_prob = pair_scores(keys, values, queries, grads, table_ref)
    near_largest = near_stats_ref[0, 0:1]
    largest = jnp.maximum(near_largest, jnp.max(scores, axis=0, keepdims=True))
    raised = jnp.exp(scores - largest)
    shift = jnp.exp(near_largest - largest)
    total = near_stats_ref[0, 1:2] * shift + column_sum(raised)
    inverse = 1.0 / total
    near_scale = shift * inverse
    row_dot = near_stats_ref[0, 2:3] * near_scale + column_sum(raised * grad_prob) * inverse
    stats_ref[0, 0:1] = near_scale
    stats_ref[0, 1:2] = row_dot
    far = score_gradient(raised * inverse, grad_prob, row_dot)
    lon = score_gradient(lon_raised_ref[0] * near_scale, lon_prob_ref[0], row_dot)
    weights = jnp.concatenate([lon[0], far[0]], axis=0)
    dscore = jnp.concatenate([lon[1], far[1]], axis=0)
    weights_ref[0] = weights
    dscore_ref[0] = dscore
    for slot, coefficients, other in ((0, dscore, queries), (1, weights, grads)):
        grad = jnp.dot(coefficients, other, preferred_element_type=F32)
        dlon_odd_ref[slot] = grad[:SIDE]
        dlon_even_ref[slot] = grad[SIDE : 2 * SIDE]
        back_even_ref[slot] = grad[2 * SIDE : 4 * SIDE].astype(BF16)
        back_odd_ref[slot] = grad[4 * SIDE :].astype(BF16)


def lat_kernel(
    q_ref, g_ref, lat_raised_ref, lat_prob_ref, stats_ref, back_even_ref, back_odd_ref, weights_ref, dscore_ref
):
    weights, dscore = score_gradient(lat_raised_ref[0] * stats_ref[0, 0:1], lat_prob_ref[0], stats_ref[0, 1:2])
    weights_ref[0] = weights
    dscore_ref[0] = dscore
    for slot, coefficients, other in ((0, dscore, scaled_queries(q_ref)), (1, weights, both_heads(g_ref[...]))):
        grad = jnp.dot(coefficients, other, preferred_element_type=F32).astype(BF16)
        back_even_ref[slot] = grad[:BAND]
        back_odd_ref[slot] = grad[BAND:]


def own_kernel(
    q_ref, g_ref, k_ref, v_ref, lon_odd_ref, lon_even_ref, lat_even_ref, lat_odd_ref, c0_ref, c1_ref, c2_ref, c3_ref,
    own_raised_ref, own_prob_ref, stats_ref, far_weights_ref, far_dscore_ref, lat_weights_ref, lat_dscore_ref,
    out_ref, dq_ref, own_ref,
):
    own_weights, own_dscore = score_gradient(
        own_raised_ref[0] * stats_ref[0, 0:1], own_prob_ref[0], stats_ref[0, 1:2]
    )
    for slot, coefficients, other in (
        (0, own_dscore, scaled_queries(q_ref)), (1, own_weights, both_heads(g_ref[...]))
    ):
        own_ref[slot] = jnp.dot(coefficients, other, preferred_element_type=F32)
    parts = (lon_odd_ref, lon_even_ref, c0_ref, c1_ref, c2_ref, c3_ref, lat_even_ref, lat_odd_ref)
    keys = jnp.concatenate([k_ref[...]] + [part[0] for part in parts], axis=0)
    values = jnp.concatenate([v_ref[...]] + [part[1] for part in parts], axis=0)
    weights = jnp.concatenate([own_weights, far_weights_ref[0], lat_weights_ref[0]], axis=0)
    dscore = jnp.concatenate([own_dscore, far_dscore_ref[0], lat_dscore_ref[0]], axis=0)

    def per_query(cells, coefficients):
        turned = jnp.dot(cells.T, coefficients, preferred_element_type=F32)
        mine = jnp.concatenate([turned[:HEAD_DIM, :CELLS], turned[HEAD_DIM:, CELLS:]], axis=0)
        return mine.T

    out_ref[...] = per_query(values, weights).astype(BF16)
    dq_ref[...] = (per_query(keys, dscore) * FACTOR).astype(BF16)


def middle_kernel(dlon_odd_ref, dlon_even_ref, back_even_ref, back_odd_ref, send_odd_ref, send_even_ref):
    for index, (mine, send) in enumerate(((dlon_odd_ref, send_odd_ref), (dlon_even_ref, send_even_ref))):
        piece = pl.ds(index * SIDE, SIDE)
        send[...] = (mine[...] + back_even_ref[:, piece].astype(F32) + back_odd_ref[:, piece].astype(F32)).astype(BF16)


def final_kernel(own_ref, back_even_ref, back_odd_ref, side_odd_ref, side_even_ref, dk_ref, dv_ref, sum_ref):
    lon_odd = is_odd("lon")
    lat_odd = is_odd("lat")
    start_even = pl.multiple_of(jnp.where(lat_odd, 0, CELLS - BAND), 32)
    start_odd = pl.multiple_of(jnp.where(lat_odd, CELLS - BAND, 0), 32)
    shape = (CELLS, SIDE)
    cell = lax.broadcasted_iota(jnp.int32, shape, 0)
    place = lax.broadcasted_iota(jnp.int32, shape, 1)

    def spread(first_col):
        return (cell == (place % ROWS) * COLS + first_col + place // ROWS).astype(BF16)

    spread_odd = spread(jnp.where(lon_odd, COLS - RADIUS, 0))
    spread_even = spread(jnp.where(lon_odd, 0, COLS - RADIUS))
    for slot, out in ((0, dk_ref), (1, dv_ref)):
        sum_ref[...] = (
            own_ref[slot]
            + jnp.dot(spread_odd, side_odd_ref[slot], preferred_element_type=F32)
            + jnp.dot(spread_even, side_even_ref[slot], preferred_element_type=F32)
        )
        sum_ref[pl.ds(start_even, BAND), :] += back_even_ref[slot].astype(F32)
        sum_ref[pl.ds(start_odd, BAND), :] += back_odd_ref[slot].astype(F32)
        out[...] = sum_ref[...].astype(BF16)


def arr(shape, dtype):
    return jax.ShapeDtypeStruct(shape, dtype)


PARAMS = pltpu.CompilerParams(vmem_limit_bytes=32 * 1024 * 1024)


def cut(shape):
    if len(shape) == 2:
        return pl.BlockSpec((shape[0], PAIR), lambda i: (0, i))
    return pl.BlockSpec((shape[0], shape[1], PAIR), lambda i: (0, 0, i))


def by_pair(shape):
    return pl.BlockSpec((1, shape[1], shape[2]), lambda i: (i, 0, 0))


def by_two(shape):
    return pl.BlockSpec((2, shape[1], shape[2]), lambda i: (i, 0, 0))


def per_pair_call(kernel, name, operands, results, flops):
    pairs = operands[0][0].shape[1] // PAIR
    moved = sum(x.size * x.dtype.itemsize for x, _ in operands)
    return pl.pallas_call(
        kernel,
        out_shape=[x for x, _ in results],
        grid=(pairs,),
        in_specs=[spec(x.shape) for x, spec in operands],
        out_specs=[spec(x.shape) for x, spec in results],
        compiler_params=PARAMS,
        cost_estimate=pl.CostEstimate(flops=flops, bytes_accessed=moved, transcendentals=0),
        name=name,
    )(*[x for x, _ in operands])


def shards(queries, key_cells, value_cells, grad_output, rel_bias):
    block = queries.shape
    heads = rel_bias.shape[0]
    feat = block[-1]
    pairs = feat // PAIR
    q, k, v, g = (x.reshape(CELLS, feat) for x in (queries, key_cells, value_cells, grad_output))
    side, band = (2, SIDE, feat), (2, BAND, feat)
    work = 2 * CELLS * feat

    hbm = pl.BlockSpec(memory_space=pltpu.HBM)
    lon_odd, lon_even, lat_even, lat_odd, line = pl.pallas_call(
        pack_kernel,
        out_shape=[arr(side, BF16), arr(side, BF16), arr(band, BF16), arr(band, BF16), arr((heads, TABLE), F32)],
        in_specs=[hbm, hbm, hbm],
        scratch_shapes=[
            pltpu.VMEM((CELLS, feat), BF16),
            pltpu.VMEM((CELLS, feat), BF16),
            pltpu.VMEM(rel_bias.shape, F32),
            pltpu.SemaphoreType.DMA((3,)),
        ],
        compiler_params=PARAMS,
        name="pack",
    )(k, v, rel_bias)

    lon_odd = pair_exchange(lon_odd, "lon", 1, True)
    lon_even = pair_exchange(lon_even, "lon", 0, True)
    lat_even = pair_exchange(lat_even, "lat", 0, False)
    lat_odd = pair_exchange(lat_odd, "lat", 1, False)

    table, corner_table = pl.pallas_call(
        bias_kernel,
        out_shape=[arr((heads, NEAR, CELLS), F32), arr((heads, CORNERS, CELLS), F32)],
        grid=(heads,),
        in_specs=[pl.BlockSpec((heads, TABLE), lambda i: (0, 0))],
        out_specs=[
            pl.BlockSpec((1, NEAR, CELLS), lambda i: (i, 0, 0)),
            pl.BlockSpec((1, CORNERS, CELLS), lambda i: (i, 0, 0)),
        ],
        compiler_params=PARAMS,
        cost_estimate=pl.CostEstimate(flops=heads * NEAR * CELLS, bytes_accessed=8 * heads * NEAR * CELLS, transcendentals=0),
        name="bias_table",
    )(line)

    lon_even, table, corner_table = lax.optimization_barrier((lon_even, table, corner_table))
    lon_odd, lat_even, lat_odd = lax.optimization_barrier((lon_odd, lat_even, lat_odd))
    c1 = pair_exchange(lon_even, "lat", 0, False)
    c3 = pair_exchange(lon_even, "lat", 1, False)
    c0 = pair_exchange(lon_odd, "lat", 0, False)
    c2 = pair_exchange(lon_odd, "lat", 1, False)
    corners = [(c, cut) for c in (c0, c1, c2, c3)]

    mine = [(q, cut), (g, cut)]
    near = [(x, cut) for x in (k, v, lon_odd, lon_even, lat_even, lat_odd)]
    stats = (arr((pairs, 8, 2 * CELLS), F32), by_pair)

    def scored(rows, dtype):
        return [(arr((pairs, rows, 2 * CELLS), dtype), by_pair)] * 2

    spans = (CELLS, 2 * SIDE, 2 * BAND)
    own_raised, own_prob, lon_raised, lon_prob, lat_raised, lat_prob, near_stats = per_pair_call(
        near_kernel, "near", mine + near + [(table, by_two)],
        [x for rows in spans for x in scored(rows, F32)] + [stats], 4 * work * NEAR,
    )
    corner_even, corner_odd, dlon_odd, dlon_even, far_weights, far_dscore, all_stats = per_pair_call(
        corner_kernel, "corner",
        mine + corners + [(corner_table, by_two)] + [(x, by_pair) for x in (lon_raised, lon_prob, near_stats)],
        [(arr((2, 2 * SIDE, feat), BF16), cut)] * 2 + [(arr(side, F32), cut)] * 2
        + scored(2 * SIDE + CORNERS, BF16) + [stats], 4 * work * CORNERS,
    )
    corner_even = pair_exchange(corner_even, "lat", 0, False)
    corner_odd = pair_exchange(corner_odd, "lat", 1, False)
    back_even, back_odd, lat_weights, lat_dscore = per_pair_call(
        lat_kernel, "lat_rows", mine + [(x, by_pair) for x in (lat_raised, lat_prob, all_stats)],
        [(arr(band, BF16), cut)] * 2 + scored(2 * BAND, BF16), 4 * work * BAND,
    )
    back_even = pair_exchange(back_even, "lat", 0, False)
    back_odd = pair_exchange(back_odd, "lat", 1, False)
    send_odd, send_even = pl.pallas_call(
        middle_kernel,
        out_shape=[arr(side, BF16), arr(side, BF16)],
        compiler_params=PARAMS,
        name="middle",
    )(dlon_odd, dlon_even, corner_even, corner_odd)
    side_odd = pair_exchange(send_odd, "lon", 1, True)
    side_even = pair_exchange(send_even, "lon", 0, True)
    scores = (own_raised, own_prob, all_stats, far_weights, far_dscore, lat_weights, lat_dscore)
    out, dq, own = per_pair_call(
        own_kernel, "own", mine + near + corners + [(x, by_pair) for x in scores],
        [(arr((CELLS, feat), BF16), cut)] * 2 + [(arr((2, CELLS, feat), F32), cut)], 4 * work * (NEAR + CORNERS),
    )
    dk, dv = pl.pallas_call(
        final_kernel,
        out_shape=[arr((CELLS, feat), BF16), arr((CELLS, feat), BF16)],
        scratch_shapes=[pltpu.VMEM((CELLS, feat), F32)],
        compiler_params=PARAMS,
        name="final",
    )(own, back_even, back_odd, side_odd, side_even)
    return tuple(x.reshape(block) for x in (out, dq, dk, dv))


def solution(mesh):
    spec = P("lat", "lon", None)
    return jax.shard_map(
        shards, mesh=mesh, in_specs=(spec, spec, spec, spec, P()), out_specs=(spec,) * 4, check_vma=False
    )
```

```python
import jax
import jax.numpy as jnp
from jax import lax
from jax.experimental import pallas as pl
from jax.experimental.pallas import tpu as pltpu
from jax.sharding import PartitionSpec as P

HEAD_DIM = 64
RADIUS = 6
SPAN = 2 * RADIUS + 1
ROWS = 8
COLS = 16
CELLS = ROWS * COLS
SIDE = ROWS * RADIUS
BAND = RADIUS * COLS
PAIR = 2 * HEAD_DIM
BASE = 336
TABLE = 512
MASKED = -1e30

OWN_AT = 0
LON_AT = CELLS
LAT_AT = LON_AT + 2 * SIDE
NEAR = LAT_AT + 2 * BAND
CORNERS = 4 * SIDE

F32 = jnp.float32
BF16 = jnp.bfloat16


def pair_exchange(value, axis, odd, wrap):
    count = lax.axis_size(axis)
    pairs = []
    for first in range(odd, count, 2):
        second = first + 1
        if second >= count and not wrap:
            continue
        second %= count
        pairs += [(first, second), (second, first)]
    return lax.ppermute(value, axis, pairs)


def is_odd(axis):
    return lax.axis_index(axis) % 2 == 1


def pick_matrix(first_col):
    shape = (SIDE, CELLS)
    place = lax.broadcasted_iota(jnp.int32, shape, 0)
    cell = lax.broadcasted_iota(jnp.int32, shape, 1)
    source = (place % ROWS) * COLS + first_col + place // ROWS
    return (cell == source).astype(BF16)


def pack_kernel(k_hbm, v_hbm, q_hbm, g_hbm, lon_odd_ref, lon_even_ref, k_ref, v_ref, q_ref, g_ref, sems):
    copies = [
        pltpu.make_async_copy(source, target, sems.at[index])
        for index, (source, target) in enumerate(((k_hbm, k_ref), (v_hbm, v_ref), (q_hbm, q_ref), (g_hbm, g_ref)))
    ]
    for copy in copies:
        copy.start()
    lon_odd = is_odd("lon")
    pick_odd = pick_matrix(jnp.where(lon_odd, COLS - RADIUS, 0))
    pick_even = pick_matrix(jnp.where(lon_odd, 0, COLS - RADIUS))
    for slot, source in ((0, k_ref), (1, v_ref)):
        copies[slot].wait()
        whole = source[...]
        lon_odd_ref[slot] = jnp.dot(pick_odd, whole, preferred_element_type=F32).astype(BF16)
        lon_even_ref[slot] = jnp.dot(pick_even, whole, preferred_element_type=F32).astype(BF16)
    copies[2].wait()
    copies[3].wait()


def lat_starts():
    lat_odd = is_odd("lat")
    even = jnp.where(lat_odd, 0, CELLS - BAND)
    return pl.multiple_of(even, 32), pl.multiple_of(CELLS - BAND - even, 32)


def rows_kernel(k_ref, v_ref, lat_even_ref, lat_odd_ref):
    for start, out in zip(lat_starts(), (lat_even_ref, lat_odd_ref)):
        out[0] = k_ref[pl.ds(start, BAND), :]
        out[1] = v_ref[pl.ds(start, BAND), :]


def bias_kernel(bias_ref, table_ref, corner_ref, line_ref):
    head = pl.program_id(0)

    @pl.when(head == 0)
    def _():
        shape = (SPAN * SPAN, TABLE)
        entry = lax.broadcasted_iota(jnp.int32, shape, 0)
        offset = BASE - lax.broadcasted_iota(jnp.int32, shape, 1)
        chosen = (offset == (entry // SPAN) * COLS + entry % SPAN).astype(F32)
        line = jnp.dot(bias_ref[...], chosen, preferred_element_type=F32, precision=lax.Precision.HIGHEST)
        offset = BASE - lax.broadcasted_iota(jnp.int32, (1, TABLE), 1)
        valid = (offset >= 0) & (offset < SPAN * COLS) & (offset % COLS < SPAN)
        line_ref[...] = jnp.where(valid, line, MASKED)

    lon_odd = is_odd("lon")
    lat_odd = is_odd("lat")
    has_north = lax.axis_index("lat") > 0
    has_south = lax.axis_index("lat") < lax.axis_size("lat") - 1
    line = jnp.broadcast_to(line_ref[pl.ds(head, 1), :], (8, TABLE))
    by_one = pltpu.roll(line, 0, 1, stride=1, stride_axis=0)
    by_row = pltpu.roll(line, 0, 1, stride=COLS, stride_axis=0)
    query_col = lax.broadcasted_iota(jnp.int32, (8, CELLS), 1) % COLS
    sub = lax.broadcasted_iota(jnp.int32, (8, CELLS), 0)

    def window(source, row, col):
        first = BASE - (COLS * row + col)
        return source[:, first : first + CELLS]

    def near(delta):
        return (delta >= 0) & (delta < SPAN)

    def put(at, values, target=table_ref):
        target[0, pl.ds(pl.multiple_of(at, 8), 8), :] = values

    def cells(at, row, row_count, there):
        for half in range(COLS // 8):
            allowed = near(RADIUS + 8 * half + sub - query_col)
            if there is not None:
                allowed = allowed & there
            for step in range(row_count):
                values = window(by_one, row + step, RADIUS + 8 * half)
                put(at + step * COLS + 8 * half, jnp.where(allowed, values, MASKED))

    def sides(at, row, first_col, there, target=table_ref):
        for step in range(RADIUS):
            allowed = near(first_col + step - query_col)
            if there is not None:
                allowed = allowed & there
            values = window(by_row, row, first_col + step)
            put(at + step * ROWS, jnp.where(allowed, values, MASKED), target)

    west, east = 0, COLS + RADIUS
    west_slot = jnp.where(lon_odd, SIDE, 0)
    east_slot = SIDE - west_slot
    cells(OWN_AT, RADIUS, ROWS, None)
    sides(LON_AT + west_slot, RADIUS, west, None)
    sides(LON_AT + east_slot, RADIUS, east, None)
    north_slot = jnp.where(lat_odd, 0, 1)
    south_slot = 1 - north_slot
    for slot, row, there in ((north_slot, 0, has_north), (south_slot, ROWS + RADIUS, has_south)):
        cells(LAT_AT + slot * BAND, row, RADIUS, there)
        first = row if row else row - (ROWS - RADIUS)
        sides(slot * 2 * SIDE + west_slot, first, west, there, corner_ref)
        sides(slot * 2 * SIDE + east_slot, first, east, there, corner_ref)


LAST = (((1,), (1,)), ((), ()))
FACTOR = HEAD_DIM ** (-0.5)


def join_kernel(lon_odd_ref, lon_even_ref, out_ref):
    out_ref[:, :SIDE] = lon_odd_ref[...]
    out_ref[:, SIDE:] = lon_even_ref[...]


def over_pairs(width, body):
    def step(pair, carry):
        body(pair, pl.ds(pl.multiple_of(pair * PAIR, PAIR), PAIR))
        return carry

    lax.fori_loop(0, width // PAIR, step, 0)


def both_heads(block):
    first_head = lax.broadcasted_iota(jnp.int32, block.shape, 1) < HEAD_DIM
    zero = jnp.zeros_like(block)
    return jnp.concatenate([jnp.where(first_head, block, zero), jnp.where(first_head, zero, block)], axis=0)


def scaled(block):
    return both_heads(block * jnp.asarray(FACTOR, BF16))


def pair_scores(keys, values, queries, grads, table_ref, pair):
    scores = lax.dot_general(keys, queries, LAST, preferred_element_type=F32)
    scores = scores + jnp.concatenate([table_ref[2 * pair], table_ref[2 * pair + 1]], axis=1)
    grad_prob = lax.dot_general(values, grads, LAST, preferred_element_type=F32)
    return scores, grad_prob


def column_sum(x):
    return jnp.sum(x, axis=0, keepdims=True)


def score_gradient(probability, grad_prob, row_dot):
    return probability.astype(BF16), (probability * (grad_prob - row_dot)).astype(BF16)


def near_kernel(
    q_ref, g_ref, k_ref, v_ref, lon_odd_ref, lon_even_ref, lat_even_ref, lat_odd_ref, table_ref,
    raised_ref, prob_ref, stats_ref,
):
    parts = (lon_odd_ref, lon_even_ref, lat_even_ref, lat_odd_ref)

    def body(pair, at):
        keys = jnp.concatenate([k_ref[:, at]] + [part[0, :, at] for part in parts], axis=0)
        values = jnp.concatenate([v_ref[:, at]] + [part[1, :, at] for part in parts], axis=0)
        queries, grads = scaled(q_ref[:, at]), both_heads(g_ref[:, at])
        scores, grad_prob = pair_scores(keys, values, queries, grads, table_ref, pair)
        largest = jnp.max(scores, axis=0, keepdims=True)
        raised = jnp.exp(scores - largest)
        raised_ref[pair] = raised
        prob_ref[pair] = grad_prob
        stats_ref[pair, 0:1] = largest
        stats_ref[pair, 1:2] = column_sum(raised)
        stats_ref[pair, 2:3] = column_sum(raised * grad_prob)

    over_pairs(q_ref.shape[1], body)


def corner_kernel(
    q_ref, g_ref, corner_even_ref, corner_odd_ref, table_ref, near_stats_ref,
    back_even_ref, back_odd_ref, weights_ref, dscore_ref, stats_ref,
):
    def body(pair, at):
        keys = jnp.concatenate([corner_even_ref[0, :, at], corner_odd_ref[0, :, at]], axis=0)
        values = jnp.concatenate([corner_even_ref[1, :, at], corner_odd_ref[1, :, at]], axis=0)
        queries, grads = scaled(q_ref[:, at]), both_heads(g_ref[:, at])
        scores, grad_prob = pair_scores(keys, values, queries, grads, table_ref, pair)
        near_largest = near_stats_ref[pair, 0:1]
        largest = jnp.maximum(near_largest, jnp.max(scores, axis=0, keepdims=True))
        raised = jnp.exp(scores - largest)
        shift = jnp.exp(near_largest - largest)
        total = near_stats_ref[pair, 1:2] * shift + column_sum(raised)
        inverse = 1.0 / total
        near_scale = shift * inverse
        row_dot = near_stats_ref[pair, 2:3] * near_scale + column_sum(raised * grad_prob) * inverse
        stats_ref[pair, 0:1] = near_scale
        stats_ref[pair, 1:2] = row_dot
        weights, dscore = score_gradient(raised * inverse, grad_prob, row_dot)
        weights_ref[pair] = weights
        dscore_ref[pair] = dscore
        for slot, coefficients, other in ((0, dscore, queries), (1, weights, grads)):
            grad = jnp.dot(coefficients, other, preferred_element_type=F32).astype(BF16)
            back_even_ref[slot, :, at] = grad[: 2 * SIDE]
            back_odd_ref[slot, :, at] = grad[2 * SIDE :]

    over_pairs(q_ref.shape[1], body)


def sides_kernel(
    q_ref, g_ref, raised_ref, prob_ref, stats_ref,
    dlon_ref, back_even_ref, back_odd_ref, weights_ref, dscore_ref,
):
    def body(pair, at):
        weights, dscore = score_gradient(
            raised_ref[pair, LON_AT:] * stats_ref[pair, 0:1], prob_ref[pair, LON_AT:], stats_ref[pair, 1:2]
        )
        weights_ref[pair] = weights
        dscore_ref[pair] = dscore
        for slot, coefficients, other in ((0, dscore, scaled(q_ref[:, at])), (1, weights, both_heads(g_ref[:, at]))):
            grad = jnp.dot(coefficients, other, preferred_element_type=F32)
            dlon_ref[slot, :, at] = grad[: 2 * SIDE]
            back_even_ref[slot, :, at] = grad[2 * SIDE : 2 * SIDE + BAND].astype(BF16)
            back_odd_ref[slot, :, at] = grad[2 * SIDE + BAND :].astype(BF16)

    over_pairs(q_ref.shape[1], body)


def own_kernel(
    q_ref, g_ref, k_ref, v_ref, lon_odd_ref, lon_even_ref, lat_even_ref, lat_odd_ref, corner_even_ref, corner_odd_ref,
    raised_ref, prob_ref, stats_ref, side_weights_ref, side_dscore_ref, corner_weights_ref, corner_dscore_ref,
    out_ref, dq_ref, own_ref,
):
    parts = (lon_odd_ref, lon_even_ref, lat_even_ref, lat_odd_ref, corner_even_ref, corner_odd_ref)

    def per_query(cells, coefficients):
        turned = jnp.dot(cells.T, coefficients, preferred_element_type=F32)
        mine = jnp.concatenate([turned[:HEAD_DIM, :CELLS], turned[HEAD_DIM:, CELLS:]], axis=0)
        return mine.T

    def body(pair, at):
        own_weights, own_dscore = score_gradient(
            raised_ref[pair, :LON_AT] * stats_ref[pair, 0:1], prob_ref[pair, :LON_AT], stats_ref[pair, 1:2]
        )
        own_ref[0, :, at] = jnp.dot(own_dscore, scaled(q_ref[:, at]), preferred_element_type=F32)
        own_ref[1, :, at] = jnp.dot(own_weights, both_heads(g_ref[:, at]), preferred_element_type=F32)
        keys = jnp.concatenate([k_ref[:, at]] + [part[0, :, at] for part in parts], axis=0)
        values = jnp.concatenate([v_ref[:, at]] + [part[1, :, at] for part in parts], axis=0)
        weights = jnp.concatenate([own_weights, side_weights_ref[pair], corner_weights_ref[pair]], axis=0)
        dscore = jnp.concatenate([own_dscore, side_dscore_ref[pair], corner_dscore_ref[pair]], axis=0)
        out_ref[:, at] = per_query(values, weights).astype(BF16)
        dq_ref[:, at] = (per_query(keys, dscore) * FACTOR).astype(BF16)

    over_pairs(q_ref.shape[1], body)


def middle_kernel(dlon_ref, back_even_ref, back_odd_ref, send_odd_ref, send_even_ref):
    for index, send in enumerate((send_odd_ref, send_even_ref)):
        piece = pl.ds(index * SIDE, SIDE)
        total = dlon_ref[:, piece] + back_even_ref[:, piece].astype(F32) + back_odd_ref[:, piece].astype(F32)
        send[...] = total.astype(BF16)


def final_kernel(own_ref, back_even_ref, back_odd_ref, side_odd_ref, side_even_ref, dk_ref, dv_ref, sum_ref):
    lon_odd = is_odd("lon")
    start_even, start_odd = lat_starts()
    shape = (CELLS, SIDE)
    cell = lax.broadcasted_iota(jnp.int32, shape, 0)
    place = lax.broadcasted_iota(jnp.int32, shape, 1)

    def spread(first_col):
        return (cell == (place % ROWS) * COLS + first_col + place // ROWS).astype(BF16)

    spread_odd = spread(jnp.where(lon_odd, COLS - RADIUS, 0))
    spread_even = spread(jnp.where(lon_odd, 0, COLS - RADIUS))
    for slot, out in ((0, dk_ref), (1, dv_ref)):
        sum_ref[...] = (
            own_ref[slot]
            + jnp.dot(spread_odd, side_odd_ref[slot], preferred_element_type=F32)
            + jnp.dot(spread_even, side_even_ref[slot], preferred_element_type=F32)
        )
        sum_ref[pl.ds(start_even, BAND), :] += back_even_ref[slot].astype(F32)
        sum_ref[pl.ds(start_odd, BAND), :] += back_odd_ref[slot].astype(F32)
        out[...] = sum_ref[...].astype(BF16)


def arr(shape, dtype):
    return jax.ShapeDtypeStruct(shape, dtype)


def call(kernel, name, operands, results, flops=0, **more):
    moved = sum(x.size * x.dtype.itemsize for x in operands)
    return pl.pallas_call(
        kernel,
        out_shape=results,
        compiler_params=pltpu.CompilerParams(vmem_limit_bytes=32 * 1024 * 1024),
        cost_estimate=pl.CostEstimate(flops=flops, bytes_accessed=moved, transcendentals=0),
        name=name,
        **more,
    )(*operands)


def shards(queries, key_cells, value_cells, grad_output, rel_bias):
    block = queries.shape
    heads = rel_bias.shape[0]
    feat = block[-1]
    pairs = feat // PAIR
    cells = arr((CELLS, feat), BF16)
    side, band, corner = (arr((2, rows, feat), BF16) for rows in (SIDE, BAND, 2 * SIDE))
    work = 2 * CELLS * feat
    barrier = lax.optimization_barrier

    arguments = [
        pltpu.with_memory_space_constraint(x.reshape(CELLS, feat), pltpu.HBM)
        for x in (key_cells, value_cells, queries, grad_output)
    ]
    lon_odd, lon_even, k, v, q, g = call(
        pack_kernel, "pack", arguments, [side, side, cells, cells, cells, cells],
        in_specs=[pl.BlockSpec(memory_space=pltpu.HBM)] * 4,
        scratch_shapes=[pltpu.SemaphoreType.DMA((4,))],
    )
    lon_odd = pair_exchange(lon_odd, "lon", 1, True)
    lon_even = pair_exchange(lon_even, "lon", 0, True)
    lat_even, lat_odd = call(rows_kernel, "rows", [k, v], [band, band])
    lat_even = pair_exchange(lat_even, "lat", 0, False)
    lat_odd = pair_exchange(lat_odd, "lat", 1, True)

    rel_bias, _ = barrier((rel_bias, q))
    table, corner_table = call(
        bias_kernel, "bias_table", [rel_bias],
        [arr((heads, NEAR, CELLS), F32), arr((heads, CORNERS, CELLS), F32)], heads * NEAR * CELLS,
        grid=(heads,),
        in_specs=[pl.BlockSpec(rel_bias.shape, lambda i: (0, 0))],
        out_specs=[
            pl.BlockSpec((1, NEAR, CELLS), lambda i: (i, 0, 0)),
            pl.BlockSpec((1, CORNERS, CELLS), lambda i: (i, 0, 0)),
        ],
        scratch_shapes=[pltpu.VMEM((heads, TABLE), F32)],
    )

    lon_odd, lon_even, table, corner_table = barrier((lon_odd, lon_even, table, corner_table))
    lon_odd, lon_even, lat_even, lat_odd = barrier((lon_odd, lon_even, lat_even, lat_odd))
    joined, = call(join_kernel, "join", [lon_odd, lon_even], [corner])
    corner_even = pair_exchange(joined, "lat", 0, False)
    corner_odd = pair_exchange(joined, "lat", 1, False)

    def scored(rows, dtype):
        return [arr((pairs, rows, 2 * CELLS), dtype)] * 2

    stats = arr((pairs, 8, 2 * CELLS), F32)
    near = [k, v, lon_odd, lon_even, lat_even, lat_odd]
    raised, prob, near_stats = call(
        near_kernel, "near", [q, g, *near, table], scored(NEAR, F32) + [stats], 4 * work * NEAR
    )
    back_corner_even, back_corner_odd, corner_weights, corner_dscore, stats = call(
        corner_kernel, "corner", [q, g, corner_even, corner_odd, corner_table, near_stats],
        [corner, corner] + scored(CORNERS, BF16) + [stats], 4 * work * CORNERS,
    )
    back_corner_even = pair_exchange(back_corner_even, "lat", 0, False)
    back_corner_odd = pair_exchange(back_corner_odd, "lat", 1, False)
    dlon, back_even, back_odd, side_weights, side_dscore = call(
        sides_kernel, "sides", [q, g, raised, prob, stats],
        [arr(corner.shape, F32), band, band] + scored(NEAR - LON_AT, BF16), 4 * work * (NEAR - LON_AT),
    )
    back_even = pair_exchange(back_even, "lat", 0, False)
    back_odd = pair_exchange(back_odd, "lat", 1, False)
    send_odd, send_even = call(middle_kernel, "middle", [dlon, back_corner_even, back_corner_odd], [side, side])
    side_odd = pair_exchange(send_odd, "lon", 1, True)
    side_even = pair_exchange(send_even, "lon", 0, True)
    out, dq, own = call(
        own_kernel, "own",
        [q, g, *near, corner_even, corner_odd, raised, prob, stats, side_weights, side_dscore, corner_weights, corner_dscore],
        [cells, cells, arr((2, CELLS, feat), F32)], 4 * work * (NEAR + CORNERS),
    )
    dk, dv = call(
        final_kernel, "final", [own, back_even, back_odd, side_odd, side_even], [cells, cells],
        scratch_shapes=[pltpu.VMEM((CELLS, feat), F32)],
    )
    return tuple(x.reshape(block) for x in (out, dq, dk, dv))


def solution(mesh):
    spec = P("lat", "lon", None)
    return jax.shard_map(
        shards, mesh=mesh, in_specs=(spec, spec, spec, spec, P()), out_specs=(spec,) * 4, check_vma=False
    )
```

```python
import jax
import jax.numpy as jnp
from jax import lax
from jax.experimental import pallas as pl
from jax.experimental.pallas import tpu as pltpu
from jax.sharding import PartitionSpec as P

HEAD_DIM = 64
RADIUS = 6
SPAN = 2 * RADIUS + 1
ROWS = 8
COLS = 16
CELLS = ROWS * COLS
SIDE = ROWS * RADIUS
BAND = RADIUS * COLS
PAIR = 2 * HEAD_DIM
BASE = 336
TABLE = 512
MASKED = -1e30

OWN_AT = 0
LON_AT = CELLS
LAT_AT = LON_AT + 2 * SIDE
NEAR = LAT_AT + 2 * BAND
CORNERS = 4 * SIDE

F32 = jnp.float32
BF16 = jnp.bfloat16


def pair_exchange(value, axis, odd, wrap):
    count = lax.axis_size(axis)
    pairs = []
    for first in range(odd, count, 2):
        second = first + 1
        if second >= count and not wrap:
            continue
        second %= count
        pairs += [(first, second), (second, first)]
    return lax.ppermute(value, axis, pairs)


def odd_rows_exchange(value):
    lats, lons = lax.axis_size("lat"), lax.axis_size("lon")
    pairs = []
    for lat in range(lats):
        for lon in range(lons):
            other = lat + 1 if lat % 2 else lat - 1
            inside = 0 <= other < lats
            target = (other, lon) if inside else (lat, lon ^ 1)
            pairs.append((lat * lons + lon, target[0] * lons + target[1]))
    return lax.ppermute(value, ("lat", "lon"), pairs)


def is_odd(axis):
    return lax.axis_index(axis) % 2 == 1


def pick_matrix(first_col):
    shape = (SIDE, CELLS)
    place = lax.broadcasted_iota(jnp.int32, shape, 0)
    cell = lax.broadcasted_iota(jnp.int32, shape, 1)
    source = (place % ROWS) * COLS + first_col + place // ROWS
    return (cell == source).astype(BF16)


def pack_kernel(k_hbm, v_hbm, q_hbm, g_hbm, lon_odd_ref, lon_even_ref, k_ref, v_ref, q_ref, g_ref, sems):
    copies = [
        pltpu.make_async_copy(source, target, sems.at[index])
        for index, (source, target) in enumerate(((k_hbm, k_ref), (v_hbm, v_ref), (q_hbm, q_ref), (g_hbm, g_ref)))
    ]
    for copy in copies:
        copy.start()
    lon_odd = is_odd("lon")
    pick_odd = pick_matrix(jnp.where(lon_odd, COLS - RADIUS, 0))
    pick_even = pick_matrix(jnp.where(lon_odd, 0, COLS - RADIUS))
    for slot, source in ((0, k_ref), (1, v_ref)):
        copies[slot].wait()
        whole = source[...]
        lon_odd_ref[slot] = jnp.dot(pick_odd, whole, preferred_element_type=F32).astype(BF16)
        lon_even_ref[slot] = jnp.dot(pick_even, whole, preferred_element_type=F32).astype(BF16)
    copies[2].wait()
    copies[3].wait()


def lat_starts():
    lat_odd = is_odd("lat")
    even = jnp.where(lat_odd, 0, CELLS - BAND)
    return pl.multiple_of(even, 32), pl.multiple_of(CELLS - BAND - even, 32)


def rows_kernel(k_ref, v_ref, lat_even_ref, lat_odd_ref):
    for start, out in zip(lat_starts(), (lat_even_ref, lat_odd_ref)):
        out[0] = k_ref[pl.ds(start, BAND), :]
        out[1] = v_ref[pl.ds(start, BAND), :]


def bias_kernel(bias_ref, table_ref, corner_ref, line_ref):
    head = pl.program_id(0)

    @pl.when(head == 0)
    def _():
        shape = (SPAN * SPAN, TABLE)
        entry = lax.broadcasted_iota(jnp.int32, shape, 0)
        offset = BASE - lax.broadcasted_iota(jnp.int32, shape, 1)
        chosen = (offset == (entry // SPAN) * COLS + entry % SPAN).astype(F32)
        line = jnp.dot(bias_ref[...], chosen, preferred_element_type=F32, precision=lax.Precision.HIGHEST)
        offset = BASE - lax.broadcasted_iota(jnp.int32, (1, TABLE), 1)
        valid = (offset >= 0) & (offset < SPAN * COLS) & (offset % COLS < SPAN)
        line_ref[...] = jnp.where(valid, line, MASKED)

    lon_odd = is_odd("lon")
    lat_odd = is_odd("lat")
    has_north = lax.axis_index("lat") > 0
    has_south = lax.axis_index("lat") < lax.axis_size("lat") - 1
    line = jnp.broadcast_to(line_ref[pl.ds(head, 1), :], (8, TABLE))
    by_one = pltpu.roll(line, 0, 1, stride=1, stride_axis=0)
    by_row = pltpu.roll(line, 0, 1, stride=COLS, stride_axis=0)
    query_col = lax.broadcasted_iota(jnp.int32, (8, CELLS), 1) % COLS
    sub = lax.broadcasted_iota(jnp.int32, (8, CELLS), 0)

    def window(source, row, col):
        first = BASE - (COLS * row + col)
        return source[:, first : first + CELLS]

    def near(delta):
        return (delta >= 0) & (delta < SPAN)

    def put(at, values, target=table_ref):
        target[0, pl.ds(pl.multiple_of(at, 8), 8), :] = values

    def cells(at, row, row_count, there):
        for half in range(COLS // 8):
            allowed = near(RADIUS + 8 * half + sub - query_col)
            if there is not None:
                allowed = allowed & there
            for step in range(row_count):
                values = window(by_one, row + step, RADIUS + 8 * half)
                put(at + step * COLS + 8 * half, jnp.where(allowed, values, MASKED))

    def sides(at, row, first_col, there, target=table_ref):
        for step in range(RADIUS):
            allowed = near(first_col + step - query_col)
            if there is not None:
                allowed = allowed & there
            values = window(by_row, row, first_col + step)
            put(at + step * ROWS, jnp.where(allowed, values, MASKED), target)

    west, east = 0, COLS + RADIUS
    west_slot = jnp.where(lon_odd, SIDE, 0)
    east_slot = SIDE - west_slot
    cells(OWN_AT, RADIUS, ROWS, None)
    sides(LON_AT + west_slot, RADIUS, west, None)
    sides(LON_AT + east_slot, RADIUS, east, None)
    north_slot = jnp.where(lat_odd, 0, 1)
    south_slot = 1 - north_slot
    for slot, row, there in ((north_slot, 0, has_north), (south_slot, ROWS + RADIUS, has_south)):
        cells(LAT_AT + slot * BAND, row, RADIUS, there)
        first = row if row else row - (ROWS - RADIUS)
        sides(slot * 2 * SIDE + west_slot, first, west, there, corner_ref)
        sides(slot * 2 * SIDE + east_slot, first, east, there, corner_ref)


LAST = (((1,), (1,)), ((), ()))
FACTOR = HEAD_DIM ** (-0.5)


def join_kernel(lon_odd_ref, lon_even_ref, out_ref):
    out_ref[:, :SIDE] = lon_odd_ref[...]
    out_ref[:, SIDE:] = lon_even_ref[...]


def over_pairs(width, body):
    for pair in range(width // PAIR):
        body(pair, pl.ds(pair * PAIR, PAIR))


def both_heads(block):
    first_head = lax.broadcasted_iota(jnp.int32, block.shape, 1) < HEAD_DIM
    zero = jnp.zeros_like(block)
    return jnp.concatenate([jnp.where(first_head, block, zero), jnp.where(first_head, zero, block)], axis=0)


def scaled(block):
    return both_heads(block * jnp.asarray(FACTOR, BF16))


def pair_scores(keys, values, queries, grads, table_ref, pair):
    scores = lax.dot_general(keys, queries, LAST, preferred_element_type=F32)
    scores = scores + jnp.concatenate([table_ref[2 * pair], table_ref[2 * pair + 1]], axis=1)
    grad_prob = lax.dot_general(values, grads, LAST, preferred_element_type=F32)
    return scores, grad_prob


def column_sum(x):
    return jnp.sum(x, axis=0, keepdims=True)


def score_gradient(probability, grad_prob, row_dot):
    return probability.astype(BF16), (probability * (grad_prob - row_dot)).astype(BF16)


def near_kernel(
    q_ref, g_ref, k_ref, v_ref, lon_odd_ref, lon_even_ref, lat_even_ref, lat_odd_ref, table_ref,
    raised_ref, prob_ref, stats_ref,
):
    parts = (lon_odd_ref, lon_even_ref, lat_even_ref, lat_odd_ref)

    def body(pair, at):
        keys = jnp.concatenate([k_ref[:, at]] + [part[0, :, at] for part in parts], axis=0)
        values = jnp.concatenate([v_ref[:, at]] + [part[1, :, at] for part in parts], axis=0)
        queries, grads = scaled(q_ref[:, at]), both_heads(g_ref[:, at])
        scores, grad_prob = pair_scores(keys, values, queries, grads, table_ref, pair)
        largest = jnp.max(scores, axis=0, keepdims=True)
        raised = jnp.exp(scores - largest)
        raised_ref[pair] = raised
        prob_ref[pair] = grad_prob
        stats_ref[pair, 0:1] = largest
        stats_ref[pair, 1:2] = column_sum(raised)
        stats_ref[pair, 2:3] = column_sum(raised * grad_prob)

    over_pairs(q_ref.shape[1], body)


def corner_kernel(
    q_ref, g_ref, corner_even_ref, corner_odd_ref, table_ref, near_stats_ref,
    back_even_ref, back_odd_ref, weights_ref, dscore_ref, stats_ref,
):
    def body(pair, at):
        keys = jnp.concatenate([corner_even_ref[0, :, at], corner_odd_ref[0, :, at]], axis=0)
        values = jnp.concatenate([corner_even_ref[1, :, at], corner_odd_ref[1, :, at]], axis=0)
        queries, grads = scaled(q_ref[:, at]), both_heads(g_ref[:, at])
        scores, grad_prob = pair_scores(keys, values, queries, grads, table_ref, pair)
        near_largest = near_stats_ref[pair, 0:1]
        largest = jnp.maximum(near_largest, jnp.max(scores, axis=0, keepdims=True))
        raised = jnp.exp(scores - largest)
        shift = jnp.exp(near_largest - largest)
        total = near_stats_ref[pair, 1:2] * shift + column_sum(raised)
        inverse = 1.0 / total
        near_scale = shift * inverse
        row_dot = near_stats_ref[pair, 2:3] * near_scale + column_sum(raised * grad_prob) * inverse
        stats_ref[pair, 0:1] = near_scale
        stats_ref[pair, 1:2] = row_dot
        weights, dscore = score_gradient(raised * inverse, grad_prob, row_dot)
        weights_ref[pair] = weights
        dscore_ref[pair] = dscore
        for slot, coefficients, other in ((0, dscore, queries), (1, weights, grads)):
            grad = jnp.dot(coefficients, other, preferred_element_type=F32).astype(BF16)
            back_even_ref[slot, :, at] = grad[: 2 * SIDE]
            back_odd_ref[slot, :, at] = grad[2 * SIDE :]

    over_pairs(q_ref.shape[1], body)


def sides_kernel(
    q_ref, g_ref, raised_ref, prob_ref, stats_ref,
    dlon_ref, back_even_ref, back_odd_ref, weights_ref, dscore_ref,
):
    def body(pair, at):
        weights, dscore = score_gradient(
            raised_ref[pair, LON_AT:] * stats_ref[pair, 0:1], prob_ref[pair, LON_AT:], stats_ref[pair, 1:2]
        )
        weights_ref[pair] = weights
        dscore_ref[pair] = dscore
        for slot, coefficients, other in ((0, dscore, scaled(q_ref[:, at])), (1, weights, both_heads(g_ref[:, at]))):
            grad = jnp.dot(coefficients, other, preferred_element_type=F32)
            dlon_ref[slot, :, at] = grad[: 2 * SIDE]
            back_even_ref[slot, :, at] = grad[2 * SIDE : 2 * SIDE + BAND].astype(BF16)
            back_odd_ref[slot, :, at] = grad[2 * SIDE + BAND :].astype(BF16)

    over_pairs(q_ref.shape[1], body)


def own_kernel(
    q_ref, g_ref, k_ref, v_ref, lon_odd_ref, lon_even_ref, lat_even_ref, lat_odd_ref, corner_even_ref, corner_odd_ref,
    raised_ref, prob_ref, stats_ref, side_weights_ref, side_dscore_ref, corner_weights_ref, corner_dscore_ref,
    out_ref, dq_ref, own_ref,
):
    parts = (lon_odd_ref, lon_even_ref, lat_even_ref, lat_odd_ref, corner_even_ref, corner_odd_ref)

    def per_query(cells, coefficients):
        turned = jnp.dot(cells.T, coefficients, preferred_element_type=F32)
        mine = jnp.concatenate([turned[:HEAD_DIM, :CELLS], turned[HEAD_DIM:, CELLS:]], axis=0)
        return mine.T

    def body(pair, at):
        own_weights, own_dscore = score_gradient(
            raised_ref[pair, :LON_AT] * stats_ref[pair, 0:1], prob_ref[pair, :LON_AT], stats_ref[pair, 1:2]
        )
        own_ref[0, :, at] = jnp.dot(own_dscore, scaled(q_ref[:, at]), preferred_element_type=F32)
        own_ref[1, :, at] = jnp.dot(own_weights, both_heads(g_ref[:, at]), preferred_element_type=F32)
        keys = jnp.concatenate([k_ref[:, at]] + [part[0, :, at] for part in parts], axis=0)
        values = jnp.concatenate([v_ref[:, at]] + [part[1, :, at] for part in parts], axis=0)
        weights = jnp.concatenate([own_weights, side_weights_ref[pair], corner_weights_ref[pair]], axis=0)
        dscore = jnp.concatenate([own_dscore, side_dscore_ref[pair], corner_dscore_ref[pair]], axis=0)
        out_ref[:, at] = per_query(values, weights).astype(BF16)
        dq_ref[:, at] = (per_query(keys, dscore) * FACTOR).astype(BF16)

    over_pairs(q_ref.shape[1], body)


def middle_kernel(dlon_ref, back_even_ref, back_odd_ref, send_odd_ref, send_even_ref):
    for index, send in enumerate((send_odd_ref, send_even_ref)):
        piece = pl.ds(index * SIDE, SIDE)
        total = dlon_ref[:, piece] + back_even_ref[:, piece].astype(F32) + back_odd_ref[:, piece].astype(F32)
        send[...] = total.astype(BF16)


def final_kernel(own_ref, back_even_ref, back_odd_ref, side_odd_ref, side_even_ref, dk_ref, dv_ref, sum_ref):
    lon_odd = is_odd("lon")
    start_even, start_odd = lat_starts()
    shape = (CELLS, SIDE)
    cell = lax.broadcasted_iota(jnp.int32, shape, 0)
    place = lax.broadcasted_iota(jnp.int32, shape, 1)

    def spread(first_col):
        return (cell == (place % ROWS) * COLS + first_col + place // ROWS).astype(BF16)

    spread_odd = spread(jnp.where(lon_odd, COLS - RADIUS, 0))
    spread_even = spread(jnp.where(lon_odd, 0, COLS - RADIUS))
    for slot, out in ((0, dk_ref), (1, dv_ref)):
        sum_ref[...] = (
            own_ref[slot]
            + jnp.dot(spread_odd, side_odd_ref[slot], preferred_element_type=F32)
            + jnp.dot(spread_even, side_even_ref[slot], preferred_element_type=F32)
        )
        sum_ref[pl.ds(start_even, BAND), :] += back_even_ref[slot].astype(F32)
        sum_ref[pl.ds(start_odd, BAND), :] += back_odd_ref[slot].astype(F32)
        out[...] = sum_ref[...].astype(BF16)


def arr(shape, dtype):
    return jax.ShapeDtypeStruct(shape, dtype)


def call(kernel, name, operands, results, flops=0, **more):
    moved = sum(x.size * x.dtype.itemsize for x in operands)
    return pl.pallas_call(
        kernel,
        out_shape=results,
        compiler_params=pltpu.CompilerParams(vmem_limit_bytes=32 * 1024 * 1024),
        cost_estimate=pl.CostEstimate(flops=flops, bytes_accessed=moved, transcendentals=0),
        name=name,
        **more,
    )(*operands)


def shards(queries, key_cells, value_cells, grad_output, rel_bias):
    block = queries.shape
    heads = rel_bias.shape[0]
    feat = block[-1]
    pairs = feat // PAIR
    cells = arr((CELLS, feat), BF16)
    side, band, corner = (arr((2, rows, feat), BF16) for rows in (SIDE, BAND, 2 * SIDE))
    work = 2 * CELLS * feat
    barrier = lax.optimization_barrier

    arguments = [
        pltpu.with_memory_space_constraint(x.reshape(CELLS, feat), pltpu.HBM)
        for x in (key_cells, value_cells, queries, grad_output)
    ]
    lon_odd, lon_even, k, v, q, g = call(
        pack_kernel, "pack", arguments, [side, side, cells, cells, cells, cells],
        in_specs=[pl.BlockSpec(memory_space=pltpu.HBM)] * 4,
        scratch_shapes=[pltpu.SemaphoreType.DMA((4,))],
    )
    lon_odd = pair_exchange(lon_odd, "lon", 1, True)
    lon_even = pair_exchange(lon_even, "lon", 0, True)
    lat_even, lat_odd = call(rows_kernel, "rows", [k, v], [band, band])
    lat_even = pair_exchange(lat_even, "lat", 0, False)
    lat_odd = pair_exchange(lat_odd, "lat", 1, True)

    rel_bias, _ = barrier((rel_bias, q))
    table, corner_table = call(
        bias_kernel, "bias_table", [rel_bias],
        [arr((heads, NEAR, CELLS), F32), arr((heads, CORNERS, CELLS), F32)], heads * NEAR * CELLS,
        grid=(heads,),
        in_specs=[pl.BlockSpec(rel_bias.shape, lambda i: (0, 0))],
        out_specs=[
            pl.BlockSpec((1, NEAR, CELLS), lambda i: (i, 0, 0)),
            pl.BlockSpec((1, CORNERS, CELLS), lambda i: (i, 0, 0)),
        ],
        scratch_shapes=[pltpu.VMEM((heads, TABLE), F32)],
    )

    lon_odd, lon_even, table, corner_table = barrier((lon_odd, lon_even, table, corner_table))
    joined, = call(join_kernel, "join", [lon_odd, lon_even], [corner])
    corner_even = pair_exchange(joined, "lat", 0, False)
    corner_odd = odd_rows_exchange(joined)

    def scored(rows, dtype):
        return [arr((pairs, rows, 2 * CELLS), dtype)] * 2

    stats = arr((pairs, 8, 2 * CELLS), F32)
    near = [k, v, lon_odd, lon_even, lat_even, lat_odd]
    raised, prob, near_stats = call(
        near_kernel, "near", [q, g, *near, table], scored(NEAR, F32) + [stats], 4 * work * NEAR
    )
    back_corner_even, back_corner_odd, corner_weights, corner_dscore, stats = call(
        corner_kernel, "corner", [q, g, corner_even, corner_odd, corner_table, near_stats],
        [corner, corner] + scored(CORNERS, BF16) + [stats], 4 * work * CORNERS,
    )
    back_corner_even = pair_exchange(back_corner_even, "lat", 0, False)
    back_corner_odd = odd_rows_exchange(back_corner_odd)
    dlon, back_even, back_odd, side_weights, side_dscore = call(
        sides_kernel, "sides", [q, g, raised, prob, stats],
        [arr(corner.shape, F32), band, band] + scored(NEAR - LON_AT, BF16), 4 * work * (NEAR - LON_AT),
    )
    back_even = pair_exchange(back_even, "lat", 0, False)
    back_odd = odd_rows_exchange(back_odd)
    send_odd, send_even = call(middle_kernel, "middle", [dlon, back_corner_even, back_corner_odd], [side, side])
    side_odd = pair_exchange(send_odd, "lon", 1, True)
    side_even = pair_exchange(send_even, "lon", 0, True)
    out, dq, own = call(
        own_kernel, "own",
        [q, g, *near, corner_even, corner_odd, raised, prob, stats, side_weights, side_dscore, corner_weights, corner_dscore],
        [cells, cells, arr((2, CELLS, feat), F32)], 4 * work * (NEAR + CORNERS),
    )
    dk, dv = call(
        final_kernel, "final", [own, back_even, back_odd, side_odd, side_even], [cells, cells],
        scratch_shapes=[pltpu.VMEM((CELLS, feat), F32)],
    )
    return tuple(x.reshape(block) for x in (out, dq, dk, dv))


def solution(mesh):
    spec = P("lat", "lon", None)
    return jax.shard_map(
        shards, mesh=mesh, in_specs=(spec, spec, spec, spec, P()), out_specs=(spec,) * 4, check_vma=False
    )
```

```python
import jax
import jax.numpy as jnp
from jax import lax
from jax.experimental import pallas as pl
from jax.experimental.pallas import tpu as pltpu
from jax.sharding import PartitionSpec as P

HEAD_DIM = 64
RADIUS = 6
SPAN = 2 * RADIUS + 1
ROWS = 8
COLS = 16
CELLS = ROWS * COLS
SIDE = ROWS * RADIUS
BAND = RADIUS * COLS
PAIR = 2 * HEAD_DIM
BASE = 336
TABLE = 512
MASKED = -1e30

OWN_AT = 0
LON_AT = CELLS
LAT_AT = LON_AT + 2 * SIDE
NEAR = LAT_AT + 2 * BAND
CORNERS = 4 * SIDE

F32 = jnp.float32
BF16 = jnp.bfloat16


def pair_exchange(value, axis, odd, wrap):
    count = lax.axis_size(axis)
    pairs = []
    for first in range(odd, count, 2):
        second = first + 1
        if second >= count and not wrap:
            continue
        second %= count
        pairs += [(first, second), (second, first)]
    return lax.ppermute(value, axis, pairs)


def odd_rows_exchange(value):
    lats, lons = lax.axis_size("lat"), lax.axis_size("lon")
    pairs = []
    for lat in range(lats):
        for lon in range(lons):
            other = lat + 1 if lat % 2 else lat - 1
            inside = 0 <= other < lats
            target = (other, lon) if inside else (lat, lon ^ 1)
            pairs.append((lat * lons + lon, target[0] * lons + target[1]))
    return lax.ppermute(value, ("lat", "lon"), pairs)


def is_odd(axis):
    return lax.axis_index(axis) % 2 == 1


def pick_matrix(first_col):
    shape = (SIDE, CELLS)
    place = lax.broadcasted_iota(jnp.int32, shape, 0)
    cell = lax.broadcasted_iota(jnp.int32, shape, 1)
    source = (place % ROWS) * COLS + first_col + place // ROWS
    return (cell == source).astype(BF16)


def pack_kernel(k_hbm, v_hbm, bias_hbm, lon_odd_ref, lon_even_ref, k_ref, v_ref, bias_ref, sems):
    copies = [
        pltpu.make_async_copy(source, target, sems.at[index])
        for index, (source, target) in enumerate(((k_hbm, k_ref), (v_hbm, v_ref), (bias_hbm, bias_ref)))
    ]
    for copy in copies:
        copy.start()
    lon_odd = is_odd("lon")
    pick_odd = pick_matrix(jnp.where(lon_odd, COLS - RADIUS, 0))
    pick_even = pick_matrix(jnp.where(lon_odd, 0, COLS - RADIUS))
    for slot, source in ((0, k_ref), (1, v_ref)):
        copies[slot].wait()
        whole = source[...]
        lon_odd_ref[slot] = jnp.dot(pick_odd, whole, preferred_element_type=F32).astype(BF16)
        lon_even_ref[slot] = jnp.dot(pick_even, whole, preferred_element_type=F32).astype(BF16)
    copies[2].wait()


def lat_starts():
    lat_odd = is_odd("lat")
    even = jnp.where(lat_odd, 0, CELLS - BAND)
    return pl.multiple_of(even, 32), pl.multiple_of(CELLS - BAND - even, 32)


def rows_kernel(k_ref, v_ref, lat_even_ref, lat_odd_ref):
    for start, out in zip(lat_starts(), (lat_even_ref, lat_odd_ref)):
        out[0] = k_ref[pl.ds(start, BAND), :]
        out[1] = v_ref[pl.ds(start, BAND), :]


def bias_kernel(bias_ref, q_hbm, g_hbm, table_ref, corner_ref, q_ref, g_ref, line_ref, sems):
    copies = [
        pltpu.make_async_copy(source, target, sems.at[index])
        for index, (source, target) in enumerate(((q_hbm, q_ref), (g_hbm, g_ref)))
    ]
    for copy in copies:
        copy.start()
    lon_odd = is_odd("lon")
    lat_odd = is_odd("lat")
    has_north = lax.axis_index("lat") > 0
    has_south = lax.axis_index("lat") < lax.axis_size("lat") - 1
    shape = (SPAN * SPAN, TABLE)
    entry = lax.broadcasted_iota(jnp.int32, shape, 0)
    offset = BASE - lax.broadcasted_iota(jnp.int32, shape, 1)
    chosen = (offset == (entry // SPAN) * COLS + entry % SPAN).astype(F32)
    lines = jnp.dot(bias_ref[...], chosen, preferred_element_type=F32, precision=lax.Precision.HIGHEST)
    offset = BASE - lax.broadcasted_iota(jnp.int32, (1, TABLE), 1)
    valid = (offset >= 0) & (offset < SPAN * COLS) & (offset % COLS < SPAN)
    line_ref[...] = jnp.where(valid, lines, MASKED)
    query_col = lax.broadcasted_iota(jnp.int32, (8, CELLS), 1) % COLS
    sub = lax.broadcasted_iota(jnp.int32, (8, CELLS), 0)

    def near(delta):
        return (delta >= 0) & (delta < SPAN)

    west, east = 0, COLS + RADIUS
    west_slot = jnp.where(lon_odd, SIDE, 0)
    east_slot = SIDE - west_slot
    north_slot = jnp.where(lat_odd, 0, 1)
    south_slot = 1 - north_slot

    def fill(head, carry):
        line = jnp.broadcast_to(line_ref[pl.ds(head, 1), :], (8, TABLE))
        by_one = pltpu.roll(line, 0, 1, stride=1, stride_axis=0)
        by_row = pltpu.roll(line, 0, 1, stride=COLS, stride_axis=0)

        def window(source, row, col):
            first = BASE - (COLS * row + col)
            return source[:, first : first + CELLS]

        def put(at, values, allowed, target):
            target[head, pl.ds(pl.multiple_of(at, 8), 8), :] = jnp.where(allowed, values, MASKED)

        def cells(at, row, row_count, there):
            for half in range(COLS // 8):
                allowed = near(RADIUS + 8 * half + sub - query_col)
                if there is not None:
                    allowed = allowed & there
                for step in range(row_count):
                    values = window(by_one, row + step, RADIUS + 8 * half)
                    put(at + step * COLS + 8 * half, values, allowed, table_ref)

        def sides(at, row, first_col, there, target):
            for step in range(RADIUS):
                allowed = near(first_col + step - query_col)
                if there is not None:
                    allowed = allowed & there
                put(at + step * ROWS, window(by_row, row, first_col + step), allowed, target)

        cells(OWN_AT, RADIUS, ROWS, None)
        sides(LON_AT + west_slot, RADIUS, west, None, table_ref)
        sides(LON_AT + east_slot, RADIUS, east, None, table_ref)
        for slot, row, there in ((north_slot, 0, has_north), (south_slot, ROWS + RADIUS, has_south)):
            cells(LAT_AT + slot * BAND, row, RADIUS, there)
            first = row if row else row - (ROWS - RADIUS)
            sides(slot * 2 * SIDE + west_slot, first, west, there, corner_ref)
            sides(slot * 2 * SIDE + east_slot, first, east, there, corner_ref)
        return carry

    lax.fori_loop(0, bias_ref.shape[0], fill, 0)
    for copy in copies:
        copy.wait()


LAST = (((1,), (1,)), ((), ()))
FACTOR = HEAD_DIM ** (-0.5)


def join_kernel(lon_odd_ref, lon_even_ref, out_ref):
    out_ref[:, :SIDE] = lon_odd_ref[...]
    out_ref[:, SIDE:] = lon_even_ref[...]


def over_pairs(width, body):
    for pair in range(width // PAIR):
        body(pair, pl.ds(pair * PAIR, PAIR))


def both_heads(block):
    first_head = lax.broadcasted_iota(jnp.int32, block.shape, 1) < HEAD_DIM
    zero = jnp.zeros_like(block)
    return jnp.concatenate([jnp.where(first_head, block, zero), jnp.where(first_head, zero, block)], axis=0)


def scaled(block):
    return both_heads(block * jnp.asarray(FACTOR, BF16))


def pair_scores(keys, values, queries, grads, table_ref, pair):
    scores = lax.dot_general(keys, queries, LAST, preferred_element_type=F32)
    scores = scores + jnp.concatenate([table_ref[2 * pair], table_ref[2 * pair + 1]], axis=1)
    grad_prob = lax.dot_general(values, grads, LAST, preferred_element_type=F32)
    return scores, grad_prob


def column_sum(x):
    return jnp.sum(x, axis=0, keepdims=True)


def score_gradient(probability, grad_prob, row_dot):
    return probability.astype(BF16), (probability * (grad_prob - row_dot)).astype(BF16)


def near_kernel(
    q_ref, g_ref, k_ref, v_ref, lon_odd_ref, lon_even_ref, lat_even_ref, lat_odd_ref, table_ref,
    raised_ref, prob_ref, stats_ref,
):
    parts = (lon_odd_ref, lon_even_ref, lat_even_ref, lat_odd_ref)

    def body(pair, at):
        keys = jnp.concatenate([k_ref[:, at]] + [part[0, :, at] for part in parts], axis=0)
        values = jnp.concatenate([v_ref[:, at]] + [part[1, :, at] for part in parts], axis=0)
        queries, grads = scaled(q_ref[:, at]), both_heads(g_ref[:, at])
        scores, grad_prob = pair_scores(keys, values, queries, grads, table_ref, pair)
        largest = jnp.max(scores, axis=0, keepdims=True)
        raised = jnp.exp(scores - largest)
        raised_ref[pair] = raised
        prob_ref[pair] = grad_prob
        stats_ref[pair, 0:1] = largest
        stats_ref[pair, 1:2] = column_sum(raised)
        stats_ref[pair, 2:3] = column_sum(raised * grad_prob)

    over_pairs(q_ref.shape[1], body)


def corner_kernel(
    q_ref, g_ref, corner_even_ref, corner_odd_ref, table_ref, near_stats_ref,
    back_even_ref, back_odd_ref, weights_ref, dscore_ref, stats_ref,
):
    scored = []

    def score(pair, at):
        keys = jnp.concatenate([corner_even_ref[0, :, at], corner_odd_ref[0, :, at]], axis=0)
        values = jnp.concatenate([corner_even_ref[1, :, at], corner_odd_ref[1, :, at]], axis=0)
        queries, grads = scaled(q_ref[:, at]), both_heads(g_ref[:, at])
        scored.append((queries, grads, *pair_scores(keys, values, queries, grads, table_ref, pair)))

    over_pairs(q_ref.shape[1], score)

    def differentiate(pair, at):
        queries, grads, scores, grad_prob = scored[pair]
        near_largest = near_stats_ref[pair, 0:1]
        largest = jnp.maximum(near_largest, jnp.max(scores, axis=0, keepdims=True))
        raised = jnp.exp(scores - largest)
        shift = jnp.exp(near_largest - largest)
        total = near_stats_ref[pair, 1:2] * shift + column_sum(raised)
        inverse = 1.0 / total
        near_scale = shift * inverse
        row_dot = near_stats_ref[pair, 2:3] * near_scale + column_sum(raised * grad_prob) * inverse
        stats_ref[pair, 0:1] = near_scale
        stats_ref[pair, 1:2] = row_dot
        weights, dscore = score_gradient(raised * inverse, grad_prob, row_dot)
        weights_ref[pair] = weights
        dscore_ref[pair] = dscore
        for slot, coefficients, other in ((0, dscore, queries), (1, weights, grads)):
            grad = jnp.dot(coefficients, other, preferred_element_type=F32).astype(BF16)
            back_even_ref[slot, :, at] = grad[: 2 * SIDE]
            back_odd_ref[slot, :, at] = grad[2 * SIDE :]

    over_pairs(q_ref.shape[1], differentiate)


def sides_kernel(
    q_ref, g_ref, raised_ref, prob_ref, stats_ref,
    dlon_ref, back_even_ref, back_odd_ref, weights_ref, dscore_ref,
):
    def body(pair, at):
        weights, dscore = score_gradient(
            raised_ref[pair, LON_AT:] * stats_ref[pair, 0:1], prob_ref[pair, LON_AT:], stats_ref[pair, 1:2]
        )
        weights_ref[pair] = weights
        dscore_ref[pair] = dscore
        for slot, coefficients, other in ((0, dscore, scaled(q_ref[:, at])), (1, weights, both_heads(g_ref[:, at]))):
            grad = jnp.dot(coefficients, other, preferred_element_type=F32)
            dlon_ref[slot, :, at] = grad[: 2 * SIDE]
            back_even_ref[slot, :, at] = grad[2 * SIDE : 2 * SIDE + BAND].astype(BF16)
            back_odd_ref[slot, :, at] = grad[2 * SIDE + BAND :].astype(BF16)

    over_pairs(q_ref.shape[1], body)


def own_kernel(
    q_ref, g_ref, k_ref, v_ref, lon_odd_ref, lon_even_ref, lat_even_ref, lat_odd_ref, corner_even_ref, corner_odd_ref,
    raised_ref, prob_ref, stats_ref, side_weights_ref, side_dscore_ref, corner_weights_ref, corner_dscore_ref,
    out_ref, dq_ref, own_ref,
):
    parts = (lon_odd_ref, lon_even_ref, lat_even_ref, lat_odd_ref, corner_even_ref, corner_odd_ref)

    def per_query(cells, coefficients):
        turned = jnp.dot(cells.T, coefficients, preferred_element_type=F32)
        mine = jnp.concatenate([turned[:HEAD_DIM, :CELLS], turned[HEAD_DIM:, CELLS:]], axis=0)
        return mine.T

    def body(pair, at):
        own_weights, own_dscore = score_gradient(
            raised_ref[pair, :LON_AT] * stats_ref[pair, 0:1], prob_ref[pair, :LON_AT], stats_ref[pair, 1:2]
        )
        own_ref[0, :, at] = jnp.dot(own_dscore, scaled(q_ref[:, at]), preferred_element_type=F32)
        own_ref[1, :, at] = jnp.dot(own_weights, both_heads(g_ref[:, at]), preferred_element_type=F32)
        keys = jnp.concatenate([k_ref[:, at]] + [part[0, :, at] for part in parts], axis=0)
        values = jnp.concatenate([v_ref[:, at]] + [part[1, :, at] for part in parts], axis=0)
        weights = jnp.concatenate([own_weights, side_weights_ref[pair], corner_weights_ref[pair]], axis=0)
        dscore = jnp.concatenate([own_dscore, side_dscore_ref[pair], corner_dscore_ref[pair]], axis=0)
        out_ref[:, at] = per_query(values, weights).astype(BF16)
        dq_ref[:, at] = (per_query(keys, dscore) * FACTOR).astype(BF16)

    over_pairs(q_ref.shape[1], body)


def middle_kernel(dlon_ref, back_even_ref, back_odd_ref, send_odd_ref, send_even_ref):
    for index, send in enumerate((send_odd_ref, send_even_ref)):
        piece = pl.ds(index * SIDE, SIDE)
        total = dlon_ref[:, piece] + back_even_ref[:, piece].astype(F32) + back_odd_ref[:, piece].astype(F32)
        send[...] = total.astype(BF16)


def final_kernel(own_ref, back_even_ref, back_odd_ref, side_odd_ref, side_even_ref, dk_ref, dv_ref, sum_ref):
    lon_odd = is_odd("lon")
    start_even, start_odd = lat_starts()
    shape = (CELLS, SIDE)
    cell = lax.broadcasted_iota(jnp.int32, shape, 0)
    place = lax.broadcasted_iota(jnp.int32, shape, 1)

    def spread(first_col):
        return (cell == (place % ROWS) * COLS + first_col + place // ROWS).astype(BF16)

    spread_odd = spread(jnp.where(lon_odd, COLS - RADIUS, 0))
    spread_even = spread(jnp.where(lon_odd, 0, COLS - RADIUS))
    for slot, out in ((0, dk_ref), (1, dv_ref)):
        sum_ref[...] = (
            own_ref[slot]
            + jnp.dot(spread_odd, side_odd_ref[slot], preferred_element_type=F32)
            + jnp.dot(spread_even, side_even_ref[slot], preferred_element_type=F32)
        )
        sum_ref[pl.ds(start_even, BAND), :] += back_even_ref[slot].astype(F32)
        sum_ref[pl.ds(start_odd, BAND), :] += back_odd_ref[slot].astype(F32)
        out[...] = sum_ref[...].astype(BF16)


def arr(shape, dtype):
    return jax.ShapeDtypeStruct(shape, dtype)


def call(kernel, name, operands, results, flops=0, **more):
    moved = sum(x.size * x.dtype.itemsize for x in operands)
    return pl.pallas_call(
        kernel,
        out_shape=results,
        compiler_params=pltpu.CompilerParams(vmem_limit_bytes=32 * 1024 * 1024),
        cost_estimate=pl.CostEstimate(flops=flops, bytes_accessed=moved, transcendentals=0),
        name=name,
        **more,
    )(*operands)


def shards(queries, key_cells, value_cells, grad_output, rel_bias):
    block = queries.shape
    heads = rel_bias.shape[0]
    feat = block[-1]
    pairs = feat // PAIR
    cells = arr((CELLS, feat), BF16)
    side, band, corner = (arr((2, rows, feat), BF16) for rows in (SIDE, BAND, 2 * SIDE))
    work = 2 * CELLS * feat
    barrier = lax.optimization_barrier

    def in_hbm(x):
        return pltpu.with_memory_space_constraint(x, pltpu.HBM)

    hbm, vmem = (pl.BlockSpec(memory_space=space) for space in (pltpu.HBM, pltpu.VMEM))
    arguments = [in_hbm(x) for x in (key_cells.reshape(CELLS, feat), value_cells.reshape(CELLS, feat), rel_bias)]
    lon_odd, lon_even, k, v, rel_bias = call(
        pack_kernel, "pack", arguments, [side, side, cells, cells, arr(rel_bias.shape, F32)],
        in_specs=[hbm] * 3,
        scratch_shapes=[pltpu.SemaphoreType.DMA((3,))],
    )
    lon_odd = pair_exchange(lon_odd, "lon", 1, True)
    lon_even = pair_exchange(lon_even, "lon", 0, True)
    lat_even, lat_odd = call(rows_kernel, "rows", [k, v], [band, band])
    lat_even = pair_exchange(lat_even, "lat", 0, False)
    lat_odd = pair_exchange(lat_odd, "lat", 1, True)

    table, corner_table, q, g = call(
        bias_kernel, "bias_table",
        [rel_bias, in_hbm(queries.reshape(CELLS, feat)), in_hbm(grad_output.reshape(CELLS, feat))],
        [arr((heads, NEAR, CELLS), F32), arr((heads, CORNERS, CELLS), F32), cells, cells], heads * NEAR * CELLS,
        in_specs=[vmem, hbm, hbm],
        scratch_shapes=[pltpu.VMEM((heads, TABLE), F32), pltpu.SemaphoreType.DMA((2,))],
    )

    lon_odd, lon_even, table, corner_table = barrier((lon_odd, lon_even, table, corner_table))
    joined, = call(join_kernel, "join", [lon_odd, lon_even], [corner])
    corner_even = pair_exchange(joined, "lat", 0, False)
    corner_odd = odd_rows_exchange(joined)

    def scored(rows, dtype):
        return [arr((pairs, rows, 2 * CELLS), dtype)] * 2

    stats = arr((pairs, 8, 2 * CELLS), F32)
    near = [k, v, lon_odd, lon_even, lat_even, lat_odd]
    raised, prob, near_stats = call(
        near_kernel, "near", [q, g, *near, table], scored(NEAR, F32) + [stats], 4 * work * NEAR
    )
    back_corner_even, back_corner_odd, corner_weights, corner_dscore, stats = call(
        corner_kernel, "corner", [q, g, corner_even, corner_odd, corner_table, near_stats],
        [corner, corner] + scored(CORNERS, BF16) + [stats], 4 * work * CORNERS,
    )
    back_corner_even = pair_exchange(back_corner_even, "lat", 0, False)
    back_corner_odd = odd_rows_exchange(back_corner_odd)
    dlon, back_even, back_odd, side_weights, side_dscore = call(
        sides_kernel, "sides", [q, g, raised, prob, stats],
        [arr(corner.shape, F32), band, band] + scored(NEAR - LON_AT, BF16), 4 * work * (NEAR - LON_AT),
    )
    back_even = pair_exchange(back_even, "lat", 0, False)
    back_odd = odd_rows_exchange(back_odd)
    send_odd, send_even = call(middle_kernel, "middle", [dlon, back_corner_even, back_corner_odd], [side, side])
    side_odd = pair_exchange(send_odd, "lon", 1, True)
    side_even = pair_exchange(send_even, "lon", 0, True)
    out, dq, own = call(
        own_kernel, "own",
        [q, g, *near, corner_even, corner_odd, raised, prob, stats, side_weights, side_dscore, corner_weights, corner_dscore],
        [cells, cells, arr((2, CELLS, feat), F32)], 4 * work * (NEAR + CORNERS),
    )
    dk, dv = call(
        final_kernel, "final", [own, back_even, back_odd, side_odd, side_even], [cells, cells],
        scratch_shapes=[pltpu.VMEM((CELLS, feat), F32)],
    )
    return tuple(x.reshape(block) for x in (out, dq, dk, dv))


def solution(mesh):
    spec = P("lat", "lon", None)
    return jax.shard_map(
        shards, mesh=mesh, in_specs=(spec, spec, spec, spec, P()), out_specs=(spec,) * 4, check_vma=False
    )
```

```python
import functools

import jax
import jax.numpy as jnp
from jax import lax
from jax.experimental import pallas as pl
from jax.experimental.pallas import tpu as pltpu
from jax.sharding import PartitionSpec as P

HEAD_DIM = 64
RADIUS = 6
SPAN = 2 * RADIUS + 1
ROWS = 8
COLS = 16
CELLS = ROWS * COLS
SIDE = ROWS * RADIUS
BAND = RADIUS * COLS
PAIR = 2 * HEAD_DIM
BASE = 336
TABLE = 512
MASKED = -1e30

OWN_AT = 0
LON_AT = CELLS
LAT_AT = LON_AT + 2 * SIDE
NEAR = LAT_AT + 2 * BAND
CORNERS = 4 * SIDE

F32 = jnp.float32
BF16 = jnp.bfloat16


def pair_exchange(value, axis, odd, wrap):
    count = lax.axis_size(axis)
    pairs = []
    for first in range(odd, count, 2):
        second = first + 1
        if second >= count and not wrap:
            continue
        second %= count
        pairs += [(first, second), (second, first)]
    return lax.ppermute(value, axis, pairs)


def odd_rows_exchange(value):
    lats, lons = lax.axis_size("lat"), lax.axis_size("lon")
    pairs = []
    for lat in range(lats):
        for lon in range(lons):
            other = lat + 1 if lat % 2 else lat - 1
            inside = 0 <= other < lats
            target = (other, lon) if inside else (lat, lon ^ (1 if lons % 4 else 2))
            pairs.append((lat * lons + lon, target[0] * lons + target[1]))
    return lax.ppermute(value, ("lat", "lon"), pairs)


def is_odd(axis):
    return lax.axis_index(axis) % 2 == 1


def pick_matrix(first_col):
    shape = (SIDE, CELLS)
    place = lax.broadcasted_iota(jnp.int32, shape, 0)
    cell = lax.broadcasted_iota(jnp.int32, shape, 1)
    source = (place % ROWS) * COLS + first_col + place // ROWS
    return (cell == source).astype(BF16)


def pack_kernel(k_hbm, v_hbm, bias_hbm, lon_odd_ref, lon_even_ref, k_ref, v_ref, bias_ref, sems):
    copies = [
        pltpu.make_async_copy(source, target, sems.at[index])
        for index, (source, target) in enumerate(((k_hbm, k_ref), (v_hbm, v_ref), (bias_hbm, bias_ref)))
    ]
    for copy in copies:
        copy.start()
    lon_odd = is_odd("lon")
    pick_odd = pick_matrix(jnp.where(lon_odd, COLS - RADIUS, 0))
    pick_even = pick_matrix(jnp.where(lon_odd, 0, COLS - RADIUS))
    for slot, source in ((0, k_ref), (1, v_ref)):
        copies[slot].wait()
        whole = source[...]
        lon_odd_ref[slot] = jnp.dot(pick_odd, whole, preferred_element_type=F32).astype(BF16)
        lon_even_ref[slot] = jnp.dot(pick_even, whole, preferred_element_type=F32).astype(BF16)
    copies[2].wait()


def lat_starts():
    lat_odd = is_odd("lat")
    even = jnp.where(lat_odd, 0, CELLS - BAND)
    return pl.multiple_of(even, 32), pl.multiple_of(CELLS - BAND - even, 32)


def rows_kernel(k_ref, v_ref, lat_even_ref, lat_odd_ref):
    for start, out in zip(lat_starts(), (lat_even_ref, lat_odd_ref)):
        out[0] = k_ref[pl.ds(start, BAND), :]
        out[1] = v_ref[pl.ds(start, BAND), :]


def bias_kernel(bias_ref, q_hbm, g_hbm, table_ref, corner_ref, q_ref, g_ref, line_ref, sems):
    copies = [
        pltpu.make_async_copy(source, target, sems.at[index])
        for index, (source, target) in enumerate(((q_hbm, q_ref), (g_hbm, g_ref)))
    ]
    for copy in copies:
        copy.start()
    lon_odd = is_odd("lon")
    lat_odd = is_odd("lat")
    has_north = lax.axis_index("lat") > 0
    has_south = lax.axis_index("lat") < lax.axis_size("lat") - 1
    shape = (SPAN * SPAN, TABLE)
    entry = lax.broadcasted_iota(jnp.int32, shape, 0)
    offset = BASE - lax.broadcasted_iota(jnp.int32, shape, 1)
    chosen = (offset == (entry // SPAN) * COLS + entry % SPAN).astype(F32)
    lines = jnp.dot(bias_ref[...], chosen, preferred_element_type=F32, precision=lax.Precision.HIGHEST)
    offset = BASE - lax.broadcasted_iota(jnp.int32, (1, TABLE), 1)
    valid = (offset >= 0) & (offset < SPAN * COLS) & (offset % COLS < SPAN)
    line_ref[...] = jnp.where(valid, lines, MASKED)
    query_col = lax.broadcasted_iota(jnp.int32, (8, CELLS), 1) % COLS
    sub = lax.broadcasted_iota(jnp.int32, (8, CELLS), 0)

    def near(delta):
        return (delta >= 0) & (delta < SPAN)

    west, east = 0, COLS + RADIUS
    west_slot = jnp.where(lon_odd, SIDE, 0)
    east_slot = SIDE - west_slot
    north_slot = jnp.where(lat_odd, 0, 1)
    south_slot = 1 - north_slot

    def fill(head, carry):
        line = jnp.broadcast_to(line_ref[pl.ds(head, 1), :], (8, TABLE))
        by_one = pltpu.roll(line, 0, 1, stride=1, stride_axis=0)
        by_row = pltpu.roll(line, 0, 1, stride=COLS, stride_axis=0)

        def window(source, row, col):
            first = BASE - (COLS * row + col)
            return source[:, first : first + CELLS]

        def put(at, values, allowed, target):
            target[head, pl.ds(pl.multiple_of(at, 8), 8), :] = jnp.where(allowed, values, MASKED)

        def cells(at, row, row_count, there):
            for half in range(COLS // 8):
                allowed = near(RADIUS + 8 * half + sub - query_col)
                if there is not None:
                    allowed = allowed & there
                for step in range(row_count):
                    values = window(by_one, row + step, RADIUS + 8 * half)
                    put(at + step * COLS + 8 * half, values, allowed, table_ref)

        def sides(at, row, first_col, there, target):
            for step in range(RADIUS):
                allowed = near(first_col + step - query_col)
                if there is not None:
                    allowed = allowed & there
                put(at + step * ROWS, window(by_row, row, first_col + step), allowed, target)

        cells(OWN_AT, RADIUS, ROWS, None)
        sides(LON_AT + west_slot, RADIUS, west, None, table_ref)
        sides(LON_AT + east_slot, RADIUS, east, None, table_ref)
        for slot, row, there in ((north_slot, 0, has_north), (south_slot, ROWS + RADIUS, has_south)):
            cells(LAT_AT + slot * BAND, row, RADIUS, there)
            first = row if row else row - (ROWS - RADIUS)
            sides(slot * 2 * SIDE + west_slot, first, west, there, corner_ref)
            sides(slot * 2 * SIDE + east_slot, first, east, there, corner_ref)
        return carry

    lax.fori_loop(0, bias_ref.shape[0], fill, 0)
    for copy in copies:
        copy.wait()


LAST = (((1,), (1,)), ((), ()))
FACTOR = HEAD_DIM ** (-0.5)


def join_kernel(lon_odd_ref, lon_even_ref, out_ref):
    out_ref[:, :SIDE] = lon_odd_ref[...]
    out_ref[:, SIDE:] = lon_even_ref[...]


def over_pairs(width, body):
    for pair in range(width // PAIR):
        body(pair, pl.ds(pair * PAIR, PAIR))


def both_heads(block):
    first_head = lax.broadcasted_iota(jnp.int32, block.shape, 1) < HEAD_DIM
    zero = jnp.zeros_like(block)
    return jnp.concatenate([jnp.where(first_head, block, zero), jnp.where(first_head, zero, block)], axis=0)


def scaled(block):
    return both_heads(block * jnp.asarray(FACTOR, BF16))


def pair_scores(keys, values, queries, grads, table_ref, pair):
    scores = lax.dot_general(keys, queries, LAST, preferred_element_type=F32)
    scores = scores + jnp.concatenate([table_ref[2 * pair], table_ref[2 * pair + 1]], axis=1)
    grad_prob = lax.dot_general(values, grads, LAST, preferred_element_type=F32)
    return scores, grad_prob


def column_sum(x):
    return jnp.sum(x, axis=0, keepdims=True)


def score_gradient(probability, grad_prob, row_dot):
    return probability.astype(BF16), (probability * (grad_prob - row_dot)).astype(BF16)


def near_kernel(
    q_ref, g_ref, k_ref, v_ref, lon_odd_ref, lon_even_ref, lat_even_ref, lat_odd_ref, table_ref,
    raised_ref, prob_ref, stats_ref,
):
    parts = (lon_odd_ref, lon_even_ref, lat_even_ref, lat_odd_ref)

    def body(pair, at):
        keys = jnp.concatenate([k_ref[:, at]] + [part[0, :, at] for part in parts], axis=0)
        values = jnp.concatenate([v_ref[:, at]] + [part[1, :, at] for part in parts], axis=0)
        queries, grads = scaled(q_ref[:, at]), both_heads(g_ref[:, at])
        scores, grad_prob = pair_scores(keys, values, queries, grads, table_ref, pair)
        largest = jnp.max(scores, axis=0, keepdims=True)
        raised = jnp.exp(scores - largest)
        raised_ref[pair] = raised
        prob_ref[pair] = grad_prob
        stats_ref[pair, 0:1] = largest
        stats_ref[pair, 1:2] = column_sum(raised)
        stats_ref[pair, 2:3] = column_sum(raised * grad_prob)

    over_pairs(q_ref.shape[1], body)


def corner_kernel(
    q_ref, g_ref, corner_even_ref, corner_odd_ref, table_ref, near_stats_ref,
    first_even_ref, first_odd_ref, second_even_ref, second_odd_ref, weights_ref, dscore_ref, stats_ref,
):
    scored = []

    def score(pair, at):
        keys = jnp.concatenate([corner_even_ref[0, :, at], corner_odd_ref[0, :, at]], axis=0)
        values = jnp.concatenate([corner_even_ref[1, :, at], corner_odd_ref[1, :, at]], axis=0)
        queries, grads = scaled(q_ref[:, at]), both_heads(g_ref[:, at])
        scored.append((queries, grads, *pair_scores(keys, values, queries, grads, table_ref, pair)))

    over_pairs(q_ref.shape[1], score)

    def differentiate(pair, at):
        queries, grads, scores, grad_prob = scored[pair]
        near_largest = near_stats_ref[pair, 0:1]
        largest = jnp.maximum(near_largest, jnp.max(scores, axis=0, keepdims=True))
        raised = jnp.exp(scores - largest)
        shift = jnp.exp(near_largest - largest)
        total = near_stats_ref[pair, 1:2] * shift + column_sum(raised)
        inverse = 1.0 / total
        near_scale = shift * inverse
        row_dot = near_stats_ref[pair, 2:3] * near_scale + column_sum(raised * grad_prob) * inverse
        stats_ref[pair, 0:1] = near_scale
        stats_ref[pair, 1:2] = row_dot
        weights, dscore = score_gradient(raised * inverse, grad_prob, row_dot)
        weights_ref[pair] = weights
        dscore_ref[pair] = dscore
        for slot, coefficients, other in ((0, dscore, queries), (1, weights, grads)):
            grad = jnp.dot(coefficients, other, preferred_element_type=F32).astype(BF16)
            for index, out in enumerate((second_even_ref, first_even_ref, second_odd_ref, first_odd_ref)):
                out[slot, :, at] = grad[index * SIDE : (index + 1) * SIDE]

    over_pairs(q_ref.shape[1], differentiate)


def sides_kernel(
    q_ref, g_ref, raised_ref, prob_ref, stats_ref,
    dlon_ref, back_even_ref, back_odd_ref, weights_ref, dscore_ref,
):
    def body(pair, at):
        weights, dscore = score_gradient(
            raised_ref[pair, LON_AT:] * stats_ref[pair, 0:1], prob_ref[pair, LON_AT:], stats_ref[pair, 1:2]
        )
        weights_ref[pair] = weights
        dscore_ref[pair] = dscore
        for slot, coefficients, other in ((0, dscore, scaled(q_ref[:, at])), (1, weights, both_heads(g_ref[:, at]))):
            grad = jnp.dot(coefficients, other, preferred_element_type=F32)
            dlon_ref[slot, :, at] = grad[: 2 * SIDE]
            back_even_ref[slot, :, at] = grad[2 * SIDE : 2 * SIDE + BAND].astype(BF16)
            back_odd_ref[slot, :, at] = grad[2 * SIDE + BAND :].astype(BF16)

    over_pairs(q_ref.shape[1], body)


def own_kernel(
    q_ref, g_ref, k_ref, v_ref, lon_odd_ref, lon_even_ref, lat_even_ref, lat_odd_ref, corner_even_ref, corner_odd_ref,
    raised_ref, prob_ref, stats_ref, side_weights_ref, side_dscore_ref, corner_weights_ref, corner_dscore_ref,
    out_ref, dq_ref, own_ref,
):
    parts = (lon_odd_ref, lon_even_ref, lat_even_ref, lat_odd_ref, corner_even_ref, corner_odd_ref)

    def per_query(cells, coefficients):
        turned = jnp.dot(cells.T, coefficients, preferred_element_type=F32)
        mine = jnp.concatenate([turned[:HEAD_DIM, :CELLS], turned[HEAD_DIM:, CELLS:]], axis=0)
        return mine.T

    def body(pair, at):
        own_weights, own_dscore = score_gradient(
            raised_ref[pair, :LON_AT] * stats_ref[pair, 0:1], prob_ref[pair, :LON_AT], stats_ref[pair, 1:2]
        )
        own_ref[0, :, at] = jnp.dot(own_dscore, scaled(q_ref[:, at]), preferred_element_type=F32)
        own_ref[1, :, at] = jnp.dot(own_weights, both_heads(g_ref[:, at]), preferred_element_type=F32)
        keys = jnp.concatenate([k_ref[:, at]] + [part[0, :, at] for part in parts], axis=0)
        values = jnp.concatenate([v_ref[:, at]] + [part[1, :, at] for part in parts], axis=0)
        weights = jnp.concatenate([own_weights, side_weights_ref[pair], corner_weights_ref[pair]], axis=0)
        dscore = jnp.concatenate([own_dscore, side_dscore_ref[pair], corner_dscore_ref[pair]], axis=0)
        out_ref[:, at] = per_query(values, weights).astype(BF16)
        dq_ref[:, at] = (per_query(keys, dscore) * FACTOR).astype(BF16)

    over_pairs(q_ref.shape[1], body)


def middle_kernel(at, dlon_ref, back_even_ref, back_odd_ref, send_ref):
    total = dlon_ref[:, pl.ds(at, SIDE)] + back_even_ref[...].astype(F32) + back_odd_ref[...].astype(F32)
    send_ref[...] = total.astype(BF16)


def final_kernel(own_ref, back_even_ref, back_odd_ref, side_even_ref, side_odd_ref, dk_ref, dv_ref, sum_ref):
    lon_odd = is_odd("lon")
    start_even, start_odd = lat_starts()
    shape = (CELLS, SIDE)
    cell = lax.broadcasted_iota(jnp.int32, shape, 0)
    place = lax.broadcasted_iota(jnp.int32, shape, 1)

    def spread(first_col):
        return (cell == (place % ROWS) * COLS + first_col + place // ROWS).astype(BF16)

    spread_odd = spread(jnp.where(lon_odd, COLS - RADIUS, 0))
    spread_even = spread(jnp.where(lon_odd, 0, COLS - RADIUS))
    for slot, out in ((0, dk_ref), (1, dv_ref)):
        sum_ref[...] = (
            own_ref[slot]
            + jnp.dot(spread_odd, side_odd_ref[slot], preferred_element_type=F32)
            + jnp.dot(spread_even, side_even_ref[slot], preferred_element_type=F32)
        )
        sum_ref[pl.ds(start_even, BAND), :] += back_even_ref[slot].astype(F32)
        sum_ref[pl.ds(start_odd, BAND), :] += back_odd_ref[slot].astype(F32)
        out[...] = sum_ref[...].astype(BF16)


def arr(shape, dtype):
    return jax.ShapeDtypeStruct(shape, dtype)


def call(kernel, name, operands, results, flops=0, **more):
    moved = sum(x.size * x.dtype.itemsize for x in operands)
    return pl.pallas_call(
        kernel,
        out_shape=results,
        compiler_params=pltpu.CompilerParams(vmem_limit_bytes=32 * 1024 * 1024),
        cost_estimate=pl.CostEstimate(flops=flops, bytes_accessed=moved, transcendentals=0),
        name=name,
        **more,
    )(*operands)


def shards(queries, key_cells, value_cells, grad_output, rel_bias):
    block = queries.shape
    heads = rel_bias.shape[0]
    feat = block[-1]
    pairs = feat // PAIR
    cells = arr((CELLS, feat), BF16)
    side, band, corner = (arr((2, rows, feat), BF16) for rows in (SIDE, BAND, 2 * SIDE))
    work = 2 * CELLS * feat
    barrier = lax.optimization_barrier

    def in_hbm(x):
        return pltpu.with_memory_space_constraint(x, pltpu.HBM)

    hbm, vmem = (pl.BlockSpec(memory_space=space) for space in (pltpu.HBM, pltpu.VMEM))
    arguments = [in_hbm(x) for x in (key_cells.reshape(CELLS, feat), value_cells.reshape(CELLS, feat), rel_bias)]
    lon_odd, lon_even, k, v, rel_bias = call(
        pack_kernel, "pack", arguments, [side, side, cells, cells, arr(rel_bias.shape, F32)],
        in_specs=[hbm] * 3,
        scratch_shapes=[pltpu.SemaphoreType.DMA((3,))],
    )
    lon_odd = pair_exchange(lon_odd, "lon", 1, True)
    lon_even = pair_exchange(lon_even, "lon", 0, True)
    lat_even, lat_odd = call(rows_kernel, "rows", [k, v], [band, band])
    lat_even = pair_exchange(lat_even, "lat", 0, False)
    lat_odd = pair_exchange(lat_odd, "lat", 1, True)

    table, corner_table, q, g = call(
        bias_kernel, "bias_table",
        [rel_bias, in_hbm(queries.reshape(CELLS, feat)), in_hbm(grad_output.reshape(CELLS, feat))],
        [arr((heads, NEAR, CELLS), F32), arr((heads, CORNERS, CELLS), F32), cells, cells], heads * NEAR * CELLS,
        in_specs=[vmem, hbm, hbm],
        scratch_shapes=[pltpu.VMEM((heads, TABLE), F32), pltpu.SemaphoreType.DMA((2,))],
    )

    lon_odd, lon_even, table, corner_table = barrier((lon_odd, lon_even, table, corner_table))
    joined, = call(join_kernel, "join", [lon_odd, lon_even], [corner])
    corner_even = pair_exchange(joined, "lat", 0, False)
    corner_odd = odd_rows_exchange(joined)

    def scored(rows, dtype):
        return [arr((pairs, rows, 2 * CELLS), dtype)] * 2

    stats = arr((pairs, 8, 2 * CELLS), F32)
    near = [k, v, lon_odd, lon_even, lat_even, lat_odd]
    raised, prob, near_stats = call(
        near_kernel, "near", [q, g, *near, table], scored(NEAR, F32) + [stats], 4 * work * NEAR
    )
    first_even, first_odd, second_even, second_odd, corner_weights, corner_dscore, stats = call(
        corner_kernel, "corner", [q, g, corner_even, corner_odd, corner_table, near_stats],
        [side] * 4 + scored(CORNERS, BF16) + [stats], 4 * work * CORNERS,
    )
    first_even = pair_exchange(first_even, "lat", 0, False)
    first_odd = odd_rows_exchange(first_odd)
    second_even = pair_exchange(second_even, "lat", 0, False)
    second_odd = odd_rows_exchange(second_odd)
    dlon, back_even, back_odd, side_weights, side_dscore = call(
        sides_kernel, "sides", [q, g, raised, prob, stats],
        [arr(corner.shape, F32), band, band] + scored(NEAR - LON_AT, BF16), 4 * work * (NEAR - LON_AT),
    )
    back_even = pair_exchange(back_even, "lat", 0, False)
    back_odd = odd_rows_exchange(back_odd)

    def middle(at, *received):
        return call(functools.partial(middle_kernel, at), "middle", [dlon, *received], [side])[0]

    side_even = pair_exchange(middle(SIDE, first_even, first_odd), "lon", 0, True)
    side_odd = pair_exchange(middle(0, second_even, second_odd), "lon", 1, True)
    out, dq, own = call(
        own_kernel, "own",
        [q, g, *near, corner_even, corner_odd, raised, prob, stats, side_weights, side_dscore, corner_weights, corner_dscore],
        [cells, cells, arr((2, CELLS, feat), F32)], 4 * work * (NEAR + CORNERS),
    )
    dk, dv = call(
        final_kernel, "final", [own, back_even, back_odd, side_even, side_odd], [cells, cells],
        scratch_shapes=[pltpu.VMEM((CELLS, feat), F32)],
    )
    return tuple(x.reshape(block) for x in (out, dq, dk, dv))


def solution(mesh):
    spec = P("lat", "lon", None)
    return jax.shard_map(
        shards, mesh=mesh, in_specs=(spec, spec, spec, spec, P()), out_specs=(spec,) * 4, check_vma=False
    )
```

```python
import functools

import jax
import jax.numpy as jnp
from jax import lax
from jax.experimental import pallas as pl
from jax.experimental.pallas import tpu as pltpu
from jax.sharding import PartitionSpec as P

HEAD_DIM = 64
RADIUS = 6
SPAN = 2 * RADIUS + 1
ROWS = 8
COLS = 16
CELLS = ROWS * COLS
SIDE = ROWS * RADIUS
BAND = RADIUS * COLS
PAIR = 2 * HEAD_DIM
BASE = 336
TABLE = 512
MASKED = -1e30

OWN_AT = 0
LON_AT = CELLS
LAT_AT = LON_AT + 2 * SIDE
NEAR = LAT_AT + 2 * BAND
AROUND = NEAR + 4 * SIDE
LANES = 128

F32 = jnp.float32
BF16 = jnp.bfloat16


def pair_exchange(value, axis, odd, wrap):
    count = lax.axis_size(axis)
    pairs = []
    for first in range(odd, count, 2):
        second = first + 1
        if second >= count and not wrap:
            continue
        second %= count
        pairs += [(first, second), (second, first)]
    return lax.ppermute(value, axis, pairs)


def odd_rows_exchange(value):
    lats, lons = lax.axis_size("lat"), lax.axis_size("lon")
    pairs = []
    for lat in range(lats):
        for lon in range(lons):
            other = lat + 1 if lat % 2 else lat - 1
            inside = 0 <= other < lats
            target = (other, lon) if inside else (lat, lon ^ (1 if lons % 4 else 2))
            pairs.append((lat * lons + lon, target[0] * lons + target[1]))
    return lax.ppermute(value, ("lat", "lon"), pairs)


def is_odd(axis):
    return lax.axis_index(axis) % 2 == 1


def pick_matrix(first_col):
    shape = (SIDE, CELLS)
    place = lax.broadcasted_iota(jnp.int32, shape, 0)
    cell = lax.broadcasted_iota(jnp.int32, shape, 1)
    source = (place % ROWS) * COLS + first_col + place // ROWS
    return (cell == source).astype(BF16)


def pack_kernel(k_hbm, v_hbm, bias_hbm, lon_odd_ref, lon_even_ref, k_ref, v_ref, bias_ref, sems):
    copies = [
        pltpu.make_async_copy(source, target, sems.at[index])
        for index, (source, target) in enumerate(((k_hbm, k_ref), (v_hbm, v_ref), (bias_hbm, bias_ref)))
    ]
    for copy in copies:
        copy.start()
    lon_odd = is_odd("lon")
    first_cols = (jnp.where(lon_odd, COLS - RADIUS, 0), jnp.where(lon_odd, 0, COLS - RADIUS))
    picks = jnp.concatenate([pick_matrix(first_col) for first_col in first_cols], axis=0)
    for slot, source in ((0, k_ref), (1, v_ref)):
        copies[slot].wait()
        both = jnp.dot(picks, source[...], preferred_element_type=F32).astype(BF16)
        lon_odd_ref[slot] = both[:SIDE]
        lon_even_ref[slot] = both[SIDE:]
    copies[2].wait()


def lat_starts():
    lat_odd = is_odd("lat")
    even = jnp.where(lat_odd, 0, CELLS - BAND)
    return pl.multiple_of(even, 32), pl.multiple_of(CELLS - BAND - even, 32)


def rows_kernel(k_ref, v_ref, lat_even_ref, lat_odd_ref):
    for start, out in zip(lat_starts(), (lat_even_ref, lat_odd_ref)):
        out[0] = k_ref[pl.ds(start, BAND), :]
        out[1] = v_ref[pl.ds(start, BAND), :]


def bias_lines(bias_ref, line_ref):
    offset = BASE - lax.broadcasted_iota(jnp.int32, (1, TABLE), 1)
    row, col = offset // COLS, offset % COLS
    valid = (offset >= 0) & (row < SPAN) & (col < SPAN)
    entry = lax.broadcasted_iota(jnp.int32, (SPAN * SPAN, TABLE), 0)
    chosen = jnp.where(entry == jnp.where(valid, row * SPAN + col, -1), 1.0, 0.0).astype(BF16)
    rest = bias_ref[...]
    total = jnp.zeros((rest.shape[0], TABLE), F32)
    for _ in range(3):
        part = rest.astype(BF16)
        total = total + jnp.dot(part, chosen, preferred_element_type=F32)
        rest = rest - part.astype(F32)
    line_ref[...] = jnp.where(valid, total, MASKED)


def spread_rows(line_ref, spread_ref):
    heads = line_ref.shape[0]
    lines = [jnp.broadcast_to(line_ref[head : head + 1], (8, TABLE)) for head in range(heads)]
    x = jnp.concatenate(lines, axis=0)
    sub = lax.broadcasted_iota(jnp.int32, x.shape, 0)
    for index, stride in enumerate((1, COLS)):
        turned = x
        for bit in (1, 2, 4):
            turned = jnp.where((sub & bit) != 0, pltpu.roll(turned, bit * stride, 1), turned)
        for head in range(heads):
            spread_ref[index, head] = turned[8 * head : 8 * head + 8]


def windows(source, col, rows):
    firsts = [BASE - (COLS * row + col) for row in rows]
    turn = firsts[0] % LANES
    turned = pltpu.roll(source, TABLE - turn, 1) if turn else source
    return [turned[:, first - turn : first - turn + CELLS] for first in firsts]


def near(delta, there=None):
    allowed = (delta >= 0) & (delta < SPAN)
    return allowed if there is None else allowed & there


def places():
    west_slot = jnp.where(is_odd("lon"), SIDE, 0)
    north_slot = jnp.where(is_odd("lat"), 0, 1)
    has_north = lax.axis_index("lat") > 0
    has_south = lax.axis_index("lat") < lax.axis_size("lat") - 1
    sides = ((0, west_slot), (COLS + RADIUS, SIDE - west_slot))
    own_col = lax.broadcasted_iota(jnp.int32, (8, CELLS), 1) % COLS
    sub = lax.broadcasted_iota(jnp.int32, (8, CELLS), 0)
    return sides, north_slot, 1 - north_slot, has_north, has_south, own_col, sub


def bias_kernel(bias_ref, q_hbm, g_hbm, table_ref, q_ref, g_ref, line_ref, spread_ref, sems):
    copies = [
        pltpu.make_async_copy(source, target, sems.at[index])
        for index, (source, target) in enumerate(((q_hbm, q_ref), (g_hbm, g_ref)))
    ]
    for copy in copies:
        copy.start()
    bias_lines(bias_ref, line_ref)
    spread_rows(line_ref, spread_ref)
    sides, north_slot, south_slot, has_north, has_south, own_col, sub = places()

    def fill(head, carry):
        def put(at, values, allowed):
            table_ref[head, pl.ds(pl.multiple_of(at, 8), 8), :] = jnp.where(allowed, values, MASKED)

        by_one = spread_ref[0, head]
        for half in range(COLS // 8):
            delta = RADIUS + 8 * half + sub - own_col
            own, north, south = near(delta), near(delta, has_north), near(delta, has_south)
            for step in range(8):
                rows = [row for row in (step, step + 8, step + 16) if row < 2 * RADIUS + ROWS]
                for row, values in zip(rows, windows(by_one, RADIUS + 8 * half, rows)):
                    if row < RADIUS:
                        put(LAT_AT + north_slot * BAND + row * COLS + 8 * half, values, north)
                    elif row < RADIUS + ROWS:
                        put(OWN_AT + (row - RADIUS) * COLS + 8 * half, values, own)
                    else:
                        put(LAT_AT + south_slot * BAND + (row - RADIUS - ROWS) * COLS + 8 * half, values, south)
        by_row = spread_ref[1, head]
        rows = (RADIUS - ROWS, RADIUS, RADIUS + ROWS)
        for first_col, lon_slot in sides:
            for step in range(RADIUS):
                delta = first_col + step - own_col
                above, beside, below = windows(by_row, first_col + step, rows)
                at = lon_slot + step * ROWS
                put(LON_AT + at, beside, near(delta))
                put(NEAR + north_slot * 2 * SIDE + at, above, near(delta, has_north))
                put(NEAR + south_slot * 2 * SIDE + at, below, near(delta, has_south))
        return carry

    lax.fori_loop(0, bias_ref.shape[0], fill, 0, unroll=8)
    for copy in copies:
        copy.wait()


def band_bias_kernel(bias_ref, after_ref, table_ref, line_ref, spread_ref):
    del after_ref
    bias_lines(bias_ref, line_ref)
    spread_rows(line_ref, spread_ref)
    sides, north_slot, south_slot, has_north, has_south, own_col, sub = places()
    lane = lax.broadcasted_iota(jnp.int32, (8, CELLS), 1)
    bands = ((north_slot, RADIUS, has_north & (lane < BAND)), (south_slot, -ROWS, has_south & (lane < BAND)))

    def fill(head, carry):
        def put(slot, at, values, allowed):
            table_ref[slot, head, pl.ds(pl.multiple_of(at, 8), 8), :] = jnp.where(allowed, values, MASKED)

        by_one = spread_ref[0, head]
        for half in range(COLS // 8):
            delta = RADIUS + 8 * half + sub - own_col
            masks = [near(delta, there) for _, _, there in bands]
            for step in range(ROWS):
                rows = [next(row for row in range(ROWS) if (RADIUS + row + shift - step) % 8 == 0) for _, shift, _ in bands]
                found = windows(by_one, RADIUS + 8 * half, [RADIUS + row + band[1] for row, band in zip(rows, bands)])
                for row, band, mask, values in zip(rows, bands, masks, found):
                    put(band[0], OWN_AT + row * COLS + 8 * half, values, mask)
        by_row = spread_ref[1, head]
        for slot, shift, there in bands:
            for first_col, lon_slot in sides:
                for step in range(RADIUS):
                    (values,) = windows(by_row, first_col + step, (RADIUS + shift,))
                    put(slot, LON_AT + lon_slot + step * ROWS, values, near(first_col + step - own_col, there))
        return carry

    lax.fori_loop(0, bias_ref.shape[0], fill, 0, unroll=8)


LAST = (((1,), (1,)), ((), ()))
FACTOR = HEAD_DIM ** (-0.5)


def join_kernel(lon_odd_ref, lon_even_ref, out_ref):
    out_ref[:, :SIDE] = lon_odd_ref[...]
    out_ref[:, SIDE:] = lon_even_ref[...]


def over_pairs(width, body):
    return [body(pair, pl.ds(pair * PAIR, PAIR)) for pair in range(width // PAIR)]


def stacked(slot, at, own_ref, *refs):
    return jnp.concatenate([own_ref[:, at]] + [ref[slot, :, at] for ref in refs], axis=0)


def both_heads(block):
    first_head = lax.broadcasted_iota(jnp.int32, block.shape, 1) < HEAD_DIM
    zero = jnp.zeros_like(block)
    return jnp.concatenate([jnp.where(first_head, block, zero), jnp.where(first_head, zero, block)], axis=0)


def scaled(block):
    return both_heads(block * jnp.asarray(FACTOR, BF16))


def two_tables(table_ref, pair, rows):
    return jnp.concatenate([table_ref[2 * pair, rows], table_ref[2 * pair + 1, rows]], axis=1)


def times(left, right):
    return lax.dot_general(left, right, LAST, preferred_element_type=F32)


def column_sum(x):
    return jnp.sum(x, axis=0, keepdims=True)


def score_gradient(probability, grad_prob, row_dot):
    return probability.astype(BF16), (probability * (grad_prob - row_dot)).astype(BF16)


def near_kernel(
    q_ref, g_ref, k_ref, v_ref, lon_odd_ref, lon_even_ref, lat_even_ref, lat_odd_ref, table_ref,
    raised_ref, prob_ref, stats_ref,
):
    parts = (lon_odd_ref, lon_even_ref, lat_even_ref, lat_odd_ref)

    def body(pair, at):
        scores = times(stacked(0, at, k_ref, *parts), scaled(q_ref[:, at])) + two_tables(table_ref, pair, pl.ds(0, NEAR))
        grad_prob = times(stacked(1, at, v_ref, *parts), both_heads(g_ref[:, at]))
        largest = jnp.max(scores, axis=0, keepdims=True)
        raised = jnp.exp(scores - largest)
        raised_ref[pair] = raised
        prob_ref[pair] = grad_prob
        stats_ref[pair, 0:1] = largest
        stats_ref[pair, 1:2] = column_sum(raised)
        stats_ref[pair, 2:3] = column_sum(raised * grad_prob)

    over_pairs(q_ref.shape[1], body)


def corner_kernel(
    q_ref, g_ref, corner_even_ref, corner_odd_ref, table_ref, near_stats_ref,
    raised_ref, prob_ref, stats_ref, send_even_ref, send_odd_ref, lines_ref,
):
    def score(pair, at):
        keys, values = (
            jnp.concatenate([corner_even_ref[slot, :, at], corner_odd_ref[slot, :, at]], axis=0) for slot in (0, 1)
        )
        scores = times(keys, scaled(q_ref[:, at])) + two_tables(table_ref, pair, pl.ds(NEAR, AROUND - NEAR))
        return scores, times(values, both_heads(g_ref[:, at]))

    scored = over_pairs(q_ref.shape[1], score)
    for pair, (scores, grad_prob) in enumerate(scored):
        near_largest = near_stats_ref[pair, 0:1]
        largest = jnp.maximum(near_largest, jnp.max(scores, axis=0, keepdims=True))
        raised = jnp.exp(scores - largest)
        shift = jnp.exp(near_largest - largest)
        total = near_stats_ref[pair, 1:2] * shift + column_sum(raised)
        inverse = 1.0 / total
        near_scale = shift * inverse
        row_dot = near_stats_ref[pair, 2:3] * near_scale + column_sum(raised * grad_prob) * inverse
        raised_ref[pair] = raised
        prob_ref[pair] = grad_prob
        stats_ref[pair, 0:1] = near_scale
        stats_ref[pair, 1:2] = row_dot
        stats_ref[pair, 2:3] = inverse
        for index, line in enumerate((largest + jnp.log(total), row_dot)):
            for head in (0, 1):
                at = 4 * pair + 2 * index + head
                lines_ref[at : at + 1] = line[:, head * CELLS : (head + 1) * CELLS]
    lines = lines_ref[...]
    low_rows = pltpu.roll(lines, BAND, 1)
    lat_odd = is_odd("lat")
    send_even_ref[...] = jnp.where(lat_odd, lines, low_rows)
    send_odd_ref[...] = jnp.where(lat_odd, low_rows, lines)


def near_gradient(raised_ref, prob_ref, stats_ref, pair, rows):
    return score_gradient(raised_ref[pair, rows] * stats_ref[pair, 0:1], prob_ref[pair, rows], stats_ref[pair, 1:2])


def band_lines(lines_refs, pair):
    def row(first):
        return jnp.concatenate([ref[line : line + 1] for ref in lines_refs for line in (first, first + 1)], axis=1)

    return row(4 * pair), row(4 * pair + 2)


def band_queries(queries_refs, slot, at, prepare):
    empty = jnp.zeros((CELLS - BAND, PAIR), BF16)
    return jnp.concatenate([prepare(jnp.concatenate([ref[slot, :, at], empty], axis=0)) for ref in queries_refs], axis=0)


def band_tables(table_ref, pair, rows):
    return jnp.concatenate([table_ref[slot, 2 * pair + head, rows] for slot in (0, 1) for head in (0, 1)], axis=1)


def side_scores_kernel(
    q_ref, g_ref, raised_ref, prob_ref, stats_ref, lon_odd_ref, lon_even_ref, queries_even_ref, queries_odd_ref, table_ref,
    dlon_ref, scores_ref, prob_out_ref, band_q_ref, band_g_ref,
):
    queries_refs = (queries_even_ref, queries_odd_ref)

    def body(pair, at):
        keys, values = (
            jnp.concatenate([lon_odd_ref[slot, :, at], lon_even_ref[slot, :, at]], axis=0) for slot in (0, 1)
        )
        queries = band_queries(queries_refs, 0, at, scaled)
        grads = band_queries(queries_refs, 1, at, both_heads)
        band_q_ref[pair] = queries
        band_g_ref[pair] = grads
        scores_ref[pair] = times(keys, queries) + band_tables(table_ref, pair, pl.ds(LON_AT, 2 * SIDE))
        prob_out_ref[pair] = times(values, grads)
        weights, dscore = near_gradient(raised_ref, prob_ref, stats_ref, pair, pl.ds(LON_AT, LAT_AT - LON_AT))
        dlon_ref[0, :, at] = jnp.dot(dscore, scaled(q_ref[:, at]), preferred_element_type=F32)
        dlon_ref[1, :, at] = jnp.dot(weights, both_heads(g_ref[:, at]), preferred_element_type=F32)

    over_pairs(q_ref.shape[1], body)


def side_band_kernel(
    dlon_ref, scores_ref, prob_ref, band_q_ref, band_g_ref, lines_even_ref, lines_odd_ref, send_odd_ref, send_even_ref
):
    lines_refs = (lines_even_ref, lines_odd_ref)

    def score(pair, at):
        log_total, row_dot = band_lines(lines_refs, pair)
        return score_gradient(jnp.exp(scores_ref[pair] - log_total), prob_ref[pair], row_dot)

    width = dlon_ref.shape[2]
    scored = over_pairs(width, score)

    def finish(pair, at):
        weights, dscore = scored[pair]
        for slot, coefficients, other in ((0, dscore, band_q_ref), (1, weights, band_g_ref)):
            total = dlon_ref[slot, :, at] + jnp.dot(coefficients, other[pair], preferred_element_type=F32)
            send_odd_ref[slot, :, at] = total[:SIDE].astype(BF16)
            send_even_ref[slot, :, at] = total[SIDE:].astype(BF16)

    over_pairs(width, finish)


def own_kernel(
    q_ref, g_ref, k_ref, v_ref, lon_odd_ref, lon_even_ref, lat_even_ref, lat_odd_ref, corner_even_ref, corner_odd_ref,
    raised_ref, prob_ref, corner_raised_ref, corner_prob_ref, stats_ref, out_ref, dq_ref, own_ref,
):
    parts = (lon_odd_ref, lon_even_ref, lat_even_ref, lat_odd_ref, corner_even_ref, corner_odd_ref)

    def per_query(cells, coefficients):
        turned = jnp.dot(cells.T, coefficients, preferred_element_type=F32)
        mine = jnp.concatenate([turned[:HEAD_DIM, :CELLS], turned[HEAD_DIM:, CELLS:]], axis=0)
        return mine.T

    def body(pair, at):
        nearby = near_gradient(raised_ref, prob_ref, stats_ref, pair, pl.ds(0, NEAR))
        far = score_gradient(
            corner_raised_ref[pair] * stats_ref[pair, 2:3], corner_prob_ref[pair], stats_ref[pair, 1:2]
        )
        weights, dscore = (jnp.concatenate(x, axis=0) for x in zip(nearby, far))
        own_ref[0, :, at] = jnp.dot(dscore[:LON_AT], scaled(q_ref[:, at]), preferred_element_type=F32)
        own_ref[1, :, at] = jnp.dot(weights[:LON_AT], both_heads(g_ref[:, at]), preferred_element_type=F32)
        out_ref[:, at] = per_query(stacked(1, at, v_ref, *parts), weights).astype(BF16)
        dq_ref[:, at] = (per_query(stacked(0, at, k_ref, *parts), dscore) * FACTOR).astype(BF16)

    over_pairs(q_ref.shape[1], body)


def own_band_kernel(
    k_ref, v_ref, band_q_ref, band_g_ref, table_ref, lines_even_ref, lines_odd_ref, own_ref, total_ref
):
    def score(pair, at):
        log_total, row_dot = band_lines((lines_even_ref, lines_odd_ref), pair)
        scores = times(k_ref[:, at], band_q_ref[pair]) + band_tables(table_ref, pair, pl.ds(OWN_AT, CELLS))
        return score_gradient(jnp.exp(scores - log_total), times(v_ref[:, at], band_g_ref[pair]), row_dot)

    scored = over_pairs(k_ref.shape[1], score)

    def finish(pair, at):
        weights, dscore = scored[pair]
        for slot, coefficients, other in ((0, dscore, band_q_ref), (1, weights, band_g_ref)):
            grad = jnp.dot(coefficients, other[pair], preferred_element_type=F32)
            total_ref[slot, :, at] = own_ref[slot, :, at] + grad

    over_pairs(k_ref.shape[1], finish)


def final_kernel(total_ref, side_even_ref, side_odd_ref, dk_ref, dv_ref):
    lon_odd = is_odd("lon")
    shape = (CELLS, SIDE)
    cell = lax.broadcasted_iota(jnp.int32, shape, 0)
    place = lax.broadcasted_iota(jnp.int32, shape, 1)

    def spread(first_col):
        return (cell == (place % ROWS) * COLS + first_col + place // ROWS).astype(BF16)

    spread_odd = spread(jnp.where(lon_odd, COLS - RADIUS, 0))
    spread_even = spread(jnp.where(lon_odd, 0, COLS - RADIUS))
    for slot, out in ((0, dk_ref), (1, dv_ref)):
        total = (
            total_ref[slot]
            + jnp.dot(spread_odd, side_odd_ref[slot], preferred_element_type=F32)
            + jnp.dot(spread_even, side_even_ref[slot], preferred_element_type=F32)
        )
        out[...] = total.astype(BF16)


def arr(shape, dtype):
    return jax.ShapeDtypeStruct(shape, dtype)


def call(kernel, name, operands, results, flops=0, **more):
    moved = sum(x.size * x.dtype.itemsize for x in operands)
    return pl.pallas_call(
        kernel,
        out_shape=results,
        compiler_params=pltpu.CompilerParams(vmem_limit_bytes=32 * 1024 * 1024),
        cost_estimate=pl.CostEstimate(flops=flops, bytes_accessed=moved, transcendentals=0),
        name=name,
        **more,
    )(*operands)


def shards(queries, key_cells, value_cells, grad_output, rel_bias):
    block = queries.shape
    heads = rel_bias.shape[0]
    feat = block[-1]
    pairs = feat // PAIR
    cells = arr((CELLS, feat), BF16)
    side, band, corner = (arr((2, rows, feat), BF16) for rows in (SIDE, BAND, 2 * SIDE))
    work = 2 * CELLS * feat
    barrier = lax.optimization_barrier

    def in_hbm(x):
        return pltpu.with_memory_space_constraint(x, pltpu.HBM)

    hbm, vmem = (pl.BlockSpec(memory_space=space) for space in (pltpu.HBM, pltpu.VMEM))
    arguments = [in_hbm(x) for x in (key_cells.reshape(CELLS, feat), value_cells.reshape(CELLS, feat), rel_bias)]
    lon_odd, lon_even, k, v, rel_bias = call(
        pack_kernel, "pack", arguments, [side, side, cells, cells, arr(rel_bias.shape, F32)],
        in_specs=[hbm] * 3,
        scratch_shapes=[pltpu.SemaphoreType.DMA((3,))],
    )
    lon_odd = pair_exchange(lon_odd, "lon", 1, True)
    lon_even = pair_exchange(lon_even, "lon", 0, True)
    lat_even, lat_odd = call(rows_kernel, "rows", [k, v], [band, band])
    lat_even = pair_exchange(lat_even, "lat", 0, False)
    lat_odd = pair_exchange(lat_odd, "lat", 1, True)

    spread = [pltpu.VMEM((heads, TABLE), F32), pltpu.VMEM((2, heads, 8, TABLE), F32)]
    table, q, g = call(
        bias_kernel, "bias_table",
        [rel_bias, in_hbm(queries.reshape(CELLS, feat)), in_hbm(grad_output.reshape(CELLS, feat))],
        [arr((heads, AROUND, CELLS), F32), cells, cells], heads * AROUND * CELLS,
        in_specs=[vmem, hbm, hbm],
        scratch_shapes=[*spread, pltpu.SemaphoreType.DMA((2,))],
    )

    lon_odd, lon_even, table = barrier((lon_odd, lon_even, table))
    joined, = call(join_kernel, "join", [lon_odd, lon_even], [corner], int(2e9))
    corner_even = pair_exchange(joined, "lat", 0, False)
    corner_odd = odd_rows_exchange(joined)

    def scored(rows):
        return [arr((pairs, rows, 2 * CELLS), F32)] * 2 + [arr((pairs, 8, 2 * CELLS), F32)]

    near = [k, v, lon_odd, lon_even, lat_even, lat_odd]
    raised, prob, near_stats = call(near_kernel, "near", [q, g, *near, table], scored(NEAR), 4 * work * NEAR)
    late_q, late_g, _ = barrier((q, g, joined))
    queries_even, queries_odd = call(rows_kernel, "query_rows", [late_q, late_g], [band, band])
    queries_even = pair_exchange(queries_even, "lat", 0, False)
    queries_odd = odd_rows_exchange(queries_odd)
    lines = arr((4 * pairs, LANES), F32)
    corner_raised, corner_prob, stats, lines_even, lines_odd = call(
        corner_kernel, "corner", [q, g, corner_even, corner_odd, table, near_stats],
        scored(AROUND - NEAR) + [lines, lines], 4 * work * (AROUND - NEAR),
        scratch_shapes=[pltpu.VMEM(lines.shape, F32)],
    )
    lines_even = pair_exchange(lines_even, "lat", 0, False)
    lines_odd = odd_rows_exchange(lines_odd)
    band_table, = call(
        band_bias_kernel, "band_table", [rel_bias, stats], [arr((2, heads, LAT_AT, CELLS), F32)],
        2 * heads * LAT_AT * CELLS,
        scratch_shapes=spread,
    )
    band_scores = [arr((pairs, 2 * SIDE, 4 * CELLS), F32)] * 2
    masked = [arr((pairs, 4 * CELLS, PAIR), BF16)] * 2
    dlon, side_scores, side_prob, band_q, band_g = call(
        side_scores_kernel, "side_scores",
        [q, g, raised, prob, stats, lon_odd, lon_even, queries_even, queries_odd, band_table],
        [arr(corner.shape, F32), *band_scores, *masked], 16 * work * SIDE,
    )
    lines_odd, dlon = barrier((lines_odd, dlon))
    send_odd, send_even = call(
        side_band_kernel, "side_band", [dlon, side_scores, side_prob, band_q, band_g, lines_even, lines_odd], [side, side],
        16 * work * SIDE,
    )
    side_even = pair_exchange(send_even, "lon", 0, True)
    side_odd = pair_exchange(send_odd, "lon", 1, True)
    out, dq, own = call(
        own_kernel, "own", [q, g, *near, corner_even, corner_odd, raised, prob, corner_raised, corner_prob, stats],
        [cells, cells, arr((2, CELLS, feat), F32)], 4 * work * AROUND,
    )
    total, = call(
        own_band_kernel, "own_band", [k, v, band_q, band_g, band_table, lines_even, lines_odd, own],
        [arr((2, CELLS, feat), F32)], 8 * work * CELLS,
    )
    dk, dv = call(final_kernel, "final", [total, side_even, side_odd], [cells, cells])
    return tuple(x.reshape(block) for x in (out, dq, dk, dv))


def solution(mesh):
    spec = P("lat", "lon", None)
    return jax.shard_map(
        shards, mesh=mesh, in_specs=(spec, spec, spec, spec, P()), out_specs=(spec,) * 4, check_vma=False
    )
```

```python
import functools

import jax
import jax.numpy as jnp
from jax import lax
from jax.experimental import pallas as pl
from jax.experimental.pallas import tpu as pltpu
from jax.sharding import PartitionSpec as P

HEAD_DIM = 64
RADIUS = 6
SPAN = 2 * RADIUS + 1
ROWS = 8
COLS = 16
CELLS = ROWS * COLS
SIDE = ROWS * RADIUS
BAND = RADIUS * COLS
PAIR = 2 * HEAD_DIM
BASE = 336
TABLE = 512
MASKED = -1e30

OWN_AT = 0
LON_AT = CELLS
LAT_AT = LON_AT + 2 * SIDE
NEAR = LAT_AT + 2 * BAND
AROUND = NEAR + 4 * SIDE
LANES = 128

F32 = jnp.float32
BF16 = jnp.bfloat16


def pair_exchange(value, axis, odd, wrap):
    count = lax.axis_size(axis)
    pairs = []
    for first in range(odd, count, 2):
        second = first + 1
        if second >= count and not wrap:
            continue
        second %= count
        pairs += [(first, second), (second, first)]
    return lax.ppermute(value, axis, pairs)


def odd_rows_exchange(value):
    lats, lons = lax.axis_size("lat"), lax.axis_size("lon")
    pairs = []
    for lat in range(lats):
        for lon in range(lons):
            other = lat + 1 if lat % 2 else lat - 1
            inside = 0 <= other < lats
            target = (other, lon) if inside else (lat, lon ^ (1 if lons % 4 else 2))
            pairs.append((lat * lons + lon, target[0] * lons + target[1]))
    return lax.ppermute(value, ("lat", "lon"), pairs)


def is_odd(axis):
    return lax.axis_index(axis) % 2 == 1


def pick_matrix(first_col):
    shape = (SIDE, CELLS)
    place = lax.broadcasted_iota(jnp.int32, shape, 0)
    cell = lax.broadcasted_iota(jnp.int32, shape, 1)
    source = (place % ROWS) * COLS + first_col + place // ROWS
    return (cell == source).astype(BF16)


def pack_kernel(k_hbm, v_hbm, bias_hbm, lon_odd_ref, lon_even_ref, k_ref, v_ref, bias_ref, sems):
    copies = [
        pltpu.make_async_copy(source, target, sems.at[index])
        for index, (source, target) in enumerate(((k_hbm, k_ref), (v_hbm, v_ref), (bias_hbm, bias_ref)))
    ]
    for copy in copies:
        copy.start()
    lon_odd = is_odd("lon")
    first_cols = (jnp.where(lon_odd, COLS - RADIUS, 0), jnp.where(lon_odd, 0, COLS - RADIUS))
    picks = jnp.concatenate([pick_matrix(first_col) for first_col in first_cols], axis=0)
    for slot, source in ((0, k_ref), (1, v_ref)):
        copies[slot].wait()
        both = jnp.dot(picks, source[...], preferred_element_type=F32).astype(BF16)
        lon_odd_ref[slot] = both[:SIDE]
        lon_even_ref[slot] = both[SIDE:]
    copies[2].wait()


def lat_starts():
    lat_odd = is_odd("lat")
    even = jnp.where(lat_odd, 0, CELLS - BAND)
    return pl.multiple_of(even, 32), pl.multiple_of(CELLS - BAND - even, 32)


def rows_kernel(k_ref, v_ref, lat_even_ref, lat_odd_ref):
    for start, out in zip(lat_starts(), (lat_even_ref, lat_odd_ref)):
        out[0] = k_ref[pl.ds(start, BAND), :]
        out[1] = v_ref[pl.ds(start, BAND), :]


def bias_lines(bias_ref, line_ref):
    offset = BASE - lax.broadcasted_iota(jnp.int32, (1, TABLE), 1)
    row, col = offset // COLS, offset % COLS
    valid = (offset >= 0) & (row < SPAN) & (col < SPAN)
    entry = lax.broadcasted_iota(jnp.int32, (SPAN * SPAN, TABLE), 0)
    chosen = jnp.where(entry == jnp.where(valid, row * SPAN + col, -1), 1.0, 0.0).astype(BF16)
    rest = bias_ref[...]
    total = jnp.zeros((rest.shape[0], TABLE), F32)
    for _ in range(3):
        part = rest.astype(BF16)
        total = total + jnp.dot(part, chosen, preferred_element_type=F32)
        rest = rest - part.astype(F32)
    line_ref[...] = jnp.where(valid, total, MASKED)


def spread_rows(line_ref, spread_ref):
    heads = line_ref.shape[0]
    lines = [jnp.broadcast_to(line_ref[head : head + 1], (8, TABLE)) for head in range(heads)]
    x = jnp.concatenate(lines, axis=0)
    sub = lax.broadcasted_iota(jnp.int32, x.shape, 0)
    for index, stride in enumerate((1, COLS)):
        turned = x
        for bit in (1, 2, 4):
            turned = jnp.where((sub & bit) != 0, pltpu.roll(turned, bit * stride, 1), turned)
        for head in range(heads):
            spread_ref[index, head] = turned[8 * head : 8 * head + 8]


def windows(source, col, rows):
    firsts = [BASE - (COLS * row + col) for row in rows]
    turn = firsts[0] % LANES
    turned = pltpu.roll(source, TABLE - turn, 1) if turn else source
    return [turned[:, first - turn : first - turn + CELLS] for first in firsts]


def near(delta, there=None):
    allowed = (delta >= 0) & (delta < SPAN)
    return allowed if there is None else allowed & there


def places():
    west_slot = jnp.where(is_odd("lon"), SIDE, 0)
    north_slot = jnp.where(is_odd("lat"), 0, 1)
    has_north = lax.axis_index("lat") > 0
    has_south = lax.axis_index("lat") < lax.axis_size("lat") - 1
    sides = ((0, west_slot), (COLS + RADIUS, SIDE - west_slot))
    own_col = lax.broadcasted_iota(jnp.int32, (8, CELLS), 1) % COLS
    sub = lax.broadcasted_iota(jnp.int32, (8, CELLS), 0)
    return sides, north_slot, 1 - north_slot, has_north, has_south, own_col, sub


def bias_kernel(bias_ref, q_hbm, g_hbm, table_ref, q_ref, g_ref, line_ref, spread_ref, sems):
    copies = [
        pltpu.make_async_copy(source, target, sems.at[index])
        for index, (source, target) in enumerate(((q_hbm, q_ref), (g_hbm, g_ref)))
    ]
    for copy in copies:
        copy.start()
    bias_lines(bias_ref, line_ref)
    spread_rows(line_ref, spread_ref)
    sides, north_slot, south_slot, has_north, has_south, own_col, sub = places()

    def fill(head, carry):
        def put(at, values, allowed):
            table_ref[head, pl.ds(pl.multiple_of(at, 8), 8), :] = jnp.where(allowed, values, MASKED)

        by_one = spread_ref[0, head]
        for half in range(COLS // 8):
            delta = RADIUS + 8 * half + sub - own_col
            own, north, south = near(delta), near(delta, has_north), near(delta, has_south)
            for step in range(8):
                rows = [row for row in (step, step + 8, step + 16) if row < 2 * RADIUS + ROWS]
                for row, values in zip(rows, windows(by_one, RADIUS + 8 * half, rows)):
                    if row < RADIUS:
                        put(LAT_AT + north_slot * BAND + row * COLS + 8 * half, values, north)
                    elif row < RADIUS + ROWS:
                        put(OWN_AT + (row - RADIUS) * COLS + 8 * half, values, own)
                    else:
                        put(LAT_AT + south_slot * BAND + (row - RADIUS - ROWS) * COLS + 8 * half, values, south)
        by_row = spread_ref[1, head]
        rows = (RADIUS - ROWS, RADIUS, RADIUS + ROWS)
        for first_col, lon_slot in sides:
            for step in range(RADIUS):
                delta = first_col + step - own_col
                above, beside, below = windows(by_row, first_col + step, rows)
                at = lon_slot + step * ROWS
                put(LON_AT + at, beside, near(delta))
                put(NEAR + north_slot * 2 * SIDE + at, above, near(delta, has_north))
                put(NEAR + south_slot * 2 * SIDE + at, below, near(delta, has_south))
        return carry

    lax.fori_loop(0, bias_ref.shape[0], fill, 0, unroll=8)
    for copy in copies:
        copy.wait()


def band_bias_kernel(bias_ref, after_ref, table_ref, line_ref, spread_ref):
    del after_ref
    bias_lines(bias_ref, line_ref)
    spread_rows(line_ref, spread_ref)
    sides, north_slot, south_slot, has_north, has_south, own_col, sub = places()
    lane = lax.broadcasted_iota(jnp.int32, (8, CELLS), 1)
    bands = ((north_slot, RADIUS, has_north & (lane < BAND)), (south_slot, -ROWS, has_south & (lane < BAND)))

    def fill(head, carry):
        def put(slot, at, values, allowed):
            table_ref[slot, head, pl.ds(pl.multiple_of(at, 8), 8), :] = jnp.where(allowed, values, MASKED)

        by_one = spread_ref[0, head]
        for half in range(COLS // 8):
            delta = RADIUS + 8 * half + sub - own_col
            masks = [near(delta, there) for _, _, there in bands]
            for step in range(ROWS):
                rows = [next(row for row in range(ROWS) if (RADIUS + row + shift - step) % 8 == 0) for _, shift, _ in bands]
                found = windows(by_one, RADIUS + 8 * half, [RADIUS + row + band[1] for row, band in zip(rows, bands)])
                for row, band, mask, values in zip(rows, bands, masks, found):
                    put(band[0], OWN_AT + row * COLS + 8 * half, values, mask)
        by_row = spread_ref[1, head]
        for slot, shift, there in bands:
            for first_col, lon_slot in sides:
                for step in range(RADIUS):
                    (values,) = windows(by_row, first_col + step, (RADIUS + shift,))
                    put(slot, LON_AT + lon_slot + step * ROWS, values, near(first_col + step - own_col, there))
        return carry

    lax.fori_loop(0, bias_ref.shape[0], fill, 0, unroll=8)


LAST = (((1,), (1,)), ((), ()))
FACTOR = HEAD_DIM ** (-0.5)


def join_kernel(lon_odd_ref, lon_even_ref, out_ref):
    out_ref[:, :SIDE] = lon_odd_ref[...]
    out_ref[:, SIDE:] = lon_even_ref[...]


def over_pairs(width, body):
    return [body(pair, pl.ds(pair * PAIR, PAIR)) for pair in range(width // PAIR)]


def stacked(slot, at, own_ref, *refs):
    return jnp.concatenate([own_ref[:, at]] + [ref[slot, :, at] for ref in refs], axis=0)


def both_heads(block):
    first_head = lax.broadcasted_iota(jnp.int32, block.shape, 1) < HEAD_DIM
    zero = jnp.zeros_like(block)
    return jnp.concatenate([jnp.where(first_head, block, zero), jnp.where(first_head, zero, block)], axis=0)


def scaled(block):
    return both_heads(block * jnp.asarray(FACTOR, BF16))


def two_tables(table_ref, pair, rows):
    return jnp.concatenate([table_ref[2 * pair, rows], table_ref[2 * pair + 1, rows]], axis=1)


def times(left, right):
    return lax.dot_general(left, right, LAST, preferred_element_type=F32)


def column_sum(x):
    return jnp.sum(x, axis=0, keepdims=True)


def score_gradient(probability, grad_prob, row_dot):
    return probability.astype(BF16), (probability * (grad_prob - row_dot)).astype(BF16)


def near_kernel(
    q_ref, g_ref, k_ref, v_ref, lon_odd_ref, lon_even_ref, lat_even_ref, lat_odd_ref, table_ref,
    raised_ref, prob_ref, stats_ref,
):
    parts = (lon_odd_ref, lon_even_ref, lat_even_ref, lat_odd_ref)

    def body(pair, at):
        scores = times(stacked(0, at, k_ref, *parts), scaled(q_ref[:, at])) + two_tables(table_ref, pair, pl.ds(0, NEAR))
        grad_prob = times(stacked(1, at, v_ref, *parts), both_heads(g_ref[:, at]))
        largest = jnp.max(scores, axis=0, keepdims=True)
        raised = jnp.exp(scores - largest)
        raised_ref[pair] = raised
        prob_ref[pair] = grad_prob
        stats_ref[pair, 0:1] = largest
        stats_ref[pair, 1:2] = column_sum(raised)
        stats_ref[pair, 2:3] = column_sum(raised * grad_prob)

    over_pairs(q_ref.shape[1], body)


def corner_kernel(
    q_ref, g_ref, corner_even_ref, corner_odd_ref, table_ref, near_stats_ref,
    raised_ref, prob_ref, stats_ref, send_even_ref, send_odd_ref, lines_ref,
):
    def score(pair, at):
        keys, values = (
            jnp.concatenate([corner_even_ref[slot, :, at], corner_odd_ref[slot, :, at]], axis=0) for slot in (0, 1)
        )
        scores = times(keys, scaled(q_ref[:, at])) + two_tables(table_ref, pair, pl.ds(NEAR, AROUND - NEAR))
        return scores, times(values, both_heads(g_ref[:, at]))

    scored = over_pairs(q_ref.shape[1], score)
    for pair, (scores, grad_prob) in enumerate(scored):
        near_largest = near_stats_ref[pair, 0:1]
        largest = jnp.maximum(near_largest, jnp.max(scores, axis=0, keepdims=True))
        raised = jnp.exp(scores - largest)
        shift = jnp.exp(near_largest - largest)
        total = near_stats_ref[pair, 1:2] * shift + column_sum(raised)
        inverse = 1.0 / total
        near_scale = shift * inverse
        row_dot = near_stats_ref[pair, 2:3] * near_scale + column_sum(raised * grad_prob) * inverse
        raised_ref[pair] = raised
        prob_ref[pair] = grad_prob
        stats_ref[pair, 0:1] = near_scale
        stats_ref[pair, 1:2] = row_dot
        stats_ref[pair, 2:3] = inverse
        for index, line in enumerate((largest + jnp.log(total), row_dot)):
            for head in (0, 1):
                at = 4 * pair + 2 * index + head
                lines_ref[at : at + 1] = line[:, head * CELLS : (head + 1) * CELLS]
    lines = lines_ref[...]
    low_rows = pltpu.roll(lines, BAND, 1)
    lat_odd = is_odd("lat")
    send_even_ref[...] = jnp.where(lat_odd, lines, low_rows)
    odd_lines = jnp.where(lat_odd, low_rows, lines)
    send_odd_ref[...] = jnp.concatenate([odd_lines] * (send_odd_ref.shape[0] // lines.shape[0]), axis=0)


def near_gradient(raised_ref, prob_ref, stats_ref, pair, rows):
    return score_gradient(raised_ref[pair, rows] * stats_ref[pair, 0:1], prob_ref[pair, rows], stats_ref[pair, 1:2])


def band_lines(lines_refs, pair):
    def row(first):
        return jnp.concatenate([ref[line : line + 1] for ref in lines_refs for line in (first, first + 1)], axis=1)

    return row(4 * pair), row(4 * pair + 2)


def band_queries(queries_refs, slot, at, prepare):
    empty = jnp.zeros((CELLS - BAND, PAIR), BF16)
    return jnp.concatenate([prepare(jnp.concatenate([ref[slot, :, at], empty], axis=0)) for ref in queries_refs], axis=0)


def band_tables(table_ref, pair, rows):
    return jnp.concatenate([table_ref[slot, 2 * pair + head, rows] for slot in (0, 1) for head in (0, 1)], axis=1)


def side_scores_kernel(
    q_ref, g_ref, raised_ref, prob_ref, stats_ref, lon_odd_ref, lon_even_ref, queries_even_ref, queries_odd_ref, table_ref,
    dlon_ref, scores_ref, prob_out_ref, band_q_ref, band_g_ref,
):
    queries_refs = (queries_even_ref, queries_odd_ref)

    def body(pair, at):
        keys, values = (
            jnp.concatenate([lon_odd_ref[slot, :, at], lon_even_ref[slot, :, at]], axis=0) for slot in (0, 1)
        )
        queries = band_queries(queries_refs, 0, at, scaled)
        grads = band_queries(queries_refs, 1, at, both_heads)
        band_q_ref[pair] = queries
        band_g_ref[pair] = grads
        scores_ref[pair] = times(keys, queries) + band_tables(table_ref, pair, pl.ds(LON_AT, 2 * SIDE))
        prob_out_ref[pair] = times(values, grads)
        weights, dscore = near_gradient(raised_ref, prob_ref, stats_ref, pair, pl.ds(LON_AT, LAT_AT - LON_AT))
        dlon_ref[0, :, at] = jnp.dot(dscore, scaled(q_ref[:, at]), preferred_element_type=F32)
        dlon_ref[1, :, at] = jnp.dot(weights, both_heads(g_ref[:, at]), preferred_element_type=F32)

    over_pairs(q_ref.shape[1], body)


def side_band_kernel(
    dlon_ref, scores_ref, prob_ref, band_q_ref, band_g_ref, lines_even_ref, lines_odd_ref, send_odd_ref, send_even_ref
):
    lines_refs = (lines_even_ref, lines_odd_ref)

    def score(pair, at):
        log_total, row_dot = band_lines(lines_refs, pair)
        return score_gradient(jnp.exp(scores_ref[pair] - log_total), prob_ref[pair], row_dot)

    width = dlon_ref.shape[2]
    scored = over_pairs(width, score)

    def finish(pair, at):
        weights, dscore = scored[pair]
        for slot, coefficients, other in ((0, dscore, band_q_ref), (1, weights, band_g_ref)):
            total = dlon_ref[slot, :, at] + jnp.dot(coefficients, other[pair], preferred_element_type=F32)
            send_odd_ref[slot, :, at] = total[:SIDE].astype(BF16)
            send_even_ref[slot, :, at] = total[SIDE:].astype(BF16)

    over_pairs(width, finish)


def own_kernel(
    q_ref, g_ref, k_ref, v_ref, lon_odd_ref, lon_even_ref, lat_even_ref, lat_odd_ref, corner_even_ref, corner_odd_ref,
    raised_ref, prob_ref, corner_raised_ref, corner_prob_ref, stats_ref, out_ref, dq_ref, own_ref,
):
    parts = (lon_odd_ref, lon_even_ref, lat_even_ref, lat_odd_ref, corner_even_ref, corner_odd_ref)

    def per_query(cells, coefficients):
        turned = jnp.dot(cells.T, coefficients, preferred_element_type=F32)
        mine = jnp.concatenate([turned[:HEAD_DIM, :CELLS], turned[HEAD_DIM:, CELLS:]], axis=0)
        return mine.T

    def body(pair, at):
        nearby = near_gradient(raised_ref, prob_ref, stats_ref, pair, pl.ds(0, NEAR))
        far = score_gradient(
            corner_raised_ref[pair] * stats_ref[pair, 2:3], corner_prob_ref[pair], stats_ref[pair, 1:2]
        )
        weights, dscore = (jnp.concatenate(x, axis=0) for x in zip(nearby, far))
        own_ref[0, :, at] = jnp.dot(dscore[:LON_AT], scaled(q_ref[:, at]), preferred_element_type=F32)
        own_ref[1, :, at] = jnp.dot(weights[:LON_AT], both_heads(g_ref[:, at]), preferred_element_type=F32)
        out_ref[:, at] = per_query(stacked(1, at, v_ref, *parts), weights).astype(BF16)
        dq_ref[:, at] = (per_query(stacked(0, at, k_ref, *parts), dscore) * FACTOR).astype(BF16)

    over_pairs(q_ref.shape[1], body)


def own_band_kernel(
    k_ref, v_ref, band_q_ref, band_g_ref, table_ref, lines_even_ref, lines_odd_ref, own_ref, total_ref
):
    def score(pair, at):
        log_total, row_dot = band_lines((lines_even_ref, lines_odd_ref), pair)
        scores = times(k_ref[:, at], band_q_ref[pair]) + band_tables(table_ref, pair, pl.ds(OWN_AT, CELLS))
        return score_gradient(jnp.exp(scores - log_total), times(v_ref[:, at], band_g_ref[pair]), row_dot)

    scored = over_pairs(k_ref.shape[1], score)

    def finish(pair, at):
        weights, dscore = scored[pair]
        for slot, coefficients, other in ((0, dscore, band_q_ref), (1, weights, band_g_ref)):
            grad = jnp.dot(coefficients, other[pair], preferred_element_type=F32)
            total_ref[slot, :, at] = own_ref[slot, :, at] + grad

    over_pairs(k_ref.shape[1], finish)


def final_kernel(total_ref, side_even_ref, side_odd_ref, dk_ref, dv_ref):
    lon_odd = is_odd("lon")
    shape = (CELLS, SIDE)
    cell = lax.broadcasted_iota(jnp.int32, shape, 0)
    place = lax.broadcasted_iota(jnp.int32, shape, 1)

    def spread(first_col):
        return (cell == (place % ROWS) * COLS + first_col + place // ROWS).astype(BF16)

    spread_odd = spread(jnp.where(lon_odd, COLS - RADIUS, 0))
    spread_even = spread(jnp.where(lon_odd, 0, COLS - RADIUS))
    for slot, out in ((0, dk_ref), (1, dv_ref)):
        total = (
            total_ref[slot]
            + jnp.dot(spread_odd, side_odd_ref[slot], preferred_element_type=F32)
            + jnp.dot(spread_even, side_even_ref[slot], preferred_element_type=F32)
        )
        out[...] = total.astype(BF16)


def arr(shape, dtype):
    return jax.ShapeDtypeStruct(shape, dtype)


def call(kernel, name, operands, results, flops=0, **more):
    moved = sum(x.size * x.dtype.itemsize for x in operands)
    return pl.pallas_call(
        kernel,
        out_shape=results,
        compiler_params=pltpu.CompilerParams(vmem_limit_bytes=32 * 1024 * 1024),
        cost_estimate=pl.CostEstimate(flops=flops, bytes_accessed=moved, transcendentals=0),
        name=name,
        **more,
    )(*operands)


def shards(queries, key_cells, value_cells, grad_output, rel_bias):
    block = queries.shape
    heads = rel_bias.shape[0]
    feat = block[-1]
    pairs = feat // PAIR
    cells = arr((CELLS, feat), BF16)
    side, band, corner = (arr((2, rows, feat), BF16) for rows in (SIDE, BAND, 2 * SIDE))
    work = 2 * CELLS * feat
    barrier = lax.optimization_barrier

    def in_hbm(x):
        return pltpu.with_memory_space_constraint(x, pltpu.HBM)

    hbm, vmem = (pl.BlockSpec(memory_space=space) for space in (pltpu.HBM, pltpu.VMEM))
    arguments = [in_hbm(x) for x in (key_cells.reshape(CELLS, feat), value_cells.reshape(CELLS, feat), rel_bias)]
    lon_odd, lon_even, k, v, rel_bias = call(
        pack_kernel, "pack", arguments, [side, side, cells, cells, arr(rel_bias.shape, F32)],
        in_specs=[hbm] * 3,
        scratch_shapes=[pltpu.SemaphoreType.DMA((3,))],
    )
    lon_odd = pair_exchange(lon_odd, "lon", 1, True)
    lon_even = pair_exchange(lon_even, "lon", 0, True)
    lat_even, lat_odd = call(rows_kernel, "rows", [k, v], [band, band])
    lat_even = pair_exchange(lat_even, "lat", 0, False)
    lat_odd = pair_exchange(lat_odd, "lat", 1, True)

    spread = [pltpu.VMEM((heads, TABLE), F32), pltpu.VMEM((2, heads, 8, TABLE), F32)]
    table, q, g = call(
        bias_kernel, "bias_table",
        [rel_bias, in_hbm(queries.reshape(CELLS, feat)), in_hbm(grad_output.reshape(CELLS, feat))],
        [arr((heads, AROUND, CELLS), F32), cells, cells], heads * AROUND * CELLS,
        in_specs=[vmem, hbm, hbm],
        scratch_shapes=[*spread, pltpu.SemaphoreType.DMA((2,))],
    )

    lon_odd, lon_even, table = barrier((lon_odd, lon_even, table))
    joined, = call(join_kernel, "join", [lon_odd, lon_even], [corner], int(2e9))
    corner_even = pair_exchange(joined, "lat", 0, False)
    corner_odd = odd_rows_exchange(joined)

    def scored(rows):
        return [arr((pairs, rows, 2 * CELLS), F32)] * 2 + [arr((pairs, 8, 2 * CELLS), F32)]

    near = [k, v, lon_odd, lon_even, lat_even, lat_odd]
    raised, prob, near_stats = call(near_kernel, "near", [q, g, *near, table], scored(NEAR), 4 * work * NEAR)
    late_q, late_g, _ = barrier((q, g, joined))
    queries_even, queries_odd = call(rows_kernel, "query_rows", [late_q, late_g], [band, band])
    queries_even = pair_exchange(queries_even, "lat", 0, False)
    queries_odd = odd_rows_exchange(queries_odd)
    band_table, = call(
        band_bias_kernel, "band_table", [rel_bias, near_stats], [arr((2, heads, LAT_AT, CELLS), F32)],
        2 * heads * LAT_AT * CELLS,
        scratch_shapes=spread,
    )
    corner_odd, band_table = barrier((corner_odd, band_table))
    lines = arr((4 * pairs, LANES), F32)
    corner_raised, corner_prob, stats, lines_even, lines_odd = call(
        corner_kernel, "corner", [q, g, corner_even, corner_odd, table, near_stats],
        scored(AROUND - NEAR) + [lines, arr((2 * lines.shape[0], LANES), F32)], 4 * work * (AROUND - NEAR),
        scratch_shapes=[pltpu.VMEM(lines.shape, F32)],
    )
    lines_even = pair_exchange(lines_even, "lat", 0, False)
    lines_odd = pair_exchange(lines_odd, "lat", 1, True)
    band_scores = [arr((pairs, 2 * SIDE, 4 * CELLS), F32)] * 2
    masked = [arr((pairs, 4 * CELLS, PAIR), BF16)] * 2
    dlon, side_scores, side_prob, band_q, band_g = call(
        side_scores_kernel, "side_scores",
        [q, g, raised, prob, stats, lon_odd, lon_even, queries_even, queries_odd, band_table],
        [arr(corner.shape, F32), *band_scores, *masked], 16 * work * SIDE,
    )
    lines_odd, dlon = barrier((lines_odd, dlon))
    send_odd, send_even = call(
        side_band_kernel, "side_band", [dlon, side_scores, side_prob, band_q, band_g, lines_even, lines_odd], [side, side],
        16 * work * SIDE,
    )
    side_even = pair_exchange(send_even, "lon", 0, True)
    side_odd = pair_exchange(send_odd, "lon", 1, True)
    out, dq, own = call(
        own_kernel, "own", [q, g, *near, corner_even, corner_odd, raised, prob, corner_raised, corner_prob, stats],
        [cells, cells, arr((2, CELLS, feat), F32)], 4 * work * AROUND,
    )
    total, = call(
        own_band_kernel, "own_band", [k, v, band_q, band_g, band_table, lines_even, lines_odd, own],
        [arr((2, CELLS, feat), F32)], 8 * work * CELLS,
    )
    dk, dv = call(final_kernel, "final", [total, side_even, side_odd], [cells, cells])
    return tuple(x.reshape(block) for x in (out, dq, dk, dv))


def solution(mesh):
    spec = P("lat", "lon", None)
    return jax.shard_map(
        shards, mesh=mesh, in_specs=(spec, spec, spec, spec, P()), out_specs=(spec,) * 4, check_vma=False
    )
```

```python
import functools

import jax
import jax.numpy as jnp
from jax import lax
from jax.experimental import pallas as pl
from jax.experimental.pallas import tpu as pltpu
from jax.sharding import PartitionSpec as P

HEAD_DIM = 64
RADIUS = 6
SPAN = 2 * RADIUS + 1
ROWS = 8
COLS = 16
CELLS = ROWS * COLS
SIDE = ROWS * RADIUS
BAND = RADIUS * COLS
PAIR = 2 * HEAD_DIM
BASE = 336
TABLE = 512
MASKED = -1e30

OWN_AT = 0
LON_AT = CELLS
LAT_AT = LON_AT + 2 * SIDE
NEAR = LAT_AT + 2 * BAND
EARLY = NEAR + 2 * SIDE
AROUND = EARLY + 2 * SIDE
LANES = 128

F32 = jnp.float32
BF16 = jnp.bfloat16


def pair_exchange(value, axis, odd, wrap):
    count = lax.axis_size(axis)
    pairs = []
    for first in range(odd, count, 2):
        second = first + 1
        if second >= count and not wrap:
            continue
        second %= count
        pairs += [(first, second), (second, first)]
    return lax.ppermute(value, axis, pairs)


def odd_rows_exchange(value):
    lats, lons = lax.axis_size("lat"), lax.axis_size("lon")
    pairs = []
    for lat in range(lats):
        for lon in range(lons):
            other = lat + 1 if lat % 2 else lat - 1
            inside = 0 <= other < lats
            target = (other, lon) if inside else (lat, lon ^ (1 if lons % 4 else 2))
            pairs.append((lat * lons + lon, target[0] * lons + target[1]))
    return lax.ppermute(value, ("lat", "lon"), pairs)


def is_odd(axis):
    return lax.axis_index(axis) % 2 == 1


def pick_matrix(first_col):
    shape = (SIDE, CELLS)
    place = lax.broadcasted_iota(jnp.int32, shape, 0)
    cell = lax.broadcasted_iota(jnp.int32, shape, 1)
    source = (place % ROWS) * COLS + first_col + place // ROWS
    return (cell == source).astype(BF16)


def pack_kernel(k_hbm, v_hbm, bias_hbm, lon_odd_ref, lon_even_ref, k_ref, v_ref, bias_ref, sems):
    copies = [
        pltpu.make_async_copy(source, target, sems.at[index])
        for index, (source, target) in enumerate(((k_hbm, k_ref), (v_hbm, v_ref), (bias_hbm, bias_ref)))
    ]
    for copy in copies:
        copy.start()
    lon_odd = is_odd("lon")
    first_cols = (jnp.where(lon_odd, COLS - RADIUS, 0), jnp.where(lon_odd, 0, COLS - RADIUS))
    picks = jnp.concatenate([pick_matrix(first_col) for first_col in first_cols], axis=0)
    for slot, source in ((0, k_ref), (1, v_ref)):
        copies[slot].wait()
        both = jnp.dot(picks, source[...], preferred_element_type=F32).astype(BF16)
        lon_odd_ref[slot] = both[:SIDE]
        lon_even_ref[slot] = both[SIDE:]
    copies[2].wait()


def lat_starts():
    lat_odd = is_odd("lat")
    even = jnp.where(lat_odd, 0, CELLS - BAND)
    return pl.multiple_of(even, 32), pl.multiple_of(CELLS - BAND - even, 32)


def rows_kernel(k_ref, v_ref, lat_even_ref, lat_odd_ref):
    for start, out in zip(lat_starts(), (lat_even_ref, lat_odd_ref)):
        out[0] = k_ref[pl.ds(start, BAND), :]
        out[1] = v_ref[pl.ds(start, BAND), :]


def bias_lines(bias_ref, line_ref):
    offset = BASE - lax.broadcasted_iota(jnp.int32, (1, TABLE), 1)
    row, col = offset // COLS, offset % COLS
    valid = (offset >= 0) & (row < SPAN) & (col < SPAN)
    entry = lax.broadcasted_iota(jnp.int32, (SPAN * SPAN, TABLE), 0)
    chosen = jnp.where(entry == jnp.where(valid, row * SPAN + col, -1), 1.0, 0.0).astype(BF16)
    rest = bias_ref[...]
    total = jnp.zeros((rest.shape[0], TABLE), F32)
    for _ in range(3):
        part = rest.astype(BF16)
        total = total + jnp.dot(part, chosen, preferred_element_type=F32)
        rest = rest - part.astype(F32)
    line_ref[...] = jnp.where(valid, total, MASKED)


def spread_rows(line_ref, spread_ref):
    heads = line_ref.shape[0]
    lines = [jnp.broadcast_to(line_ref[head : head + 1], (8, TABLE)) for head in range(heads)]
    x = jnp.concatenate(lines, axis=0)
    sub = lax.broadcasted_iota(jnp.int32, x.shape, 0)
    for index, stride in enumerate((1, COLS)):
        turned = x
        for bit in (1, 2, 4):
            turned = jnp.where((sub & bit) != 0, pltpu.roll(turned, bit * stride, 1), turned)
        for head in range(heads):
            spread_ref[index, head] = turned[8 * head : 8 * head + 8]


def windows(source, col, rows):
    firsts = [BASE - (COLS * row + col) for row in rows]
    turn = firsts[0] % LANES
    turned = pltpu.roll(source, TABLE - turn, 1) if turn else source
    return [turned[:, first - turn : first - turn + CELLS] for first in firsts]


def near(delta, there=None):
    allowed = (delta >= 0) & (delta < SPAN)
    return allowed if there is None else allowed & there


def places():
    west_slot = jnp.where(is_odd("lon"), SIDE, 0)
    north_slot = jnp.where(is_odd("lat"), 0, 1)
    has_north = lax.axis_index("lat") > 0
    has_south = lax.axis_index("lat") < lax.axis_size("lat") - 1
    sides = ((0, west_slot), (COLS + RADIUS, SIDE - west_slot))
    own_col = lax.broadcasted_iota(jnp.int32, (8, CELLS), 1) % COLS
    sub = lax.broadcasted_iota(jnp.int32, (8, CELLS), 0)
    return sides, north_slot, 1 - north_slot, has_north, has_south, own_col, sub


def bias_kernel(bias_ref, q_hbm, g_hbm, table_ref, q_ref, g_ref, line_ref, spread_ref, sems):
    copies = [
        pltpu.make_async_copy(source, target, sems.at[index])
        for index, (source, target) in enumerate(((q_hbm, q_ref), (g_hbm, g_ref)))
    ]
    for copy in copies:
        copy.start()
    bias_lines(bias_ref, line_ref)
    spread_rows(line_ref, spread_ref)
    sides, north_slot, south_slot, has_north, has_south, own_col, sub = places()

    def fill(head, carry):
        def put(at, values, allowed):
            table_ref[head, pl.ds(pl.multiple_of(at, 8), 8), :] = jnp.where(allowed, values, MASKED)

        by_one = spread_ref[0, head]
        for half in range(COLS // 8):
            delta = RADIUS + 8 * half + sub - own_col
            own, north, south = near(delta), near(delta, has_north), near(delta, has_south)
            for step in range(8):
                rows = [row for row in (step, step + 8, step + 16) if row < 2 * RADIUS + ROWS]
                for row, values in zip(rows, windows(by_one, RADIUS + 8 * half, rows)):
                    if row < RADIUS:
                        put(LAT_AT + north_slot * BAND + row * COLS + 8 * half, values, north)
                    elif row < RADIUS + ROWS:
                        put(OWN_AT + (row - RADIUS) * COLS + 8 * half, values, own)
                    else:
                        put(LAT_AT + south_slot * BAND + (row - RADIUS - ROWS) * COLS + 8 * half, values, south)
        by_row = spread_ref[1, head]
        rows = (RADIUS - ROWS, RADIUS, RADIUS + ROWS)
        for first_col, lon_slot in sides:
            for step in range(RADIUS):
                delta = first_col + step - own_col
                above, beside, below = windows(by_row, first_col + step, rows)
                at = lon_slot + step * ROWS
                put(LON_AT + at, beside, near(delta))
                put(NEAR + north_slot * 2 * SIDE + at, above, near(delta, has_north))
                put(NEAR + south_slot * 2 * SIDE + at, below, near(delta, has_south))
        return carry

    lax.fori_loop(0, bias_ref.shape[0], fill, 0, unroll=4)
    for copy in copies:
        copy.wait()


def band_bias_kernel(bias_ref, after_ref, table_ref, line_ref, spread_ref):
    del after_ref
    bias_lines(bias_ref, line_ref)
    spread_rows(line_ref, spread_ref)
    sides, north_slot, south_slot, has_north, has_south, own_col, sub = places()
    lane = lax.broadcasted_iota(jnp.int32, (8, CELLS), 1)
    bands = ((north_slot, RADIUS, has_north & (lane < BAND)), (south_slot, -ROWS, has_south & (lane < BAND)))

    def fill(head, carry):
        def put(slot, at, values, allowed):
            table_ref[slot, head, pl.ds(pl.multiple_of(at, 8), 8), :] = jnp.where(allowed, values, MASKED)

        by_one = spread_ref[0, head]
        for half in range(COLS // 8):
            delta = RADIUS + 8 * half + sub - own_col
            masks = [near(delta, there) for _, _, there in bands]
            for step in range(ROWS):
                rows = [next(row for row in range(ROWS) if (RADIUS + row + shift - step) % 8 == 0) for _, shift, _ in bands]
                found = windows(by_one, RADIUS + 8 * half, [RADIUS + row + band[1] for row, band in zip(rows, bands)])
                for row, band, mask, values in zip(rows, bands, masks, found):
                    put(band[0], OWN_AT + row * COLS + 8 * half, values, mask)
        by_row = spread_ref[1, head]
        for slot, shift, there in bands:
            for first_col, lon_slot in sides:
                for step in range(RADIUS):
                    (values,) = windows(by_row, first_col + step, (RADIUS + shift,))
                    put(slot, LON_AT + lon_slot + step * ROWS, values, near(first_col + step - own_col, there))
        return carry

    lax.fori_loop(0, bias_ref.shape[0], fill, 0, unroll=8)


LAST = (((1,), (1,)), ((), ()))
FACTOR = HEAD_DIM ** (-0.5)


def join_kernel(lon_odd_ref, lon_even_ref, out_ref):
    out_ref[:, :SIDE] = lon_odd_ref[...]
    out_ref[:, SIDE:] = lon_even_ref[...]


def over_pairs(width, body):
    return [body(pair, pl.ds(pair * PAIR, PAIR)) for pair in range(width // PAIR)]


def stacked(slot, at, own_ref, *refs):
    return jnp.concatenate([own_ref[:, at]] + [ref[slot, :, at] for ref in refs], axis=0)


def both_heads(block):
    first_head = lax.broadcasted_iota(jnp.int32, block.shape, 1) < HEAD_DIM
    zero = jnp.zeros_like(block)
    return jnp.concatenate([jnp.where(first_head, block, zero), jnp.where(first_head, zero, block)], axis=0)


def scaled(block):
    return both_heads(block * jnp.asarray(FACTOR, BF16))


def two_tables(table_ref, pair, rows):
    return jnp.concatenate([table_ref[2 * pair, rows], table_ref[2 * pair + 1, rows]], axis=1)


def times(left, right):
    return lax.dot_general(left, right, LAST, preferred_element_type=F32)


def column_sum(x):
    return jnp.sum(x, axis=0, keepdims=True)


def score_gradient(probability, grad_prob, row_dot):
    return probability.astype(BF16), (probability * (grad_prob - row_dot)).astype(BF16)


def near_kernel(
    q_ref, g_ref, k_ref, v_ref, lon_odd_ref, lon_even_ref, lat_even_ref, lat_odd_ref, corner_even_ref, table_ref,
    raised_ref, prob_ref, stats_ref,
):
    parts = (lon_odd_ref, lon_even_ref, lat_even_ref, lat_odd_ref, corner_even_ref)

    def body(pair, at):
        scores = times(stacked(0, at, k_ref, *parts), scaled(q_ref[:, at])) + two_tables(table_ref, pair, pl.ds(0, EARLY))
        grad_prob = times(stacked(1, at, v_ref, *parts), both_heads(g_ref[:, at]))
        largest = jnp.max(scores, axis=0, keepdims=True)
        raised = jnp.exp(scores - largest)
        raised_ref[pair] = raised
        prob_ref[pair] = grad_prob
        stats_ref[pair, 0:1] = largest
        stats_ref[pair, 1:2] = column_sum(raised)
        stats_ref[pair, 2:3] = column_sum(raised * grad_prob)

    over_pairs(q_ref.shape[1], body)


def corner_kernel(
    q_ref, g_ref, corner_ref, table_ref, near_stats_ref, raised_ref, prob_ref, stats_ref, send_even_ref, send_odd_ref, lines_ref
):
    def score(pair, at):
        scores = times(corner_ref[0, :, at], scaled(q_ref[:, at])) + two_tables(table_ref, pair, pl.ds(EARLY, AROUND - EARLY))
        return scores, times(corner_ref[1, :, at], both_heads(g_ref[:, at]))

    scored = over_pairs(q_ref.shape[1], score)
    for pair, (scores, grad_prob) in enumerate(scored):
        near_largest = near_stats_ref[pair, 0:1]
        largest = jnp.maximum(near_largest, jnp.max(scores, axis=0, keepdims=True))
        raised = jnp.exp(scores - largest)
        shift = jnp.exp(near_largest - largest)
        total = near_stats_ref[pair, 1:2] * shift + column_sum(raised)
        inverse = 1.0 / total
        near_scale = shift * inverse
        row_dot = near_stats_ref[pair, 2:3] * near_scale + column_sum(raised * grad_prob) * inverse
        raised_ref[pair] = raised
        prob_ref[pair] = grad_prob
        stats_ref[pair, 0:1] = near_scale
        stats_ref[pair, 1:2] = row_dot
        stats_ref[pair, 2:3] = inverse
        for index, line in enumerate((largest + jnp.log(total), row_dot)):
            for head in (0, 1):
                at = 4 * pair + 2 * index + head
                lines_ref[at : at + 1] = line[:, head * CELLS : (head + 1) * CELLS]
    lines = lines_ref[...]
    low_rows = pltpu.roll(lines, BAND, 1)
    lat_odd = is_odd("lat")
    send_even_ref[...] = jnp.where(lat_odd, lines, low_rows)
    odd_lines = jnp.where(lat_odd, low_rows, lines)
    send_odd_ref[...] = jnp.concatenate([odd_lines] * (send_odd_ref.shape[0] // lines.shape[0]), axis=0)


def near_gradient(raised_ref, prob_ref, stats_ref, pair, rows):
    return score_gradient(raised_ref[pair, rows] * stats_ref[pair, 0:1], prob_ref[pair, rows], stats_ref[pair, 1:2])


def band_lines(lines_refs, pair):
    def row(first):
        return jnp.concatenate([ref[line : line + 1] for ref in lines_refs for line in (first, first + 1)], axis=1)

    return row(4 * pair), row(4 * pair + 2)


def band_queries(queries_refs, slot, at, prepare):
    empty = jnp.zeros((CELLS - BAND, PAIR), BF16)
    return jnp.concatenate([prepare(jnp.concatenate([ref[slot, :, at], empty], axis=0)) for ref in queries_refs], axis=0)


def band_tables(table_ref, pair, rows):
    return jnp.concatenate([table_ref[slot, 2 * pair + head, rows] for slot in (0, 1) for head in (0, 1)], axis=1)


def side_scores_kernel(
    q_ref, g_ref, raised_ref, prob_ref, stats_ref, lon_odd_ref, lon_even_ref, queries_even_ref, queries_odd_ref, table_ref,
    dlon_ref, scores_ref, prob_out_ref, band_q_ref, band_g_ref,
):
    queries_refs = (queries_even_ref, queries_odd_ref)

    def body(pair, at):
        keys, values = (
            jnp.concatenate([lon_odd_ref[slot, :, at], lon_even_ref[slot, :, at]], axis=0) for slot in (0, 1)
        )
        queries = band_queries(queries_refs, 0, at, scaled)
        grads = band_queries(queries_refs, 1, at, both_heads)
        band_q_ref[pair] = queries
        band_g_ref[pair] = grads
        scores_ref[pair] = times(keys, queries) + band_tables(table_ref, pair, pl.ds(LON_AT, 2 * SIDE))
        prob_out_ref[pair] = times(values, grads)
        weights, dscore = near_gradient(raised_ref, prob_ref, stats_ref, pair, pl.ds(LON_AT, LAT_AT - LON_AT))
        dlon_ref[0, :, at] = jnp.dot(dscore, scaled(q_ref[:, at]), preferred_element_type=F32)
        dlon_ref[1, :, at] = jnp.dot(weights, both_heads(g_ref[:, at]), preferred_element_type=F32)

    over_pairs(q_ref.shape[1], body)


def side_terms(pair, at, lanes, scores_ref, prob_ref, lines_ref, band_q_ref, band_g_ref):
    log_total, row_dot = band_lines((lines_ref,), pair)
    weights, dscore = score_gradient(
        jnp.exp(scores_ref[pair, :, lanes] - log_total), prob_ref[pair, :, lanes], row_dot
    )
    return [
        jnp.dot(coefficients, other[pair, lanes], preferred_element_type=F32)
        for coefficients, other in ((dscore, band_q_ref), (weights, band_g_ref))
    ]


def side_even_kernel(dlon_ref, scores_ref, prob_ref, band_q_ref, band_g_ref, lines_ref, sum_ref):
    def body(pair, at):
        terms = side_terms(pair, at, pl.ds(0, 2 * CELLS), scores_ref, prob_ref, lines_ref, band_q_ref, band_g_ref)
        for slot, term in enumerate(terms):
            sum_ref[slot, :, at] = dlon_ref[slot, :, at] + term

    over_pairs(dlon_ref.shape[2], body)


def side_band_kernel(
    sum_ref, scores_ref, prob_ref, band_q_ref, band_g_ref, lines_ref, send_odd_ref, send_even_ref
):
    def body(pair, at):
        return side_terms(
            pair, at, pl.ds(2 * CELLS, 2 * CELLS), scores_ref, prob_ref, lines_ref, band_q_ref, band_g_ref
        )

    for pair, terms in enumerate(over_pairs(sum_ref.shape[2], body)):
        at = pl.ds(pair * PAIR, PAIR)
        for slot, term in enumerate(terms):
            total = (sum_ref[slot, :, at] + term).astype(BF16)
            send_odd_ref[slot, :, at] = total[:SIDE]
            send_even_ref[slot, :, at] = total[SIDE:]


def own_kernel(
    q_ref, g_ref, k_ref, v_ref, lon_odd_ref, lon_even_ref, lat_even_ref, lat_odd_ref, corner_even_ref, corner_odd_ref,
    raised_ref, prob_ref, corner_raised_ref, corner_prob_ref, stats_ref, out_ref, dq_ref, own_ref,
):
    parts = (lon_odd_ref, lon_even_ref, lat_even_ref, lat_odd_ref, corner_even_ref, corner_odd_ref)

    def per_query(cells, coefficients):
        turned = jnp.dot(cells.T, coefficients, preferred_element_type=F32)
        mine = jnp.concatenate([turned[:HEAD_DIM, :CELLS], turned[HEAD_DIM:, CELLS:]], axis=0)
        return mine.T

    def body(pair, at):
        nearby = near_gradient(raised_ref, prob_ref, stats_ref, pair, pl.ds(0, EARLY))
        far = score_gradient(
            corner_raised_ref[pair] * stats_ref[pair, 2:3], corner_prob_ref[pair], stats_ref[pair, 1:2]
        )
        weights, dscore = (jnp.concatenate(x, axis=0) for x in zip(nearby, far))
        own_ref[0, :, at] = jnp.dot(dscore[:LON_AT], scaled(q_ref[:, at]), preferred_element_type=F32)
        own_ref[1, :, at] = jnp.dot(weights[:LON_AT], both_heads(g_ref[:, at]), preferred_element_type=F32)
        out_ref[:, at] = per_query(stacked(1, at, v_ref, *parts), weights).astype(BF16)
        dq_ref[:, at] = (per_query(stacked(0, at, k_ref, *parts), dscore) * FACTOR).astype(BF16)

    over_pairs(q_ref.shape[1], body)


def own_band_kernel(
    k_ref, v_ref, band_q_ref, band_g_ref, table_ref, lines_even_ref, lines_odd_ref, own_ref, total_ref
):
    def score(pair, at):
        log_total, row_dot = band_lines((lines_even_ref, lines_odd_ref), pair)
        scores = times(k_ref[:, at], band_q_ref[pair]) + band_tables(table_ref, pair, pl.ds(OWN_AT, CELLS))
        return score_gradient(jnp.exp(scores - log_total), times(v_ref[:, at], band_g_ref[pair]), row_dot)

    scored = over_pairs(k_ref.shape[1], score)

    def finish(pair, at):
        weights, dscore = scored[pair]
        for slot, coefficients, other in ((0, dscore, band_q_ref), (1, weights, band_g_ref)):
            grad = jnp.dot(coefficients, other[pair], preferred_element_type=F32)
            total_ref[slot, :, at] = own_ref[slot, :, at] + grad

    over_pairs(k_ref.shape[1], finish)


def spread_matrix(first_col):
    shape = (CELLS, SIDE)
    cell = lax.broadcasted_iota(jnp.int32, shape, 0)
    place = lax.broadcasted_iota(jnp.int32, shape, 1)
    return (cell == (place % ROWS) * COLS + first_col + place // ROWS).astype(BF16)


def blend_kernel(total_ref, side_even_ref, blended_ref):
    spread = spread_matrix(jnp.where(is_odd("lon"), 0, COLS - RADIUS))
    for slot in (0, 1):
        blended_ref[slot] = total_ref[slot] + jnp.dot(spread, side_even_ref[slot], preferred_element_type=F32)


def final_kernel(blended_ref, side_odd_ref, dk_ref, dv_ref):
    spread = spread_matrix(jnp.where(is_odd("lon"), COLS - RADIUS, 0))
    for slot, out in ((0, dk_ref), (1, dv_ref)):
        total = blended_ref[slot] + jnp.dot(spread, side_odd_ref[slot], preferred_element_type=F32)
        out[...] = total.astype(BF16)


def arr(shape, dtype):
    return jax.ShapeDtypeStruct(shape, dtype)


def call(kernel, name, operands, results, flops=0, **more):
    moved = sum(x.size * x.dtype.itemsize for x in operands)
    return pl.pallas_call(
        kernel,
        out_shape=results,
        compiler_params=pltpu.CompilerParams(vmem_limit_bytes=32 * 1024 * 1024),
        cost_estimate=pl.CostEstimate(flops=flops, bytes_accessed=moved, transcendentals=0),
        name=name,
        **more,
    )(*operands)


def shards(queries, key_cells, value_cells, grad_output, rel_bias):
    block = queries.shape
    heads = rel_bias.shape[0]
    feat = block[-1]
    pairs = feat // PAIR
    cells = arr((CELLS, feat), BF16)
    side, band, corner = (arr((2, rows, feat), BF16) for rows in (SIDE, BAND, 2 * SIDE))
    work = 2 * CELLS * feat
    barrier = lax.optimization_barrier

    def in_hbm(x):
        return pltpu.with_memory_space_constraint(x, pltpu.HBM)

    hbm, vmem = (pl.BlockSpec(memory_space=space) for space in (pltpu.HBM, pltpu.VMEM))
    arguments = [in_hbm(x) for x in (key_cells.reshape(CELLS, feat), value_cells.reshape(CELLS, feat), rel_bias)]
    lon_odd, lon_even, k, v, rel_bias = call(
        pack_kernel, "pack", arguments, [side, side, cells, cells, arr(rel_bias.shape, F32)],
        in_specs=[hbm] * 3,
        scratch_shapes=[pltpu.SemaphoreType.DMA((3,))],
    )
    lon_odd = pair_exchange(lon_odd, "lon", 1, True)
    lon_even = pair_exchange(lon_even, "lon", 0, True)
    lat_even, lat_odd = call(rows_kernel, "rows", [k, v], [band, band])
    lat_even = pair_exchange(lat_even, "lat", 0, False)
    lat_odd = pair_exchange(lat_odd, "lat", 1, True)

    spread = [pltpu.VMEM((heads, TABLE), F32), pltpu.VMEM((2, heads, 8, TABLE), F32)]
    table, q, g = call(
        bias_kernel, "bias_table",
        [rel_bias, in_hbm(queries.reshape(CELLS, feat)), in_hbm(grad_output.reshape(CELLS, feat))],
        [arr((heads, AROUND, CELLS), F32), cells, cells], heads * AROUND * CELLS,
        in_specs=[vmem, hbm, hbm],
        scratch_shapes=[*spread, pltpu.SemaphoreType.DMA((2,))],
    )

    lon_odd, lon_even, table = barrier((lon_odd, lon_even, table))
    joined, = call(join_kernel, "join", [lon_odd, lon_even], [corner], int(2e9))
    corner_even = pair_exchange(joined, "lat", 0, False)
    corner_odd = odd_rows_exchange(joined)

    def scored(rows):
        return [arr((pairs, rows, 2 * CELLS), F32)] * 2 + [arr((pairs, 8, 2 * CELLS), F32)]

    near = [k, v, lon_odd, lon_even, lat_even, lat_odd]
    raised, prob, near_stats = call(near_kernel, "near", [q, g, *near, corner_even, table], scored(EARLY), 4 * work * EARLY)
    late_q, late_g, _ = barrier((q, g, joined))
    queries_even, queries_odd = call(rows_kernel, "query_rows", [late_q, late_g], [band, band])
    band_table, = call(
        band_bias_kernel, "band_table", [rel_bias, queries_odd], [arr((2, heads, LAT_AT, CELLS), F32)],
        2 * heads * LAT_AT * CELLS,
        scratch_shapes=spread,
    )
    table, band_table = barrier((table, band_table))
    queries_even = pair_exchange(queries_even, "lat", 0, False)
    queries_odd = odd_rows_exchange(queries_odd)
    lines = arr((4 * pairs, LANES), F32)
    corner_raised, corner_prob, stats, lines_even, lines_odd = call(
        corner_kernel, "corner", [q, g, corner_odd, table, near_stats],
        scored(AROUND - EARLY) + [lines, arr((2 * lines.shape[0], LANES), F32)], 4 * work * (AROUND - EARLY),
        scratch_shapes=[pltpu.VMEM(lines.shape, F32)],
    )
    lines_even = pair_exchange(lines_even, "lat", 0, False)
    lines_odd = pair_exchange(lines_odd, "lat", 1, True)
    band_scores = [arr((pairs, 2 * SIDE, 4 * CELLS), F32)] * 2
    masked = [arr((pairs, 4 * CELLS, PAIR), BF16)] * 2
    dlon, side_scores, side_prob, band_q, band_g = call(
        side_scores_kernel, "side_scores",
        [q, g, raised, prob, stats, lon_odd, lon_even, queries_even, queries_odd, band_table],
        [arr(corner.shape, F32), *band_scores, *masked], 16 * work * SIDE,
    )
    dlon, = call(
        side_even_kernel, "side_even", [dlon, side_scores, side_prob, band_q, band_g, lines_even],
        [arr(corner.shape, F32)], 8 * work * SIDE,
    )
    lines_odd, dlon = barrier((lines_odd, dlon))
    send_odd, send_even = call(
        side_band_kernel, "side_band", [dlon, side_scores, side_prob, band_q, band_g, lines_odd], [side, side],
        8 * work * SIDE,
    )
    side_even = pair_exchange(send_even, "lon", 0, True)
    side_odd = pair_exchange(send_odd, "lon", 1, True)
    out, dq, own = call(
        own_kernel, "own", [q, g, *near, corner_even, corner_odd, raised, prob, corner_raised, corner_prob, stats],
        [cells, cells, arr((2, CELLS, feat), F32)], 4 * work * AROUND,
    )
    total, = call(
        own_band_kernel, "own_band", [k, v, band_q, band_g, band_table, lines_even, lines_odd, own],
        [arr((2, CELLS, feat), F32)], 8 * work * CELLS,
    )
    blended, = call(blend_kernel, "blend", [total, side_even], [arr((2, CELLS, feat), F32)])
    dk, dv = call(final_kernel, "final", [blended, side_odd], [cells, cells])
    return tuple(x.reshape(block) for x in (out, dq, dk, dv))


def solution(mesh):
    spec = P("lat", "lon", None)
    return jax.shard_map(
        shards, mesh=mesh, in_specs=(spec, spec, spec, spec, P()), out_specs=(spec,) * 4, check_vma=False
    )
```

```python
import functools

import jax
import jax.numpy as jnp
from jax import lax
from jax.experimental import pallas as pl
from jax.experimental.pallas import tpu as pltpu
from jax.sharding import PartitionSpec as P

HEAD_DIM = 64
RADIUS = 6
SPAN = 2 * RADIUS + 1
ROWS = 8
COLS = 16
CELLS = ROWS * COLS
SIDE = ROWS * RADIUS
BAND = RADIUS * COLS
PAIR = 2 * HEAD_DIM
BASE = 336
TABLE = 512
MASKED = -1e30

OWN_AT = 0
LON_AT = CELLS
LAT_AT = LON_AT + 2 * SIDE
NEAR = LAT_AT + 2 * BAND
EARLY = NEAR + 2 * SIDE
AROUND = EARLY + 2 * SIDE
LANES = 128

F32 = jnp.float32
BF16 = jnp.bfloat16


def pair_exchange(value, axis, odd, wrap):
    count = lax.axis_size(axis)
    pairs = []
    for first in range(odd, count, 2):
        second = first + 1
        if second >= count and not wrap:
            continue
        second %= count
        pairs += [(first, second), (second, first)]
    return lax.ppermute(value, axis, pairs)


def odd_rows_exchange(value):
    lats, lons = lax.axis_size("lat"), lax.axis_size("lon")
    pairs = []
    for lat in range(lats):
        for lon in range(lons):
            other = lat + 1 if lat % 2 else lat - 1
            inside = 0 <= other < lats
            target = (other, lon) if inside else (lat, lon ^ (1 if lons % 4 else 2))
            pairs.append((lat * lons + lon, target[0] * lons + target[1]))
    return lax.ppermute(value, ("lat", "lon"), pairs)


def is_odd(axis):
    return lax.axis_index(axis) % 2 == 1


def pick_matrix(first_col):
    shape = (SIDE, CELLS)
    place = lax.broadcasted_iota(jnp.int32, shape, 0)
    cell = lax.broadcasted_iota(jnp.int32, shape, 1)
    source = (place % ROWS) * COLS + first_col + place // ROWS
    return (cell == source).astype(BF16)


def pack_kernel(k_hbm, v_hbm, bias_hbm, lon_odd_ref, lon_even_ref, k_ref, v_ref, bias_ref, sems):
    copies = [
        pltpu.make_async_copy(source, target, sems.at[index])
        for index, (source, target) in enumerate(((k_hbm, k_ref), (v_hbm, v_ref), (bias_hbm, bias_ref)))
    ]
    for copy in copies:
        copy.start()
    lon_odd = is_odd("lon")
    first_cols = (jnp.where(lon_odd, COLS - RADIUS, 0), jnp.where(lon_odd, 0, COLS - RADIUS))
    picks = jnp.concatenate([pick_matrix(first_col) for first_col in first_cols], axis=0)
    for slot, source in ((0, k_ref), (1, v_ref)):
        copies[slot].wait()
        both = jnp.dot(picks, source[...], preferred_element_type=F32).astype(BF16)
        lon_odd_ref[slot] = both[:SIDE]
        lon_even_ref[slot] = both[SIDE:]
    copies[2].wait()


def lat_starts():
    lat_odd = is_odd("lat")
    even = jnp.where(lat_odd, 0, CELLS - BAND)
    return pl.multiple_of(even, 32), pl.multiple_of(CELLS - BAND - even, 32)


def rows_kernel(k_ref, v_ref, lat_even_ref, lat_odd_ref):
    for start, out in zip(lat_starts(), (lat_even_ref, lat_odd_ref)):
        out[0] = k_ref[pl.ds(start, BAND), :]
        out[1] = v_ref[pl.ds(start, BAND), :]


def bias_lines(bias_ref, line_ref):
    offset = BASE - lax.broadcasted_iota(jnp.int32, (1, TABLE), 1)
    row, col = offset // COLS, offset % COLS
    valid = (offset >= 0) & (row < SPAN) & (col < SPAN)
    entry = lax.broadcasted_iota(jnp.int32, (SPAN * SPAN, TABLE), 0)
    chosen = jnp.where(entry == jnp.where(valid, row * SPAN + col, -1), 1.0, 0.0).astype(BF16)
    rest = bias_ref[...]
    total = jnp.zeros((rest.shape[0], TABLE), F32)
    for _ in range(3):
        part = rest.astype(BF16)
        total = total + jnp.dot(part, chosen, preferred_element_type=F32)
        rest = rest - part.astype(F32)
    line_ref[...] = jnp.where(valid, total, MASKED)


def spread_rows(line_ref, spread_ref):
    heads = line_ref.shape[0]
    lines = [jnp.broadcast_to(line_ref[head : head + 1], (8, TABLE)) for head in range(heads)]
    x = jnp.concatenate(lines, axis=0)
    sub = lax.broadcasted_iota(jnp.int32, x.shape, 0)
    for index, stride in enumerate((1, COLS)):
        turned = x
        for bit in (1, 2, 4):
            turned = jnp.where((sub & bit) != 0, pltpu.roll(turned, bit * stride, 1), turned)
        for head in range(heads):
            spread_ref[index, head] = turned[8 * head : 8 * head + 8]


def windows(source, col, rows):
    firsts = [BASE - (COLS * row + col) for row in rows]
    turn = firsts[0] % LANES
    turned = pltpu.roll(source, TABLE - turn, 1) if turn else source
    return [turned[:, first - turn : first - turn + CELLS] for first in firsts]


def near(delta, there=None):
    allowed = (delta >= 0) & (delta < SPAN)
    return allowed if there is None else allowed & there


def places():
    west_slot = jnp.where(is_odd("lon"), SIDE, 0)
    north_slot = jnp.where(is_odd("lat"), 0, 1)
    has_north = lax.axis_index("lat") > 0
    has_south = lax.axis_index("lat") < lax.axis_size("lat") - 1
    sides = ((0, west_slot), (COLS + RADIUS, SIDE - west_slot))
    own_col = lax.broadcasted_iota(jnp.int32, (8, CELLS), 1) % COLS
    sub = lax.broadcasted_iota(jnp.int32, (8, CELLS), 0)
    return sides, north_slot, 1 - north_slot, has_north, has_south, own_col, sub


def bias_kernel(bias_ref, q_hbm, g_hbm, table_ref, q_ref, g_ref, line_ref, spread_ref, sems):
    copies = [
        pltpu.make_async_copy(source, target, sems.at[index])
        for index, (source, target) in enumerate(((q_hbm, q_ref), (g_hbm, g_ref)))
    ]
    for copy in copies:
        copy.start()
    bias_lines(bias_ref, line_ref)
    spread_rows(line_ref, spread_ref)
    sides, north_slot, south_slot, has_north, has_south, own_col, sub = places()

    def fill(head, carry):
        def put(at, values, allowed):
            table_ref[head, pl.ds(pl.multiple_of(at, 8), 8), :] = jnp.where(allowed, values, MASKED)

        by_one = spread_ref[0, head]
        for half in range(COLS // 8):
            delta = RADIUS + 8 * half + sub - own_col
            own, north, south = near(delta), near(delta, has_north), near(delta, has_south)
            for step in range(8):
                rows = [row for row in (step, step + 8, step + 16) if row < 2 * RADIUS + ROWS]
                for row, values in zip(rows, windows(by_one, RADIUS + 8 * half, rows)):
                    if row < RADIUS:
                        put(LAT_AT + north_slot * BAND + row * COLS + 8 * half, values, north)
                    elif row < RADIUS + ROWS:
                        put(OWN_AT + (row - RADIUS) * COLS + 8 * half, values, own)
                    else:
                        put(LAT_AT + south_slot * BAND + (row - RADIUS - ROWS) * COLS + 8 * half, values, south)
        by_row = spread_ref[1, head]
        rows = (RADIUS - ROWS, RADIUS, RADIUS + ROWS)
        for first_col, lon_slot in sides:
            for step in range(RADIUS):
                delta = first_col + step - own_col
                above, beside, below = windows(by_row, first_col + step, rows)
                at = lon_slot + step * ROWS
                put(LON_AT + at, beside, near(delta))
                put(NEAR + north_slot * 2 * SIDE + at, above, near(delta, has_north))
                put(NEAR + south_slot * 2 * SIDE + at, below, near(delta, has_south))
        return carry

    lax.fori_loop(0, bias_ref.shape[0], fill, 0, unroll=4)
    for copy in copies:
        copy.wait()


def band_bias_kernel(bias_ref, after_ref, table_ref, line_ref, spread_ref):
    del after_ref
    bias_lines(bias_ref, line_ref)
    spread_rows(line_ref, spread_ref)
    sides, north_slot, south_slot, has_north, has_south, own_col, sub = places()
    lane = lax.broadcasted_iota(jnp.int32, (8, CELLS), 1)
    bands = ((north_slot, RADIUS, has_north & (lane < BAND)), (south_slot, -ROWS, has_south & (lane < BAND)))

    def fill(head, carry):
        def put(slot, at, values, allowed):
            table_ref[slot, head, pl.ds(pl.multiple_of(at, 8), 8), :] = jnp.where(allowed, values, MASKED)

        by_one = spread_ref[0, head]
        for half in range(COLS // 8):
            delta = RADIUS + 8 * half + sub - own_col
            masks = [near(delta, there) for _, _, there in bands]
            for step in range(ROWS):
                rows = [next(row for row in range(ROWS) if (RADIUS + row + shift - step) % 8 == 0) for _, shift, _ in bands]
                found = windows(by_one, RADIUS + 8 * half, [RADIUS + row + band[1] for row, band in zip(rows, bands)])
                for row, band, mask, values in zip(rows, bands, masks, found):
                    put(band[0], OWN_AT + row * COLS + 8 * half, values, mask)
        by_row = spread_ref[1, head]
        for slot, shift, there in bands:
            for first_col, lon_slot in sides:
                for step in range(RADIUS):
                    (values,) = windows(by_row, first_col + step, (RADIUS + shift,))
                    put(slot, LON_AT + lon_slot + step * ROWS, values, near(first_col + step - own_col, there))
        return carry

    lax.fori_loop(0, bias_ref.shape[0], fill, 0, unroll=8)


LAST = (((1,), (1,)), ((), ()))
FACTOR = HEAD_DIM ** (-0.5)


def join_kernel(lon_even_ref, lon_odd_ref, out_ref):
    out_ref[:, :SIDE] = lon_odd_ref[...]
    out_ref[:, SIDE:] = lon_even_ref[...]


def over_pairs(width, body):
    return [body(pair, pl.ds(pair * PAIR, PAIR)) for pair in range(width // PAIR)]


def stacked(slot, at, own_ref, *refs):
    return jnp.concatenate([own_ref[:, at]] + [ref[slot, :, at] for ref in refs], axis=0)


def both_heads(block):
    first_head = lax.broadcasted_iota(jnp.int32, block.shape, 1) < HEAD_DIM
    zero = jnp.zeros_like(block)
    return jnp.concatenate([jnp.where(first_head, block, zero), jnp.where(first_head, zero, block)], axis=0)


def scaled(block):
    return both_heads(block * jnp.asarray(FACTOR, BF16))


def two_tables(table_ref, pair, rows):
    return jnp.concatenate([table_ref[2 * pair, rows], table_ref[2 * pair + 1, rows]], axis=1)


def times(left, right):
    return lax.dot_general(left, right, LAST, preferred_element_type=F32)


def column_sum(x):
    return jnp.sum(x, axis=0, keepdims=True)


def score_gradient(probability, grad_prob, row_dot):
    return probability.astype(BF16), (probability * (grad_prob - row_dot)).astype(BF16)


def near_kernel(
    q_ref, g_ref, k_ref, v_ref, lon_odd_ref, lon_even_ref, lat_even_ref, lat_odd_ref, corner_even_ref, table_ref,
    raised_ref, prob_ref, stats_ref,
):
    parts = (lon_odd_ref, lon_even_ref, lat_even_ref, lat_odd_ref, corner_even_ref)

    def body(pair, at):
        scores = times(stacked(0, at, k_ref, *parts), scaled(q_ref[:, at])) + two_tables(table_ref, pair, pl.ds(0, EARLY))
        grad_prob = times(stacked(1, at, v_ref, *parts), both_heads(g_ref[:, at]))
        largest = jnp.max(scores, axis=0, keepdims=True)
        raised = jnp.exp(scores - largest)
        raised_ref[pair] = raised
        prob_ref[pair] = grad_prob
        stats_ref[pair, 0:1] = largest
        stats_ref[pair, 1:2] = column_sum(raised)
        stats_ref[pair, 2:3] = column_sum(raised * grad_prob)

    over_pairs(q_ref.shape[1], body)


def corner_kernel(
    q_ref, g_ref, corner_ref, table_ref, near_stats_ref, raised_ref, prob_ref, stats_ref, send_even_ref, send_odd_ref, lines_ref
):
    def score(pair, at):
        scores = times(corner_ref[0, :, at], scaled(q_ref[:, at])) + two_tables(table_ref, pair, pl.ds(EARLY, AROUND - EARLY))
        return scores, times(corner_ref[1, :, at], both_heads(g_ref[:, at]))

    scored = over_pairs(q_ref.shape[1], score)
    for pair, (scores, grad_prob) in enumerate(scored):
        near_largest = near_stats_ref[pair, 0:1]
        largest = jnp.maximum(near_largest, jnp.max(scores, axis=0, keepdims=True))
        raised = jnp.exp(scores - largest)
        shift = jnp.exp(near_largest - largest)
        total = near_stats_ref[pair, 1:2] * shift + column_sum(raised)
        inverse = 1.0 / total
        near_scale = shift * inverse
        row_dot = near_stats_ref[pair, 2:3] * near_scale + column_sum(raised * grad_prob) * inverse
        raised_ref[pair] = raised
        prob_ref[pair] = grad_prob
        stats_ref[pair, 0:1] = near_scale
        stats_ref[pair, 1:2] = row_dot
        stats_ref[pair, 2:3] = inverse
        for index, line in enumerate((largest + jnp.log(total), row_dot)):
            for head in (0, 1):
                at = 4 * pair + 2 * index + head
                lines_ref[at : at + 1] = line[:, head * CELLS : (head + 1) * CELLS]
    lines = lines_ref[...]
    low_rows = pltpu.roll(lines, BAND, 1)
    lat_odd = is_odd("lat")
    send_even_ref[...] = jnp.where(lat_odd, lines, low_rows)
    odd_lines = jnp.where(lat_odd, low_rows, lines)
    send_odd_ref[...] = jnp.concatenate([odd_lines] * (send_odd_ref.shape[0] // lines.shape[0]), axis=0)


def near_gradient(raised_ref, prob_ref, stats_ref, pair, rows):
    return score_gradient(raised_ref[pair, rows] * stats_ref[pair, 0:1], prob_ref[pair, rows], stats_ref[pair, 1:2])


def band_lines(lines_refs, pair):
    def row(first):
        return jnp.concatenate([ref[line : line + 1] for ref in lines_refs for line in (first, first + 1)], axis=1)

    return row(4 * pair), row(4 * pair + 2)


def band_queries(queries_refs, slot, at, prepare):
    empty = jnp.zeros((CELLS - BAND, PAIR), BF16)
    return jnp.concatenate([prepare(jnp.concatenate([ref[slot, :, at], empty], axis=0)) for ref in queries_refs], axis=0)


def band_tables(table_ref, pair, rows):
    return jnp.concatenate([table_ref[slot, 2 * pair + head, rows] for slot in (0, 1) for head in (0, 1)], axis=1)


def side_scores_kernel(
    q_ref, g_ref, raised_ref, prob_ref, stats_ref, lon_odd_ref, lon_even_ref, queries_even_ref, queries_odd_ref, table_ref,
    dlon_ref, scores_ref, prob_out_ref, band_q_ref, band_g_ref,
):
    queries_refs = (queries_even_ref, queries_odd_ref)

    def body(pair, at):
        keys, values = (
            jnp.concatenate([lon_odd_ref[slot, :, at], lon_even_ref[slot, :, at]], axis=0) for slot in (0, 1)
        )
        queries = band_queries(queries_refs, 0, at, scaled)
        grads = band_queries(queries_refs, 1, at, both_heads)
        band_q_ref[pair] = queries
        band_g_ref[pair] = grads
        scores_ref[pair] = times(keys, queries) + band_tables(table_ref, pair, pl.ds(LON_AT, 2 * SIDE))
        prob_out_ref[pair] = times(values, grads)
        weights, dscore = near_gradient(raised_ref, prob_ref, stats_ref, pair, pl.ds(LON_AT, LAT_AT - LON_AT))
        dlon_ref[0, :, at] = jnp.dot(dscore, scaled(q_ref[:, at]), preferred_element_type=F32)
        dlon_ref[1, :, at] = jnp.dot(weights, both_heads(g_ref[:, at]), preferred_element_type=F32)

    over_pairs(q_ref.shape[1], body)


def side_terms(pair, at, lanes, scores_ref, prob_ref, lines_ref, band_q_ref, band_g_ref):
    log_total, row_dot = band_lines((lines_ref,), pair)
    weights, dscore = score_gradient(
        jnp.exp(scores_ref[pair, :, lanes] - log_total), prob_ref[pair, :, lanes], row_dot
    )
    return [
        jnp.dot(coefficients, other[pair, lanes], preferred_element_type=F32)
        for coefficients, other in ((dscore, band_q_ref), (weights, band_g_ref))
    ]


def side_even_kernel(dlon_ref, scores_ref, prob_ref, band_q_ref, band_g_ref, lines_ref, sum_ref):
    def body(pair, at):
        terms = side_terms(pair, at, pl.ds(0, 2 * CELLS), scores_ref, prob_ref, lines_ref, band_q_ref, band_g_ref)
        for slot, term in enumerate(terms):
            sum_ref[slot, :, at] = dlon_ref[slot, :, at] + term

    over_pairs(dlon_ref.shape[2], body)


def side_band_kernel(
    sum_ref, scores_ref, prob_ref, band_q_ref, band_g_ref, lines_ref, send_odd_ref, send_even_ref
):
    def body(pair, at):
        return side_terms(
            pair, at, pl.ds(2 * CELLS, 2 * CELLS), scores_ref, prob_ref, lines_ref, band_q_ref, band_g_ref
        )

    for pair, terms in enumerate(over_pairs(sum_ref.shape[2], body)):
        at = pl.ds(pair * PAIR, PAIR)
        for slot, term in enumerate(terms):
            total = (sum_ref[slot, :, at] + term).astype(BF16)
            send_odd_ref[slot, :, at] = total[:SIDE]
            send_even_ref[slot, :, at] = total[SIDE:]


def own_kernel(
    q_ref, g_ref, k_ref, v_ref, lon_odd_ref, lon_even_ref, lat_even_ref, lat_odd_ref, corner_even_ref, corner_odd_ref,
    raised_ref, prob_ref, corner_raised_ref, corner_prob_ref, stats_ref, out_ref, dq_ref, own_ref,
):
    parts = (lon_odd_ref, lon_even_ref, lat_even_ref, lat_odd_ref, corner_even_ref, corner_odd_ref)

    def per_query(cells, coefficients):
        turned = jnp.dot(cells.T, coefficients, preferred_element_type=F32)
        mine = jnp.concatenate([turned[:HEAD_DIM, :CELLS], turned[HEAD_DIM:, CELLS:]], axis=0)
        return mine.T

    def body(pair, at):
        nearby = near_gradient(raised_ref, prob_ref, stats_ref, pair, pl.ds(0, EARLY))
        far = score_gradient(
            corner_raised_ref[pair] * stats_ref[pair, 2:3], corner_prob_ref[pair], stats_ref[pair, 1:2]
        )
        weights, dscore = (jnp.concatenate(x, axis=0) for x in zip(nearby, far))
        own_ref[0, :, at] = jnp.dot(dscore[:LON_AT], scaled(q_ref[:, at]), preferred_element_type=F32)
        own_ref[1, :, at] = jnp.dot(weights[:LON_AT], both_heads(g_ref[:, at]), preferred_element_type=F32)
        out_ref[:, at] = per_query(stacked(1, at, v_ref, *parts), weights).astype(BF16)
        dq_ref[:, at] = (per_query(stacked(0, at, k_ref, *parts), dscore) * FACTOR).astype(BF16)

    over_pairs(q_ref.shape[1], body)


def own_band_kernel(
    k_ref, v_ref, band_q_ref, band_g_ref, table_ref, lines_even_ref, lines_odd_ref, own_ref, total_ref
):
    def score(pair, at):
        log_total, row_dot = band_lines((lines_even_ref, lines_odd_ref), pair)
        scores = times(k_ref[:, at], band_q_ref[pair]) + band_tables(table_ref, pair, pl.ds(OWN_AT, CELLS))
        return score_gradient(jnp.exp(scores - log_total), times(v_ref[:, at], band_g_ref[pair]), row_dot)

    scored = over_pairs(k_ref.shape[1], score)

    def finish(pair, at):
        weights, dscore = scored[pair]
        for slot, coefficients, other in ((0, dscore, band_q_ref), (1, weights, band_g_ref)):
            grad = jnp.dot(coefficients, other[pair], preferred_element_type=F32)
            total_ref[slot, :, at] = own_ref[slot, :, at] + grad

    over_pairs(k_ref.shape[1], finish)


def spread_matrix(first_col):
    shape = (CELLS, SIDE)
    cell = lax.broadcasted_iota(jnp.int32, shape, 0)
    place = lax.broadcasted_iota(jnp.int32, shape, 1)
    return (cell == (place % ROWS) * COLS + first_col + place // ROWS).astype(BF16)


def blend_kernel(total_ref, side_even_ref, blended_ref):
    spread = spread_matrix(jnp.where(is_odd("lon"), 0, COLS - RADIUS))
    for slot in (0, 1):
        blended_ref[slot] = total_ref[slot] + jnp.dot(spread, side_even_ref[slot], preferred_element_type=F32)


def final_kernel(blended_ref, side_odd_ref, dk_ref, dv_ref):
    spread = spread_matrix(jnp.where(is_odd("lon"), COLS - RADIUS, 0))
    for slot, out in ((0, dk_ref), (1, dv_ref)):
        total = blended_ref[slot] + jnp.dot(spread, side_odd_ref[slot], preferred_element_type=F32)
        out[...] = total.astype(BF16)


def arr(shape, dtype):
    return jax.ShapeDtypeStruct(shape, dtype)


def call(kernel, name, operands, results, flops=0, **more):
    moved = sum(x.size * x.dtype.itemsize for x in operands)
    return pl.pallas_call(
        kernel,
        out_shape=results,
        compiler_params=pltpu.CompilerParams(vmem_limit_bytes=32 * 1024 * 1024),
        cost_estimate=pl.CostEstimate(flops=flops, bytes_accessed=moved, transcendentals=0),
        name=name,
        **more,
    )(*operands)


def shards(queries, key_cells, value_cells, grad_output, rel_bias):
    block = queries.shape
    heads = rel_bias.shape[0]
    feat = block[-1]
    pairs = feat // PAIR
    cells = arr((CELLS, feat), BF16)
    side, band, corner = (arr((2, rows, feat), BF16) for rows in (SIDE, BAND, 2 * SIDE))
    work = 2 * CELLS * feat
    barrier = lax.optimization_barrier

    def in_hbm(x):
        return pltpu.with_memory_space_constraint(x, pltpu.HBM)

    hbm, vmem = (pl.BlockSpec(memory_space=space) for space in (pltpu.HBM, pltpu.VMEM))
    arguments = [in_hbm(x) for x in (key_cells.reshape(CELLS, feat), value_cells.reshape(CELLS, feat), rel_bias)]
    lon_odd, lon_even, k, v, rel_bias = call(
        pack_kernel, "pack", arguments, [side, side, cells, cells, arr(rel_bias.shape, F32)],
        in_specs=[hbm] * 3,
        scratch_shapes=[pltpu.SemaphoreType.DMA((3,))],
    )
    lon_even = pair_exchange(lon_even, "lon", 0, True)
    lon_odd = pair_exchange(lon_odd, "lon", 1, True)
    lat_even, lat_odd = call(rows_kernel, "rows", [k, v], [band, band])
    lat_even = pair_exchange(lat_even, "lat", 0, False)
    lat_odd = pair_exchange(lat_odd, "lat", 1, True)

    spread = [pltpu.VMEM((heads, TABLE), F32), pltpu.VMEM((2, heads, 8, TABLE), F32)]
    table, q, g = call(
        bias_kernel, "bias_table",
        [rel_bias, in_hbm(queries.reshape(CELLS, feat)), in_hbm(grad_output.reshape(CELLS, feat))],
        [arr((heads, AROUND, CELLS), F32), cells, cells], heads * AROUND * CELLS,
        in_specs=[vmem, hbm, hbm],
        scratch_shapes=[*spread, pltpu.SemaphoreType.DMA((2,))],
    )

    lon_even, lon_odd, table = barrier((lon_even, lon_odd, table))
    joined, = call(join_kernel, "join", [lon_even, lon_odd], [corner], int(2e9))
    corner_even = pair_exchange(joined, "lat", 0, False)
    corner_odd = odd_rows_exchange(joined)

    def scored(rows):
        return [arr((pairs, rows, 2 * CELLS), F32)] * 2 + [arr((pairs, 8, 2 * CELLS), F32)]

    near = [k, v, lon_odd, lon_even, lat_even, lat_odd]
    raised, prob, near_stats = call(near_kernel, "near", [q, g, *near, corner_even, table], scored(EARLY), 4 * work * EARLY)
    late_q, late_g, _ = barrier((q, g, joined))
    queries_even, queries_odd = call(rows_kernel, "query_rows", [late_q, late_g], [band, band])
    band_table, = call(
        band_bias_kernel, "band_table", [rel_bias, queries_odd], [arr((2, heads, LAT_AT, CELLS), F32)],
        2 * heads * LAT_AT * CELLS,
        scratch_shapes=spread,
    )
    table, band_table = barrier((table, band_table))
    queries_even = pair_exchange(queries_even, "lat", 0, False)
    queries_odd = odd_rows_exchange(queries_odd)
    lines = arr((4 * pairs, LANES), F32)
    corner_raised, corner_prob, stats, lines_even, lines_odd = call(
        corner_kernel, "corner", [q, g, corner_odd, table, near_stats],
        scored(AROUND - EARLY) + [lines, arr((2 * lines.shape[0], LANES), F32)], 4 * work * (AROUND - EARLY),
        scratch_shapes=[pltpu.VMEM(lines.shape, F32)],
    )
    lines_even = pair_exchange(lines_even, "lat", 0, False)
    lines_odd = pair_exchange(lines_odd, "lat", 1, True)
    band_scores = [arr((pairs, 2 * SIDE, 4 * CELLS), F32)] * 2
    masked = [arr((pairs, 4 * CELLS, PAIR), BF16)] * 2
    dlon, side_scores, side_prob, band_q, band_g = call(
        side_scores_kernel, "side_scores",
        [q, g, raised, prob, stats, lon_odd, lon_even, queries_even, queries_odd, band_table],
        [arr(corner.shape, F32), *band_scores, *masked], 16 * work * SIDE,
    )
    dlon, = call(
        side_even_kernel, "side_even", [dlon, side_scores, side_prob, band_q, band_g, lines_even],
        [arr(corner.shape, F32)], 8 * work * SIDE,
    )
    lines_odd, dlon = barrier((lines_odd, dlon))
    send_odd, send_even = call(
        side_band_kernel, "side_band", [dlon, side_scores, side_prob, band_q, band_g, lines_odd], [side, side],
        8 * work * SIDE,
    )
    side_even = pair_exchange(send_even, "lon", 0, True)
    side_odd = pair_exchange(send_odd, "lon", 1, True)
    out, dq, own = call(
        own_kernel, "own", [q, g, *near, corner_even, corner_odd, raised, prob, corner_raised, corner_prob, stats],
        [cells, cells, arr((2, CELLS, feat), F32)], 4 * work * AROUND,
    )
    total, = call(
        own_band_kernel, "own_band", [k, v, band_q, band_g, band_table, lines_even, lines_odd, own],
        [arr((2, CELLS, feat), F32)], 8 * work * CELLS,
    )
    blended, = call(blend_kernel, "blend", [total, side_even], [arr((2, CELLS, feat), F32)])
    dk, dv = call(final_kernel, "final", [blended, side_odd], [cells, cells])
    return tuple(x.reshape(block) for x in (out, dq, dk, dv))


def solution(mesh):
    spec = P("lat", "lon", None)
    return jax.shard_map(
        shards, mesh=mesh, in_specs=(spec, spec, spec, spec, P()), out_specs=(spec,) * 4, check_vma=False
    )
```

```python
import functools

import jax
import jax.numpy as jnp
from jax import lax
from jax.experimental import pallas as pl
from jax.experimental.pallas import tpu as pltpu
from jax.sharding import PartitionSpec as P

HEAD_DIM = 64
RADIUS = 6
SPAN = 2 * RADIUS + 1
ROWS = 8
COLS = 16
CELLS = ROWS * COLS
SIDE = ROWS * RADIUS
BAND = RADIUS * COLS
PAIR = 2 * HEAD_DIM
BASE = 336
TABLE = 512
MASKED = -1e30

OWN_AT = 0
LON_AT = CELLS
LAT_AT = LON_AT + 2 * SIDE
NEAR = LAT_AT + 2 * BAND
EARLY = NEAR + 2 * SIDE
AROUND = EARLY + 2 * SIDE
LANES = 128

F32 = jnp.float32
BF16 = jnp.bfloat16


def pair_exchange(value, axis, odd, wrap):
    count = lax.axis_size(axis)
    pairs = []
    for first in range(odd, count, 2):
        second = first + 1
        if second >= count and not wrap:
            continue
        second %= count
        pairs += [(first, second), (second, first)]
    return lax.ppermute(value, axis, pairs)


def odd_rows_exchange(value):
    lats, lons = lax.axis_size("lat"), lax.axis_size("lon")
    pairs = []
    for lat in range(lats):
        for lon in range(lons):
            other = lat + 1 if lat % 2 else lat - 1
            inside = 0 <= other < lats
            target = (other, lon) if inside else (lat, lon ^ (1 if lons % 4 else 2))
            pairs.append((lat * lons + lon, target[0] * lons + target[1]))
    return lax.ppermute(value, ("lat", "lon"), pairs)


def is_odd(axis):
    return lax.axis_index(axis) % 2 == 1


def pick_matrix(first_col):
    shape = (SIDE, CELLS)
    place = lax.broadcasted_iota(jnp.int32, shape, 0)
    cell = lax.broadcasted_iota(jnp.int32, shape, 1)
    source = (place % ROWS) * COLS + first_col + place // ROWS
    return (cell == source).astype(BF16)


def pack_kernel(k_hbm, v_hbm, bias_hbm, lon_odd_ref, lon_even_ref, k_ref, v_ref, bias_ref, sems):
    copies = [
        pltpu.make_async_copy(source, target, sems.at[index])
        for index, (source, target) in enumerate(((k_hbm, k_ref), (v_hbm, v_ref), (bias_hbm, bias_ref)))
    ]
    for copy in copies:
        copy.start()
    lon_odd = is_odd("lon")
    first_cols = (jnp.where(lon_odd, COLS - RADIUS, 0), jnp.where(lon_odd, 0, COLS - RADIUS))
    picks = jnp.concatenate([pick_matrix(first_col) for first_col in first_cols], axis=0)
    for slot, source in ((0, k_ref), (1, v_ref)):
        copies[slot].wait()
        both = jnp.dot(picks, source[...], preferred_element_type=F32).astype(BF16)
        lon_odd_ref[slot] = both[:SIDE]
        lon_even_ref[slot] = both[SIDE:]
    copies[2].wait()


def lat_starts():
    lat_odd = is_odd("lat")
    even = jnp.where(lat_odd, 0, CELLS - BAND)
    return pl.multiple_of(even, 32), pl.multiple_of(CELLS - BAND - even, 32)


def rows_kernel(k_ref, v_ref, lat_even_ref, lat_odd_ref):
    for start, out in zip(lat_starts(), (lat_even_ref, lat_odd_ref)):
        out[0] = k_ref[pl.ds(start, BAND), :]
        out[1] = v_ref[pl.ds(start, BAND), :]


def bias_lines(bias_ref, line_ref):
    offset = BASE - lax.broadcasted_iota(jnp.int32, (1, TABLE), 1)
    row, col = offset // COLS, offset % COLS
    valid = (offset >= 0) & (row < SPAN) & (col < SPAN)
    entry = lax.broadcasted_iota(jnp.int32, (SPAN * SPAN, TABLE), 0)
    chosen = jnp.where(entry == jnp.where(valid, row * SPAN + col, -1), 1.0, 0.0).astype(BF16)
    rest = bias_ref[...]
    total = jnp.zeros((rest.shape[0], TABLE), F32)
    for _ in range(3):
        part = rest.astype(BF16)
        total = total + jnp.dot(part, chosen, preferred_element_type=F32)
        rest = rest - part.astype(F32)
    line_ref[...] = jnp.where(valid, total, MASKED)


def spread_rows(line_ref, spread_ref):
    heads = line_ref.shape[0]
    lines = [jnp.broadcast_to(line_ref[head : head + 1], (8, TABLE)) for head in range(heads)]
    x = jnp.concatenate(lines, axis=0)
    sub = lax.broadcasted_iota(jnp.int32, x.shape, 0)
    for index, stride in enumerate((1, COLS)):
        turned = x
        for bit in (1, 2, 4):
            turned = jnp.where((sub & bit) != 0, pltpu.roll(turned, bit * stride, 1), turned)
        for head in range(heads):
            spread_ref[index, head] = turned[8 * head : 8 * head + 8]


def windows(source, col, rows):
    firsts = [BASE - (COLS * row + col) for row in rows]
    turn = firsts[0] % LANES
    turned = pltpu.roll(source, TABLE - turn, 1) if turn else source
    return [turned[:, first - turn : first - turn + CELLS] for first in firsts]


def near(delta, there=None):
    allowed = (delta >= 0) & (delta < SPAN)
    return allowed if there is None else allowed & there


def places():
    west_slot = jnp.where(is_odd("lon"), SIDE, 0)
    north_slot = jnp.where(is_odd("lat"), 0, 1)
    has_north = lax.axis_index("lat") > 0
    has_south = lax.axis_index("lat") < lax.axis_size("lat") - 1
    sides = ((0, west_slot), (COLS + RADIUS, SIDE - west_slot))
    own_col = lax.broadcasted_iota(jnp.int32, (8, CELLS), 1) % COLS
    sub = lax.broadcasted_iota(jnp.int32, (8, CELLS), 0)
    return sides, north_slot, 1 - north_slot, has_north, has_south, own_col, sub


def bias_kernel(bias_ref, q_hbm, g_hbm, table_ref, q_ref, g_ref, line_ref, spread_ref, sems):
    copies = [
        pltpu.make_async_copy(source, target, sems.at[index])
        for index, (source, target) in enumerate(((q_hbm, q_ref), (g_hbm, g_ref)))
    ]
    for copy in copies:
        copy.start()
    bias_lines(bias_ref, line_ref)
    spread_rows(line_ref, spread_ref)
    sides, north_slot, south_slot, has_north, has_south, own_col, sub = places()

    def fill(head, carry):
        def put(at, values, allowed):
            table_ref[head, pl.ds(pl.multiple_of(at, 8), 8), :] = jnp.where(allowed, values, MASKED)

        by_one = spread_ref[0, head]
        for half in range(COLS // 8):
            delta = RADIUS + 8 * half + sub - own_col
            own, north, south = near(delta), near(delta, has_north), near(delta, has_south)
            for step in range(8):
                rows = [row for row in (step, step + 8, step + 16) if row < 2 * RADIUS + ROWS]
                for row, values in zip(rows, windows(by_one, RADIUS + 8 * half, rows)):
                    if row < RADIUS:
                        put(LAT_AT + north_slot * BAND + row * COLS + 8 * half, values, north)
                    elif row < RADIUS + ROWS:
                        put(OWN_AT + (row - RADIUS) * COLS + 8 * half, values, own)
                    else:
                        put(LAT_AT + south_slot * BAND + (row - RADIUS - ROWS) * COLS + 8 * half, values, south)
        by_row = spread_ref[1, head]
        rows = (RADIUS - ROWS, RADIUS, RADIUS + ROWS)
        for first_col, lon_slot in sides:
            for step in range(RADIUS):
                delta = first_col + step - own_col
                above, beside, below = windows(by_row, first_col + step, rows)
                at = lon_slot + step * ROWS
                put(LON_AT + at, beside, near(delta))
                put(NEAR + north_slot * 2 * SIDE + at, above, near(delta, has_north))
                put(NEAR + south_slot * 2 * SIDE + at, below, near(delta, has_south))
        return carry

    lax.fori_loop(0, bias_ref.shape[0], fill, 0, unroll=4)
    for copy in copies:
        copy.wait()


def band_bias_kernel(bias_ref, after_ref, table_ref, line_ref, spread_ref):
    del after_ref
    bias_lines(bias_ref, line_ref)
    spread_rows(line_ref, spread_ref)
    sides, north_slot, south_slot, has_north, has_south, own_col, sub = places()
    lane = lax.broadcasted_iota(jnp.int32, (8, CELLS), 1)
    bands = ((north_slot, RADIUS, has_north & (lane < BAND)), (south_slot, -ROWS, has_south & (lane < BAND)))

    def fill(head, carry):
        def put(slot, at, values, allowed):
            table_ref[slot, head, pl.ds(pl.multiple_of(at, 8), 8), :] = jnp.where(allowed, values, MASKED)

        by_one = spread_ref[0, head]
        for half in range(COLS // 8):
            delta = RADIUS + 8 * half + sub - own_col
            masks = [near(delta, there) for _, _, there in bands]
            for step in range(ROWS):
                rows = [next(row for row in range(ROWS) if (RADIUS + row + shift - step) % 8 == 0) for _, shift, _ in bands]
                found = windows(by_one, RADIUS + 8 * half, [RADIUS + row + band[1] for row, band in zip(rows, bands)])
                for row, band, mask, values in zip(rows, bands, masks, found):
                    put(band[0], OWN_AT + row * COLS + 8 * half, values, mask)
        by_row = spread_ref[1, head]
        for slot, shift, there in bands:
            for first_col, lon_slot in sides:
                for step in range(RADIUS):
                    (values,) = windows(by_row, first_col + step, (RADIUS + shift,))
                    put(slot, LON_AT + lon_slot + step * ROWS, values, near(first_col + step - own_col, there))
        return carry

    lax.fori_loop(0, bias_ref.shape[0], fill, 0, unroll=8)


LAST = (((1,), (1,)), ((), ()))
FACTOR = HEAD_DIM ** (-0.5)


def join_kernel(lon_even_ref, lon_odd_ref, out_ref):
    out_ref[:, :SIDE] = lon_odd_ref[...]
    out_ref[:, SIDE:] = lon_even_ref[...]


def over_pairs(width, body):
    return [body(pair, pl.ds(pair * PAIR, PAIR)) for pair in range(width // PAIR)]


def stacked(slot, at, own_ref, *refs):
    return jnp.concatenate([own_ref[:, at]] + [ref[slot, :, at] for ref in refs], axis=0)


def both_heads(block):
    first_head = lax.broadcasted_iota(jnp.int32, block.shape, 1) < HEAD_DIM
    zero = jnp.zeros_like(block)
    return jnp.concatenate([jnp.where(first_head, block, zero), jnp.where(first_head, zero, block)], axis=0)


def scaled(block):
    return both_heads(block * jnp.asarray(FACTOR, BF16))


def two_tables(table_ref, pair, rows):
    return jnp.concatenate([table_ref[2 * pair, rows], table_ref[2 * pair + 1, rows]], axis=1)


def times(left, right):
    return lax.dot_general(left, right, LAST, preferred_element_type=F32)


def column_sum(x):
    return jnp.sum(x, axis=0, keepdims=True)


def rounded_dot(probability, grad_prob):
    return column_sum(probability.astype(BF16).astype(F32) * grad_prob)


def score_gradient(probability, grad_prob, row_dot):
    return probability.astype(BF16), (probability * (grad_prob - row_dot)).astype(BF16)


def near_kernel(
    q_ref, g_ref, k_ref, v_ref, lon_odd_ref, lon_even_ref, lat_even_ref, lat_odd_ref, corner_even_ref, table_ref,
    raised_ref, prob_ref, stats_ref,
):
    parts = (lon_odd_ref, lon_even_ref, lat_even_ref, lat_odd_ref, corner_even_ref)

    def body(pair, at):
        scores = times(stacked(0, at, k_ref, *parts), scaled(q_ref[:, at])) + two_tables(table_ref, pair, pl.ds(0, EARLY))
        grad_prob = times(stacked(1, at, v_ref, *parts), both_heads(g_ref[:, at]))
        largest = jnp.max(scores, axis=0, keepdims=True)
        raised = jnp.exp(scores - largest)
        total = column_sum(raised)
        raised_ref[pair] = raised
        prob_ref[pair] = grad_prob
        stats_ref[pair, 0:1] = largest
        stats_ref[pair, 1:2] = total
        log_total = largest + jnp.log(total)
        stats_ref[pair, 2:3] = rounded_dot(raised * jnp.exp(largest - log_total), grad_prob)
        stats_ref[pair, 3:4] = log_total

    over_pairs(q_ref.shape[1], body)


def corner_kernel(
    q_ref, g_ref, corner_ref, table_ref, near_stats_ref, raised_ref, prob_ref, stats_ref, send_even_ref, send_odd_ref, lines_ref
):
    def score(pair, at):
        scores = times(corner_ref[0, :, at], scaled(q_ref[:, at])) + two_tables(table_ref, pair, pl.ds(EARLY, AROUND - EARLY))
        return scores, times(corner_ref[1, :, at], both_heads(g_ref[:, at]))

    scored = over_pairs(q_ref.shape[1], score)
    for pair, (scores, grad_prob) in enumerate(scored):
        near_largest = near_stats_ref[pair, 0:1]
        largest = jnp.maximum(near_largest, jnp.max(scores, axis=0, keepdims=True))
        raised = jnp.exp(scores - largest)
        shift = jnp.exp(near_largest - largest)
        total = near_stats_ref[pair, 1:2] * shift + column_sum(raised)
        log_total = largest + jnp.log(total)
        scale = jnp.exp(largest - log_total)
        near_scale = jnp.exp(near_largest - log_total)
        row_dot = near_stats_ref[pair, 2:3] * jnp.exp(near_stats_ref[pair, 3:4] - log_total)
        row_dot = row_dot + rounded_dot(raised * scale, grad_prob)
        raised_ref[pair] = raised
        prob_ref[pair] = grad_prob
        stats_ref[pair, 0:1] = near_scale
        stats_ref[pair, 1:2] = row_dot
        stats_ref[pair, 2:3] = scale
        for index, line in enumerate((log_total, row_dot)):
            for head in (0, 1):
                at = 4 * pair + 2 * index + head
                lines_ref[at : at + 1] = line[:, head * CELLS : (head + 1) * CELLS]
    lines = lines_ref[...]
    low_rows = pltpu.roll(lines, BAND, 1)
    lat_odd = is_odd("lat")
    send_even_ref[...] = jnp.where(lat_odd, lines, low_rows)
    odd_lines = jnp.where(lat_odd, low_rows, lines)
    send_odd_ref[...] = jnp.concatenate([odd_lines] * (send_odd_ref.shape[0] // lines.shape[0]), axis=0)


def near_gradient(raised_ref, prob_ref, stats_ref, pair, rows):
    return score_gradient(raised_ref[pair, rows] * stats_ref[pair, 0:1], prob_ref[pair, rows], stats_ref[pair, 1:2])


def band_lines(lines_refs, pair):
    def row(first):
        return jnp.concatenate([ref[line : line + 1] for ref in lines_refs for line in (first, first + 1)], axis=1)

    return row(4 * pair), row(4 * pair + 2)


def band_queries(queries_refs, slot, at, prepare):
    empty = jnp.zeros((CELLS - BAND, PAIR), BF16)
    return jnp.concatenate([prepare(jnp.concatenate([ref[slot, :, at], empty], axis=0)) for ref in queries_refs], axis=0)


def band_tables(table_ref, pair, rows):
    return jnp.concatenate([table_ref[slot, 2 * pair + head, rows] for slot in (0, 1) for head in (0, 1)], axis=1)


def side_scores_kernel(
    q_ref, g_ref, raised_ref, prob_ref, stats_ref, lon_odd_ref, lon_even_ref, queries_even_ref, queries_odd_ref, table_ref,
    dlon_ref, scores_ref, prob_out_ref, band_q_ref, band_g_ref,
):
    queries_refs = (queries_even_ref, queries_odd_ref)

    def body(pair, at):
        keys, values = (
            jnp.concatenate([lon_odd_ref[slot, :, at], lon_even_ref[slot, :, at]], axis=0) for slot in (0, 1)
        )
        queries = band_queries(queries_refs, 0, at, scaled)
        grads = band_queries(queries_refs, 1, at, both_heads)
        band_q_ref[pair] = queries
        band_g_ref[pair] = grads
        scores_ref[pair] = times(keys, queries) + band_tables(table_ref, pair, pl.ds(LON_AT, 2 * SIDE))
        prob_out_ref[pair] = times(values, grads)
        weights, dscore = near_gradient(raised_ref, prob_ref, stats_ref, pair, pl.ds(LON_AT, LAT_AT - LON_AT))
        dlon_ref[0, :, at] = jnp.dot(dscore, scaled(q_ref[:, at]), preferred_element_type=F32)
        dlon_ref[1, :, at] = jnp.dot(weights, both_heads(g_ref[:, at]), preferred_element_type=F32)

    over_pairs(q_ref.shape[1], body)


def side_terms(pair, at, lanes, scores_ref, prob_ref, lines_ref, band_q_ref, band_g_ref):
    log_total, row_dot = band_lines((lines_ref,), pair)
    weights, dscore = score_gradient(
        jnp.exp(scores_ref[pair, :, lanes] - log_total), prob_ref[pair, :, lanes], row_dot
    )
    return [
        jnp.dot(coefficients, other[pair, lanes], preferred_element_type=F32)
        for coefficients, other in ((dscore, band_q_ref), (weights, band_g_ref))
    ]


def side_even_kernel(dlon_ref, scores_ref, prob_ref, band_q_ref, band_g_ref, lines_ref, sum_ref):
    def body(pair, at):
        terms = side_terms(pair, at, pl.ds(0, 2 * CELLS), scores_ref, prob_ref, lines_ref, band_q_ref, band_g_ref)
        for slot, term in enumerate(terms):
            sum_ref[slot, :, at] = dlon_ref[slot, :, at] + term

    over_pairs(dlon_ref.shape[2], body)


def side_band_kernel(
    sum_ref, scores_ref, prob_ref, band_q_ref, band_g_ref, lines_ref, send_odd_ref, send_even_ref
):
    def body(pair, at):
        return side_terms(
            pair, at, pl.ds(2 * CELLS, 2 * CELLS), scores_ref, prob_ref, lines_ref, band_q_ref, band_g_ref
        )

    for pair, terms in enumerate(over_pairs(sum_ref.shape[2], body)):
        at = pl.ds(pair * PAIR, PAIR)
        for slot, term in enumerate(terms):
            total = (sum_ref[slot, :, at] + term).astype(BF16)
            send_odd_ref[slot, :, at] = total[:SIDE]
            send_even_ref[slot, :, at] = total[SIDE:]


def own_kernel(
    q_ref, g_ref, k_ref, v_ref, lon_odd_ref, lon_even_ref, lat_even_ref, lat_odd_ref, corner_even_ref, corner_odd_ref,
    raised_ref, prob_ref, corner_raised_ref, corner_prob_ref, stats_ref, out_ref, dq_ref, own_ref,
):
    parts = (lon_odd_ref, lon_even_ref, lat_even_ref, lat_odd_ref, corner_even_ref, corner_odd_ref)

    def per_query(cells, coefficients):
        turned = jnp.dot(cells.T, coefficients, preferred_element_type=F32)
        mine = jnp.concatenate([turned[:HEAD_DIM, :CELLS], turned[HEAD_DIM:, CELLS:]], axis=0)
        return mine.T

    def body(pair, at):
        nearby = near_gradient(raised_ref, prob_ref, stats_ref, pair, pl.ds(0, EARLY))
        far = score_gradient(
            corner_raised_ref[pair] * stats_ref[pair, 2:3], corner_prob_ref[pair], stats_ref[pair, 1:2]
        )
        weights, dscore = (jnp.concatenate(x, axis=0) for x in zip(nearby, far))
        own_ref[0, :, at] = jnp.dot(dscore[:LON_AT], scaled(q_ref[:, at]), preferred_element_type=F32)
        own_ref[1, :, at] = jnp.dot(weights[:LON_AT], both_heads(g_ref[:, at]), preferred_element_type=F32)
        out_ref[:, at] = per_query(stacked(1, at, v_ref, *parts), weights).astype(BF16)
        dq_ref[:, at] = (per_query(stacked(0, at, k_ref, *parts), dscore) * FACTOR).astype(BF16)

    over_pairs(q_ref.shape[1], body)


def own_band_kernel(
    k_ref, v_ref, band_q_ref, band_g_ref, table_ref, lines_even_ref, lines_odd_ref, own_ref, total_ref
):
    def score(pair, at):
        log_total, row_dot = band_lines((lines_even_ref, lines_odd_ref), pair)
        scores = times(k_ref[:, at], band_q_ref[pair]) + band_tables(table_ref, pair, pl.ds(OWN_AT, CELLS))
        return score_gradient(jnp.exp(scores - log_total), times(v_ref[:, at], band_g_ref[pair]), row_dot)

    scored = over_pairs(k_ref.shape[1], score)

    def finish(pair, at):
        weights, dscore = scored[pair]
        for slot, coefficients, other in ((0, dscore, band_q_ref), (1, weights, band_g_ref)):
            grad = jnp.dot(coefficients, other[pair], preferred_element_type=F32)
            total_ref[slot, :, at] = own_ref[slot, :, at] + grad

    over_pairs(k_ref.shape[1], finish)


def spread_matrix(first_col):
    shape = (CELLS, SIDE)
    cell = lax.broadcasted_iota(jnp.int32, shape, 0)
    place = lax.broadcasted_iota(jnp.int32, shape, 1)
    return (cell == (place % ROWS) * COLS + first_col + place // ROWS).astype(BF16)


def blend_kernel(total_ref, side_even_ref, blended_ref):
    spread = spread_matrix(jnp.where(is_odd("lon"), 0, COLS - RADIUS))
    for slot in (0, 1):
        blended_ref[slot] = total_ref[slot] + jnp.dot(spread, side_even_ref[slot], preferred_element_type=F32)


def final_kernel(blended_ref, side_odd_ref, dk_ref, dv_ref):
    spread = spread_matrix(jnp.where(is_odd("lon"), COLS - RADIUS, 0))
    for slot, out in ((0, dk_ref), (1, dv_ref)):
        total = blended_ref[slot] + jnp.dot(spread, side_odd_ref[slot], preferred_element_type=F32)
        out[...] = total.astype(BF16)


def arr(shape, dtype):
    return jax.ShapeDtypeStruct(shape, dtype)


def call(kernel, name, operands, results, flops=0, **more):
    moved = sum(x.size * x.dtype.itemsize for x in operands)
    return pl.pallas_call(
        kernel,
        out_shape=results,
        compiler_params=pltpu.CompilerParams(vmem_limit_bytes=32 * 1024 * 1024),
        cost_estimate=pl.CostEstimate(flops=flops, bytes_accessed=moved, transcendentals=0),
        name=name,
        **more,
    )(*operands)


def shards(queries, key_cells, value_cells, grad_output, rel_bias):
    block = queries.shape
    heads = rel_bias.shape[0]
    feat = block[-1]
    pairs = feat // PAIR
    cells = arr((CELLS, feat), BF16)
    side, band, corner = (arr((2, rows, feat), BF16) for rows in (SIDE, BAND, 2 * SIDE))
    work = 2 * CELLS * feat
    barrier = lax.optimization_barrier

    def in_hbm(x):
        return pltpu.with_memory_space_constraint(x, pltpu.HBM)

    hbm, vmem = (pl.BlockSpec(memory_space=space) for space in (pltpu.HBM, pltpu.VMEM))
    arguments = [in_hbm(x) for x in (key_cells.reshape(CELLS, feat), value_cells.reshape(CELLS, feat), rel_bias)]
    lon_odd, lon_even, k, v, rel_bias = call(
        pack_kernel, "pack", arguments, [side, side, cells, cells, arr(rel_bias.shape, F32)],
        in_specs=[hbm] * 3,
        scratch_shapes=[pltpu.SemaphoreType.DMA((3,))],
    )
    lon_even = pair_exchange(lon_even, "lon", 0, True)
    lon_odd = pair_exchange(lon_odd, "lon", 1, True)
    lat_even, lat_odd = call(rows_kernel, "rows", [k, v], [band, band])
    lat_even = pair_exchange(lat_even, "lat", 0, False)
    lat_odd = pair_exchange(lat_odd, "lat", 1, True)

    spread = [pltpu.VMEM((heads, TABLE), F32), pltpu.VMEM((2, heads, 8, TABLE), F32)]
    table, q, g = call(
        bias_kernel, "bias_table",
        [rel_bias, in_hbm(queries.reshape(CELLS, feat)), in_hbm(grad_output.reshape(CELLS, feat))],
        [arr((heads, AROUND, CELLS), F32), cells, cells], heads * AROUND * CELLS,
        in_specs=[vmem, hbm, hbm],
        scratch_shapes=[*spread, pltpu.SemaphoreType.DMA((2,))],
    )

    lon_even, lon_odd, table = barrier((lon_even, lon_odd, table))
    joined, = call(join_kernel, "join", [lon_even, lon_odd], [corner], int(2e9))
    corner_even = pair_exchange(joined, "lat", 0, False)
    corner_odd = odd_rows_exchange(joined)

    def scored(rows):
        return [arr((pairs, rows, 2 * CELLS), F32)] * 2 + [arr((pairs, 8, 2 * CELLS), F32)]

    near = [k, v, lon_odd, lon_even, lat_even, lat_odd]
    raised, prob, near_stats = call(near_kernel, "near", [q, g, *near, corner_even, table], scored(EARLY), 4 * work * EARLY)
    late_q, late_g, _ = barrier((q, g, joined))
    queries_even, queries_odd = call(rows_kernel, "query_rows", [late_q, late_g], [band, band])
    band_table, = call(
        band_bias_kernel, "band_table", [rel_bias, queries_odd], [arr((2, heads, LAT_AT, CELLS), F32)],
        2 * heads * LAT_AT * CELLS,
        scratch_shapes=spread,
    )
    table, band_table = barrier((table, band_table))
    queries_even = pair_exchange(queries_even, "lat", 0, False)
    queries_odd = odd_rows_exchange(queries_odd)
    lines = arr((4 * pairs, LANES), F32)
    corner_raised, corner_prob, stats, lines_even, lines_odd = call(
        corner_kernel, "corner", [q, g, corner_odd, table, near_stats],
        scored(AROUND - EARLY) + [lines, arr((2 * lines.shape[0], LANES), F32)], 4 * work * (AROUND - EARLY),
        scratch_shapes=[pltpu.VMEM(lines.shape, F32)],
    )
    lines_even = pair_exchange(lines_even, "lat", 0, False)
    lines_odd = pair_exchange(lines_odd, "lat", 1, True)
    band_scores = [arr((pairs, 2 * SIDE, 4 * CELLS), F32)] * 2
    masked = [arr((pairs, 4 * CELLS, PAIR), BF16)] * 2
    dlon, side_scores, side_prob, band_q, band_g = call(
        side_scores_kernel, "side_scores",
        [q, g, raised, prob, stats, lon_odd, lon_even, queries_even, queries_odd, band_table],
        [arr(corner.shape, F32), *band_scores, *masked], 16 * work * SIDE,
    )
    dlon, = call(
        side_even_kernel, "side_even", [dlon, side_scores, side_prob, band_q, band_g, lines_even],
        [arr(corner.shape, F32)], 8 * work * SIDE,
    )
    lines_odd, dlon = barrier((lines_odd, dlon))
    send_odd, send_even = call(
        side_band_kernel, "side_band", [dlon, side_scores, side_prob, band_q, band_g, lines_odd], [side, side],
        8 * work * SIDE,
    )
    side_even = pair_exchange(send_even, "lon", 0, True)
    side_odd = pair_exchange(send_odd, "lon", 1, True)
    out, dq, own = call(
        own_kernel, "own", [q, g, *near, corner_even, corner_odd, raised, prob, corner_raised, corner_prob, stats],
        [cells, cells, arr((2, CELLS, feat), F32)], 4 * work * AROUND,
    )
    total, = call(
        own_band_kernel, "own_band", [k, v, band_q, band_g, band_table, lines_even, lines_odd, own],
        [arr((2, CELLS, feat), F32)], 8 * work * CELLS,
    )
    blended, = call(blend_kernel, "blend", [total, side_even], [arr((2, CELLS, feat), F32)])
    dk, dv = call(final_kernel, "final", [blended, side_odd], [cells, cells])
    return tuple(x.reshape(block) for x in (out, dq, dk, dv))


def solution(mesh):
    spec = P("lat", "lon", None)
    return jax.shard_map(
        shards, mesh=mesh, in_specs=(spec, spec, spec, spec, P()), out_specs=(spec,) * 4, check_vma=False
    )
```

```python
import functools

import jax
import jax.numpy as jnp
from jax import lax
from jax.experimental import pallas as pl
from jax.experimental.pallas import tpu as pltpu
from jax.sharding import PartitionSpec as P

HEAD_DIM = 64
RADIUS = 6
SPAN = 2 * RADIUS + 1
ROWS = 8
COLS = 16
CELLS = ROWS * COLS
SIDE = ROWS * RADIUS
BAND = RADIUS * COLS
PAIR = 2 * HEAD_DIM
BASE = 336
TABLE = 512
MASKED = -1e30

OWN_AT = 0
LON_AT = CELLS
LAT_AT = LON_AT + 2 * SIDE
NEAR = LAT_AT + 2 * BAND
EARLY = NEAR + 2 * SIDE
AROUND = EARLY + 2 * SIDE
LANES = 128

F32 = jnp.float32
BF16 = jnp.bfloat16


def pair_exchange(value, axis, odd, wrap):
    count = lax.axis_size(axis)
    pairs = []
    for first in range(odd, count, 2):
        second = first + 1
        if second >= count and not wrap:
            continue
        second %= count
        pairs += [(first, second), (second, first)]
    return lax.ppermute(value, axis, pairs)


def ring_shift(value, by):
    count = lax.axis_size("lon")
    return lax.ppermute(value, "lon", [(lon, (lon + by) % count) for lon in range(count)])


def odd_rows_exchange(value):
    lats, lons = lax.axis_size("lat"), lax.axis_size("lon")
    pairs = []
    for lat in range(lats):
        for lon in range(lons):
            other = lat + 1 if lat % 2 else lat - 1
            inside = 0 <= other < lats
            target = (other, lon) if inside else (lat, lon ^ (1 if lons % 4 else 2))
            pairs.append((lat * lons + lon, target[0] * lons + target[1]))
    return lax.ppermute(value, ("lat", "lon"), pairs)


def is_odd(axis):
    return lax.axis_index(axis) % 2 == 1


def pick_matrix(first_col):
    shape = (SIDE, CELLS)
    place = lax.broadcasted_iota(jnp.int32, shape, 0)
    cell = lax.broadcasted_iota(jnp.int32, shape, 1)
    source = (place % ROWS) * COLS + first_col + place // ROWS
    return (cell == source).astype(BF16)


def pack_kernel(k_hbm, v_hbm, bias_hbm, lon_west_ref, lon_east_ref, k_ref, v_ref, bias_ref, sems):
    copies = [
        pltpu.make_async_copy(source, target, sems.at[index])
        for index, (source, target) in enumerate(((k_hbm, k_ref), (v_hbm, v_ref), (bias_hbm, bias_ref)))
    ]
    for copy in copies:
        copy.start()
    picks = jnp.concatenate([pick_matrix(first_col) for first_col in (COLS - RADIUS, 0)], axis=0)
    for slot, source in ((0, k_ref), (1, v_ref)):
        copies[slot].wait()
        both = jnp.dot(picks, source[...], preferred_element_type=F32).astype(BF16)
        lon_west_ref[slot] = both[:SIDE]
        lon_east_ref[slot] = both[SIDE:]
    copies[2].wait()


def lat_starts():
    lat_odd = is_odd("lat")
    even = jnp.where(lat_odd, 0, CELLS - BAND)
    return pl.multiple_of(even, 32), pl.multiple_of(CELLS - BAND - even, 32)


def rows_kernel(k_ref, v_ref, lat_even_ref, lat_odd_ref):
    for start, out in zip(lat_starts(), (lat_even_ref, lat_odd_ref)):
        out[0] = k_ref[pl.ds(start, BAND), :]
        out[1] = v_ref[pl.ds(start, BAND), :]


def bias_lines(bias_ref, line_ref):
    offset = BASE - lax.broadcasted_iota(jnp.int32, (1, TABLE), 1)
    row, col = offset // COLS, offset % COLS
    valid = (offset >= 0) & (row < SPAN) & (col < SPAN)
    entry = lax.broadcasted_iota(jnp.int32, (SPAN * SPAN, TABLE), 0)
    chosen = jnp.where(entry == jnp.where(valid, row * SPAN + col, -1), 1.0, 0.0).astype(BF16)
    rest = bias_ref[...]
    total = jnp.zeros((rest.shape[0], TABLE), F32)
    for _ in range(3):
        part = rest.astype(BF16)
        total = total + jnp.dot(part, chosen, preferred_element_type=F32)
        rest = rest - part.astype(F32)
    line_ref[...] = jnp.where(valid, total, MASKED)


def spread_rows(line_ref, spread_ref):
    heads = line_ref.shape[0]
    lines = [jnp.broadcast_to(line_ref[head : head + 1], (8, TABLE)) for head in range(heads)]
    x = jnp.concatenate(lines, axis=0)
    sub = lax.broadcasted_iota(jnp.int32, x.shape, 0)
    for index, stride in enumerate((1, COLS)):
        turned = x
        for bit in (1, 2, 4):
            turned = jnp.where((sub & bit) != 0, pltpu.roll(turned, bit * stride, 1), turned)
        for head in range(heads):
            spread_ref[index, head] = turned[8 * head : 8 * head + 8]


def windows(source, col, rows):
    firsts = [BASE - (COLS * row + col) for row in rows]
    turn = firsts[0] % LANES
    turned = pltpu.roll(source, TABLE - turn, 1) if turn else source
    return [turned[:, first - turn : first - turn + CELLS] for first in firsts]


def near(delta, there=None):
    allowed = (delta >= 0) & (delta < SPAN)
    return allowed if there is None else allowed & there


def places():
    north_slot = jnp.where(is_odd("lat"), 0, 1)
    has_north = lax.axis_index("lat") > 0
    has_south = lax.axis_index("lat") < lax.axis_size("lat") - 1
    sides = ((0, 0), (COLS + RADIUS, SIDE))
    own_col = lax.broadcasted_iota(jnp.int32, (8, CELLS), 1) % COLS
    sub = lax.broadcasted_iota(jnp.int32, (8, CELLS), 0)
    return sides, north_slot, 1 - north_slot, has_north, has_south, own_col, sub


def bias_kernel(bias_ref, q_hbm, g_hbm, table_ref, q_ref, g_ref, line_ref, spread_ref, sems):
    copies = [
        pltpu.make_async_copy(source, target, sems.at[index])
        for index, (source, target) in enumerate(((q_hbm, q_ref), (g_hbm, g_ref)))
    ]
    for copy in copies:
        copy.start()
    bias_lines(bias_ref, line_ref)
    spread_rows(line_ref, spread_ref)
    sides, north_slot, south_slot, has_north, has_south, own_col, sub = places()

    def fill(head, carry):
        def put(at, values, allowed):
            table_ref[head, pl.ds(pl.multiple_of(at, 8), 8), :] = jnp.where(allowed, values, MASKED)

        by_one = spread_ref[0, head]
        for half in range(COLS // 8):
            delta = RADIUS + 8 * half + sub - own_col
            own, north, south = near(delta), near(delta, has_north), near(delta, has_south)
            for step in range(8):
                rows = [row for row in (step, step + 8, step + 16) if row < 2 * RADIUS + ROWS]
                for row, values in zip(rows, windows(by_one, RADIUS + 8 * half, rows)):
                    if row < RADIUS:
                        put(LAT_AT + north_slot * BAND + row * COLS + 8 * half, values, north)
                    elif row < RADIUS + ROWS:
                        put(OWN_AT + (row - RADIUS) * COLS + 8 * half, values, own)
                    else:
                        put(LAT_AT + south_slot * BAND + (row - RADIUS - ROWS) * COLS + 8 * half, values, south)
        by_row = spread_ref[1, head]
        rows = (RADIUS - ROWS, RADIUS, RADIUS + ROWS)
        for first_col, lon_slot in sides:
            for step in range(RADIUS):
                delta = first_col + step - own_col
                above, beside, below = windows(by_row, first_col + step, rows)
                at = lon_slot + step * ROWS
                put(LON_AT + at, beside, near(delta))
                put(NEAR + north_slot * 2 * SIDE + at, above, near(delta, has_north))
                put(NEAR + south_slot * 2 * SIDE + at, below, near(delta, has_south))
        return carry

    lax.fori_loop(0, bias_ref.shape[0], fill, 0, unroll=4)
    for copy in copies:
        copy.wait()


def band_bias_kernel(bias_ref, after_ref, table_ref, line_ref, spread_ref):
    del after_ref
    bias_lines(bias_ref, line_ref)
    spread_rows(line_ref, spread_ref)
    sides, north_slot, south_slot, has_north, has_south, own_col, sub = places()
    lane = lax.broadcasted_iota(jnp.int32, (8, CELLS), 1)
    bands = ((north_slot, RADIUS, has_north & (lane < BAND)), (south_slot, -ROWS, has_south & (lane < BAND)))

    def fill(head, carry):
        def put(slot, at, values, allowed):
            table_ref[slot, head, pl.ds(pl.multiple_of(at, 8), 8), :] = jnp.where(allowed, values, MASKED)

        by_one = spread_ref[0, head]
        for half in range(COLS // 8):
            delta = RADIUS + 8 * half + sub - own_col
            masks = [near(delta, there) for _, _, there in bands]
            for step in range(ROWS):
                rows = [next(row for row in range(ROWS) if (RADIUS + row + shift - step) % 8 == 0) for _, shift, _ in bands]
                found = windows(by_one, RADIUS + 8 * half, [RADIUS + row + band[1] for row, band in zip(rows, bands)])
                for row, band, mask, values in zip(rows, bands, masks, found):
                    put(band[0], OWN_AT + row * COLS + 8 * half, values, mask)
        by_row = spread_ref[1, head]
        for slot, shift, there in bands:
            for first_col, lon_slot in sides:
                for step in range(RADIUS):
                    (values,) = windows(by_row, first_col + step, (RADIUS + shift,))
                    put(slot, LON_AT + lon_slot + step * ROWS, values, near(first_col + step - own_col, there))
        return carry

    lax.fori_loop(0, bias_ref.shape[0], fill, 0, unroll=8)


LAST = (((1,), (1,)), ((), ()))
FACTOR = HEAD_DIM ** (-0.5)


def join_kernel(lon_west_ref, lon_east_ref, out_ref):
    out_ref[:, :SIDE] = lon_west_ref[...]
    out_ref[:, SIDE:] = lon_east_ref[...]


def over_pairs(width, body):
    return [body(pair, pl.ds(pair * PAIR, PAIR)) for pair in range(width // PAIR)]


def stacked(slot, at, own_ref, *refs):
    return jnp.concatenate([own_ref[:, at]] + [ref[slot, :, at] for ref in refs], axis=0)


def both_heads(block):
    first_head = lax.broadcasted_iota(jnp.int32, block.shape, 1) < HEAD_DIM
    zero = jnp.zeros_like(block)
    return jnp.concatenate([jnp.where(first_head, block, zero), jnp.where(first_head, zero, block)], axis=0)


def scaled(block):
    return both_heads(block * jnp.asarray(FACTOR, BF16))


def two_tables(table_ref, pair, rows):
    return jnp.concatenate([table_ref[2 * pair, rows], table_ref[2 * pair + 1, rows]], axis=1)


def times(left, right):
    return lax.dot_general(left, right, LAST, preferred_element_type=F32)


def column_sum(x):
    return jnp.sum(x, axis=0, keepdims=True)


def rounded_dot(probability, grad_prob):
    return column_sum(probability.astype(BF16).astype(F32) * grad_prob)


def score_gradient(probability, grad_prob, row_dot):
    return probability.astype(BF16), (probability * (grad_prob - row_dot)).astype(BF16)


def near_kernel(
    q_ref, g_ref, k_ref, v_ref, lon_west_ref, lon_east_ref, lat_even_ref, lat_odd_ref, corner_even_ref, table_ref,
    raised_ref, prob_ref, stats_ref,
):
    parts = (lon_west_ref, lon_east_ref, lat_even_ref, lat_odd_ref, corner_even_ref)

    def body(pair, at):
        scores = times(stacked(0, at, k_ref, *parts), scaled(q_ref[:, at])) + two_tables(table_ref, pair, pl.ds(0, EARLY))
        grad_prob = times(stacked(1, at, v_ref, *parts), both_heads(g_ref[:, at]))
        largest = jnp.max(scores, axis=0, keepdims=True)
        raised = jnp.exp(scores - largest)
        total = column_sum(raised)
        raised_ref[pair] = raised
        prob_ref[pair] = grad_prob
        stats_ref[pair, 0:1] = largest
        stats_ref[pair, 1:2] = total
        log_total = largest + jnp.log(total)
        stats_ref[pair, 2:3] = rounded_dot(raised * jnp.exp(largest - log_total), grad_prob)
        stats_ref[pair, 3:4] = log_total

    over_pairs(q_ref.shape[1], body)


def corner_kernel(
    q_ref, g_ref, corner_ref, table_ref, near_stats_ref, raised_ref, prob_ref, stats_ref, send_even_ref, send_odd_ref, lines_ref
):
    def score(pair, at):
        scores = times(corner_ref[0, :, at], scaled(q_ref[:, at])) + two_tables(table_ref, pair, pl.ds(EARLY, AROUND - EARLY))
        return scores, times(corner_ref[1, :, at], both_heads(g_ref[:, at]))

    scored = over_pairs(q_ref.shape[1], score)
    for pair, (scores, grad_prob) in enumerate(scored):
        near_largest = near_stats_ref[pair, 0:1]
        largest = jnp.maximum(near_largest, jnp.max(scores, axis=0, keepdims=True))
        raised = jnp.exp(scores - largest)
        shift = jnp.exp(near_largest - largest)
        total = near_stats_ref[pair, 1:2] * shift + column_sum(raised)
        log_total = largest + jnp.log(total)
        scale = jnp.exp(largest - log_total)
        near_scale = jnp.exp(near_largest - log_total)
        row_dot = near_stats_ref[pair, 2:3] * jnp.exp(near_stats_ref[pair, 3:4] - log_total)
        row_dot = row_dot + rounded_dot(raised * scale, grad_prob)
        raised_ref[pair] = raised
        prob_ref[pair] = grad_prob
        stats_ref[pair, 0:1] = near_scale
        stats_ref[pair, 1:2] = row_dot
        stats_ref[pair, 2:3] = scale
        for index, line in enumerate((log_total, row_dot)):
            for head in (0, 1):
                at = 4 * pair + 2 * index + head
                lines_ref[at : at + 1] = line[:, head * CELLS : (head + 1) * CELLS]
    lines = lines_ref[...]
    low_rows = pltpu.roll(lines, BAND, 1)
    lat_odd = is_odd("lat")
    send_even_ref[...] = jnp.where(lat_odd, lines, low_rows)
    odd_lines = jnp.where(lat_odd, low_rows, lines)
    send_odd_ref[...] = jnp.concatenate([odd_lines] * (send_odd_ref.shape[0] // lines.shape[0]), axis=0)


def near_gradient(raised_ref, prob_ref, stats_ref, pair, rows):
    return score_gradient(raised_ref[pair, rows] * stats_ref[pair, 0:1], prob_ref[pair, rows], stats_ref[pair, 1:2])


def band_lines(lines_refs, pair):
    def row(first):
        return jnp.concatenate([ref[line : line + 1] for ref in lines_refs for line in (first, first + 1)], axis=1)

    return row(4 * pair), row(4 * pair + 2)


def band_queries(queries_refs, slot, at, prepare):
    empty = jnp.zeros((CELLS - BAND, PAIR), BF16)
    return jnp.concatenate([prepare(jnp.concatenate([ref[slot, :, at], empty], axis=0)) for ref in queries_refs], axis=0)


def band_tables(table_ref, pair, rows):
    return jnp.concatenate([table_ref[slot, 2 * pair + head, rows] for slot in (0, 1) for head in (0, 1)], axis=1)


def side_scores_kernel(
    q_ref, g_ref, raised_ref, prob_ref, stats_ref, lon_west_ref, lon_east_ref, queries_even_ref, queries_odd_ref, table_ref,
    dlon_ref, scores_ref, prob_out_ref, band_q_ref, band_g_ref,
):
    queries_refs = (queries_even_ref, queries_odd_ref)

    def body(pair, at):
        keys, values = (
            jnp.concatenate([lon_west_ref[slot, :, at], lon_east_ref[slot, :, at]], axis=0) for slot in (0, 1)
        )
        queries = band_queries(queries_refs, 0, at, scaled)
        grads = band_queries(queries_refs, 1, at, both_heads)
        band_q_ref[pair] = queries
        band_g_ref[pair] = grads
        scores_ref[pair] = times(keys, queries) + band_tables(table_ref, pair, pl.ds(LON_AT, 2 * SIDE))
        prob_out_ref[pair] = times(values, grads)
        weights, dscore = near_gradient(raised_ref, prob_ref, stats_ref, pair, pl.ds(LON_AT, LAT_AT - LON_AT))
        dlon_ref[0, :, at] = jnp.dot(dscore, scaled(q_ref[:, at]), preferred_element_type=F32)
        dlon_ref[1, :, at] = jnp.dot(weights, both_heads(g_ref[:, at]), preferred_element_type=F32)

    over_pairs(q_ref.shape[1], body)


def side_terms(pair, at, lanes, scores_ref, prob_ref, lines_ref, band_q_ref, band_g_ref):
    log_total, row_dot = band_lines((lines_ref,), pair)
    weights, dscore = score_gradient(
        jnp.exp(scores_ref[pair, :, lanes] - log_total), prob_ref[pair, :, lanes], row_dot
    )
    return [
        jnp.dot(coefficients, other[pair, lanes], preferred_element_type=F32)
        for coefficients, other in ((dscore, band_q_ref), (weights, band_g_ref))
    ]


def side_even_kernel(dlon_ref, scores_ref, prob_ref, band_q_ref, band_g_ref, lines_ref, sum_ref):
    def body(pair, at):
        terms = side_terms(pair, at, pl.ds(0, 2 * CELLS), scores_ref, prob_ref, lines_ref, band_q_ref, band_g_ref)
        for slot, term in enumerate(terms):
            sum_ref[slot, :, at] = dlon_ref[slot, :, at] + term

    over_pairs(dlon_ref.shape[2], body)


def side_band_kernel(
    sum_ref, scores_ref, prob_ref, band_q_ref, band_g_ref, lines_ref, send_odd_ref, send_even_ref
):
    def body(pair, at):
        return side_terms(
            pair, at, pl.ds(2 * CELLS, 2 * CELLS), scores_ref, prob_ref, lines_ref, band_q_ref, band_g_ref
        )

    for pair, terms in enumerate(over_pairs(sum_ref.shape[2], body)):
        at = pl.ds(pair * PAIR, PAIR)
        for slot, term in enumerate(terms):
            total = (sum_ref[slot, :, at] + term).astype(BF16)
            send_odd_ref[slot, :, at] = total[:SIDE]
            send_even_ref[slot, :, at] = total[SIDE:]


def own_kernel(
    q_ref, g_ref, k_ref, v_ref, lon_west_ref, lon_east_ref, lat_even_ref, lat_odd_ref, corner_even_ref, corner_odd_ref,
    raised_ref, prob_ref, corner_raised_ref, corner_prob_ref, stats_ref, out_ref, dq_ref, own_ref,
):
    parts = (lon_west_ref, lon_east_ref, lat_even_ref, lat_odd_ref, corner_even_ref, corner_odd_ref)

    def per_query(cells, coefficients):
        turned = jnp.dot(cells.T, coefficients, preferred_element_type=F32)
        mine = jnp.concatenate([turned[:HEAD_DIM, :CELLS], turned[HEAD_DIM:, CELLS:]], axis=0)
        return mine.T

    def body(pair, at):
        nearby = near_gradient(raised_ref, prob_ref, stats_ref, pair, pl.ds(0, EARLY))
        far = score_gradient(
            corner_raised_ref[pair] * stats_ref[pair, 2:3], corner_prob_ref[pair], stats_ref[pair, 1:2]
        )
        weights, dscore = (jnp.concatenate(x, axis=0) for x in zip(nearby, far))
        own_ref[0, :, at] = jnp.dot(dscore[:LON_AT], scaled(q_ref[:, at]), preferred_element_type=F32)
        own_ref[1, :, at] = jnp.dot(weights[:LON_AT], both_heads(g_ref[:, at]), preferred_element_type=F32)
        out_ref[:, at] = per_query(stacked(1, at, v_ref, *parts), weights).astype(BF16)
        dq_ref[:, at] = (per_query(stacked(0, at, k_ref, *parts), dscore) * FACTOR).astype(BF16)

    over_pairs(q_ref.shape[1], body)


def own_band_kernel(
    k_ref, v_ref, band_q_ref, band_g_ref, table_ref, lines_even_ref, lines_odd_ref, own_ref, total_ref
):
    def score(pair, at):
        log_total, row_dot = band_lines((lines_even_ref, lines_odd_ref), pair)
        scores = times(k_ref[:, at], band_q_ref[pair]) + band_tables(table_ref, pair, pl.ds(OWN_AT, CELLS))
        return score_gradient(jnp.exp(scores - log_total), times(v_ref[:, at], band_g_ref[pair]), row_dot)

    scored = over_pairs(k_ref.shape[1], score)

    def finish(pair, at):
        weights, dscore = scored[pair]
        for slot, coefficients, other in ((0, dscore, band_q_ref), (1, weights, band_g_ref)):
            grad = jnp.dot(coefficients, other[pair], preferred_element_type=F32)
            total_ref[slot, :, at] = own_ref[slot, :, at] + grad

    over_pairs(k_ref.shape[1], finish)


def spread_matrix(first_col):
    shape = (CELLS, SIDE)
    cell = lax.broadcasted_iota(jnp.int32, shape, 0)
    place = lax.broadcasted_iota(jnp.int32, shape, 1)
    return (cell == (place % ROWS) * COLS + first_col + place // ROWS).astype(BF16)


def blend_kernel(total_ref, side_east_ref, blended_ref):
    spread = spread_matrix(0)
    for slot in (0, 1):
        blended_ref[slot] = total_ref[slot] + jnp.dot(spread, side_east_ref[slot], preferred_element_type=F32)


def final_kernel(blended_ref, side_west_ref, dk_ref, dv_ref):
    spread = spread_matrix(COLS - RADIUS)
    for slot, out in ((0, dk_ref), (1, dv_ref)):
        total = blended_ref[slot] + jnp.dot(spread, side_west_ref[slot], preferred_element_type=F32)
        out[...] = total.astype(BF16)


def arr(shape, dtype):
    return jax.ShapeDtypeStruct(shape, dtype)


def call(kernel, name, operands, results, flops=0, **more):
    moved = sum(x.size * x.dtype.itemsize for x in operands)
    return pl.pallas_call(
        kernel,
        out_shape=results,
        compiler_params=pltpu.CompilerParams(vmem_limit_bytes=32 * 1024 * 1024),
        cost_estimate=pl.CostEstimate(flops=flops, bytes_accessed=moved, transcendentals=0),
        name=name,
        **more,
    )(*operands)


def shards(queries, key_cells, value_cells, grad_output, rel_bias):
    block = queries.shape
    heads = rel_bias.shape[0]
    feat = block[-1]
    pairs = feat // PAIR
    cells = arr((CELLS, feat), BF16)
    side, band, corner = (arr((2, rows, feat), BF16) for rows in (SIDE, BAND, 2 * SIDE))
    work = 2 * CELLS * feat
    barrier = lax.optimization_barrier

    def in_hbm(x):
        return pltpu.with_memory_space_constraint(x, pltpu.HBM)

    hbm, vmem = (pl.BlockSpec(memory_space=space) for space in (pltpu.HBM, pltpu.VMEM))
    arguments = [in_hbm(x) for x in (key_cells.reshape(CELLS, feat), value_cells.reshape(CELLS, feat), rel_bias)]
    lon_west, lon_east, k, v, rel_bias = call(
        pack_kernel, "pack", arguments, [side, side, cells, cells, arr(rel_bias.shape, F32)],
        in_specs=[hbm] * 3,
        scratch_shapes=[pltpu.SemaphoreType.DMA((3,))],
    )
    lon_west = ring_shift(lon_west, 1)
    lon_east = ring_shift(lon_east, -1)
    lat_even, lat_odd = call(rows_kernel, "rows", [k, v], [band, band])
    lat_even = pair_exchange(lat_even, "lat", 0, False)
    lat_odd = pair_exchange(lat_odd, "lat", 1, True)

    spread = [pltpu.VMEM((heads, TABLE), F32), pltpu.VMEM((2, heads, 8, TABLE), F32)]
    table, q, g = call(
        bias_kernel, "bias_table",
        [rel_bias, in_hbm(queries.reshape(CELLS, feat)), in_hbm(grad_output.reshape(CELLS, feat))],
        [arr((heads, AROUND, CELLS), F32), cells, cells], heads * AROUND * CELLS,
        in_specs=[vmem, hbm, hbm],
        scratch_shapes=[*spread, pltpu.SemaphoreType.DMA((2,))],
    )

    lon_west, lon_east, table = barrier((lon_west, lon_east, table))
    joined, = call(join_kernel, "join", [lon_west, lon_east], [corner], int(2e9))
    corner_even = pair_exchange(joined, "lat", 0, False)
    corner_odd = odd_rows_exchange(joined)

    def scored(rows):
        return [arr((pairs, rows, 2 * CELLS), F32)] * 2 + [arr((pairs, 8, 2 * CELLS), F32)]

    near = [k, v, lon_west, lon_east, lat_even, lat_odd]
    raised, prob, near_stats = call(near_kernel, "near", [q, g, *near, corner_even, table], scored(EARLY), 4 * work * EARLY)
    late_q, late_g, _ = barrier((q, g, joined))
    queries_even, queries_odd = call(rows_kernel, "query_rows", [late_q, late_g], [band, band])
    band_table, = call(
        band_bias_kernel, "band_table", [rel_bias, queries_odd], [arr((2, heads, LAT_AT, CELLS), F32)],
        2 * heads * LAT_AT * CELLS,
        scratch_shapes=spread,
    )
    table, band_table = barrier((table, band_table))
    queries_even = pair_exchange(queries_even, "lat", 0, False)
    queries_odd = odd_rows_exchange(queries_odd)
    lines = arr((4 * pairs, LANES), F32)
    corner_raised, corner_prob, stats, lines_even, lines_odd = call(
        corner_kernel, "corner", [q, g, corner_odd, table, near_stats],
        scored(AROUND - EARLY) + [lines, arr((2 * lines.shape[0], LANES), F32)], 4 * work * (AROUND - EARLY),
        scratch_shapes=[pltpu.VMEM(lines.shape, F32)],
    )
    lines_even = pair_exchange(lines_even, "lat", 0, False)
    lines_odd = pair_exchange(lines_odd, "lat", 1, True)
    band_scores = [arr((pairs, 2 * SIDE, 4 * CELLS), F32)] * 2
    masked = [arr((pairs, 4 * CELLS, PAIR), BF16)] * 2
    dlon, side_scores, side_prob, band_q, band_g = call(
        side_scores_kernel, "side_scores",
        [q, g, raised, prob, stats, lon_west, lon_east, queries_even, queries_odd, band_table],
        [arr(corner.shape, F32), *band_scores, *masked], 16 * work * SIDE,
    )
    dlon, = call(
        side_even_kernel, "side_even", [dlon, side_scores, side_prob, band_q, band_g, lines_even],
        [arr(corner.shape, F32)], 8 * work * SIDE,
    )
    lines_odd, dlon = barrier((lines_odd, dlon))
    send_west, send_east = call(
        side_band_kernel, "side_band", [dlon, side_scores, side_prob, band_q, band_g, lines_odd], [side, side],
        8 * work * SIDE,
    )
    side_east = ring_shift(send_east, 1)
    side_west = ring_shift(send_west, -1)
    out, dq, own = call(
        own_kernel, "own", [q, g, *near, corner_even, corner_odd, raised, prob, corner_raised, corner_prob, stats],
        [cells, cells, arr((2, CELLS, feat), F32)], 4 * work * AROUND,
    )
    total, = call(
        own_band_kernel, "own_band", [k, v, band_q, band_g, band_table, lines_even, lines_odd, own],
        [arr((2, CELLS, feat), F32)], 8 * work * CELLS,
    )
    blended, = call(blend_kernel, "blend", [total, side_east], [arr((2, CELLS, feat), F32)])
    dk, dv = call(final_kernel, "final", [blended, side_west], [cells, cells])
    return tuple(x.reshape(block) for x in (out, dq, dk, dv))


def solution(mesh):
    spec = P("lat", "lon", None)
    return jax.shard_map(
        shards, mesh=mesh, in_specs=(spec, spec, spec, spec, P()), out_specs=(spec,) * 4, check_vma=False
    )
```

```python
import functools

import jax
import jax.numpy as jnp
from jax import lax
from jax.experimental import pallas as pl
from jax.experimental.pallas import tpu as pltpu
from jax.sharding import PartitionSpec as P

HEAD_DIM = 64
RADIUS = 6
SPAN = 2 * RADIUS + 1
ROWS = 8
COLS = 16
CELLS = ROWS * COLS
SIDE = ROWS * RADIUS
BAND = RADIUS * COLS
PAIR = 2 * HEAD_DIM
BASE = 336
TABLE = 512
MASKED = -1e30

OWN_AT = 0
LON_AT = CELLS
LAT_AT = LON_AT + 2 * SIDE
NEAR = LAT_AT + 2 * BAND
EARLY = NEAR + 2 * SIDE
AROUND = EARLY + 2 * SIDE
LANES = 128

F32 = jnp.float32
BF16 = jnp.bfloat16


def pair_exchange(value, axis, odd, wrap):
    count = lax.axis_size(axis)
    pairs = []
    for first in range(odd, count, 2):
        second = first + 1
        if second >= count and not wrap:
            continue
        second %= count
        pairs += [(first, second), (second, first)]
    return lax.ppermute(value, axis, pairs)


def ring_shift(value, by):
    count = lax.axis_size("lon")
    return lax.ppermute(value, "lon", [(lon, (lon + by) % count) for lon in range(count)])


def odd_rows_exchange(value):
    lats, lons = lax.axis_size("lat"), lax.axis_size("lon")
    pairs = []
    for lat in range(lats):
        for lon in range(lons):
            other = lat + 1 if lat % 2 else lat - 1
            inside = 0 <= other < lats
            target = (other, lon) if inside else (lat, lon ^ (1 if lons % 4 else 2))
            pairs.append((lat * lons + lon, target[0] * lons + target[1]))
    return lax.ppermute(value, ("lat", "lon"), pairs)


def is_odd(axis):
    return lax.axis_index(axis) % 2 == 1


def pick_matrix(first_col):
    shape = (SIDE, CELLS)
    place = lax.broadcasted_iota(jnp.int32, shape, 0)
    cell = lax.broadcasted_iota(jnp.int32, shape, 1)
    source = (place % ROWS) * COLS + first_col + place // ROWS
    return (cell == source).astype(BF16)


def pack_kernel(k_hbm, v_hbm, bias_hbm, lon_west_ref, lon_east_ref, k_ref, v_ref, bias_ref, sems):
    copies = [
        pltpu.make_async_copy(source, target, sems.at[index])
        for index, (source, target) in enumerate(((k_hbm, k_ref), (v_hbm, v_ref), (bias_hbm, bias_ref)))
    ]
    for copy in copies:
        copy.start()
    picks = jnp.concatenate([pick_matrix(first_col) for first_col in (COLS - RADIUS, 0)], axis=0)
    for slot, source in ((0, k_ref), (1, v_ref)):
        copies[slot].wait()
        both = jnp.dot(picks, source[...], preferred_element_type=F32).astype(BF16)
        lon_west_ref[slot] = both[:SIDE]
        lon_east_ref[slot] = both[SIDE:]
    copies[2].wait()


def lat_starts():
    lat_odd = is_odd("lat")
    even = jnp.where(lat_odd, 0, CELLS - BAND)
    return pl.multiple_of(even, 32), pl.multiple_of(CELLS - BAND - even, 32)


def rows_kernel(k_ref, v_ref, lat_even_ref, lat_odd_ref):
    for start, out in zip(lat_starts(), (lat_even_ref, lat_odd_ref)):
        out[0] = k_ref[pl.ds(start, BAND), :]
        out[1] = v_ref[pl.ds(start, BAND), :]


def bias_lines(bias_ref, line_ref):
    offset = BASE - lax.broadcasted_iota(jnp.int32, (1, TABLE), 1)
    row, col = offset // COLS, offset % COLS
    valid = (offset >= 0) & (row < SPAN) & (col < SPAN)
    entry = lax.broadcasted_iota(jnp.int32, (SPAN * SPAN, TABLE), 0)
    chosen = jnp.where(entry == jnp.where(valid, row * SPAN + col, -1), 1.0, 0.0).astype(BF16)
    rest = bias_ref[...]
    total = jnp.zeros((rest.shape[0], TABLE), F32)
    for _ in range(3):
        part = rest.astype(BF16)
        total = total + jnp.dot(part, chosen, preferred_element_type=F32)
        rest = rest - part.astype(F32)
    line_ref[...] = jnp.where(valid, total, MASKED)


def spread_rows(line_ref, spread_ref):
    heads = line_ref.shape[0]
    lines = [jnp.broadcast_to(line_ref[head : head + 1], (8, TABLE)) for head in range(heads)]
    x = jnp.concatenate(lines, axis=0)
    sub = lax.broadcasted_iota(jnp.int32, x.shape, 0)
    for index, stride in enumerate((1, COLS)):
        turned = x
        for bit in (1, 2, 4):
            turned = jnp.where((sub & bit) != 0, pltpu.roll(turned, bit * stride, 1), turned)
        for head in range(heads):
            spread_ref[index, head] = turned[8 * head : 8 * head + 8]


def windows(source, col, rows):
    firsts = [BASE - (COLS * row + col) for row in rows]
    turn = firsts[0] % LANES
    turned = pltpu.roll(source, TABLE - turn, 1) if turn else source
    return [turned[:, first - turn : first - turn + CELLS] for first in firsts]


def near(delta, there=None):
    allowed = (delta >= 0) & (delta < SPAN)
    return allowed if there is None else allowed & there


def places():
    north_slot = jnp.where(is_odd("lat"), 0, 1)
    has_north = lax.axis_index("lat") > 0
    has_south = lax.axis_index("lat") < lax.axis_size("lat") - 1
    sides = ((0, 0), (COLS + RADIUS, SIDE))
    own_col = lax.broadcasted_iota(jnp.int32, (8, CELLS), 1) % COLS
    sub = lax.broadcasted_iota(jnp.int32, (8, CELLS), 0)
    return sides, north_slot, 1 - north_slot, has_north, has_south, own_col, sub


def bias_kernel(bias_ref, q_hbm, g_hbm, table_ref, q_ref, g_ref, line_ref, spread_ref, sems):
    copies = [
        pltpu.make_async_copy(source, target, sems.at[index])
        for index, (source, target) in enumerate(((q_hbm, q_ref), (g_hbm, g_ref)))
    ]
    for copy in copies:
        copy.start()
    bias_lines(bias_ref, line_ref)
    spread_rows(line_ref, spread_ref)
    sides, north_slot, south_slot, has_north, has_south, own_col, sub = places()

    def fill(head, carry):
        def put(at, values, allowed):
            table_ref[head, pl.ds(pl.multiple_of(at, 8), 8), :] = jnp.where(allowed, values, MASKED)

        by_one = spread_ref[0, head]
        for half in range(COLS // 8):
            delta = RADIUS + 8 * half + sub - own_col
            own, north, south = near(delta), near(delta, has_north), near(delta, has_south)
            for step in range(8):
                rows = [row for row in (step, step + 8, step + 16) if row < 2 * RADIUS + ROWS]
                for row, values in zip(rows, windows(by_one, RADIUS + 8 * half, rows)):
                    if row < RADIUS:
                        put(LAT_AT + north_slot * BAND + row * COLS + 8 * half, values, north)
                    elif row < RADIUS + ROWS:
                        put(OWN_AT + (row - RADIUS) * COLS + 8 * half, values, own)
                    else:
                        put(LAT_AT + south_slot * BAND + (row - RADIUS - ROWS) * COLS + 8 * half, values, south)
        by_row = spread_ref[1, head]
        rows = (RADIUS - ROWS, RADIUS, RADIUS + ROWS)
        for first_col, lon_slot in sides:
            for step in range(RADIUS):
                delta = first_col + step - own_col
                above, beside, below = windows(by_row, first_col + step, rows)
                at = lon_slot + step * ROWS
                put(LON_AT + at, beside, near(delta))
                put(NEAR + north_slot * 2 * SIDE + at, above, near(delta, has_north))
                put(NEAR + south_slot * 2 * SIDE + at, below, near(delta, has_south))
        return carry

    lax.fori_loop(0, bias_ref.shape[0], fill, 0, unroll=4)
    for copy in copies:
        copy.wait()


def band_bias_kernel(bias_ref, after_ref, table_ref, line_ref, spread_ref):
    del after_ref
    bias_lines(bias_ref, line_ref)
    spread_rows(line_ref, spread_ref)
    sides, north_slot, south_slot, has_north, has_south, own_col, sub = places()
    lane = lax.broadcasted_iota(jnp.int32, (8, CELLS), 1)
    bands = ((north_slot, RADIUS, has_north & (lane < BAND)), (south_slot, -ROWS, has_south & (lane < BAND)))

    def fill(head, carry):
        def put(slot, at, values, allowed):
            table_ref[slot, head, pl.ds(pl.multiple_of(at, 8), 8), :] = jnp.where(allowed, values, MASKED)

        by_one = spread_ref[0, head]
        for half in range(COLS // 8):
            delta = RADIUS + 8 * half + sub - own_col
            masks = [near(delta, there) for _, _, there in bands]
            for step in range(ROWS):
                rows = [next(row for row in range(ROWS) if (RADIUS + row + shift - step) % 8 == 0) for _, shift, _ in bands]
                found = windows(by_one, RADIUS + 8 * half, [RADIUS + row + band[1] for row, band in zip(rows, bands)])
                for row, band, mask, values in zip(rows, bands, masks, found):
                    put(band[0], OWN_AT + row * COLS + 8 * half, values, mask)
        by_row = spread_ref[1, head]
        for slot, shift, there in bands:
            for first_col, lon_slot in sides:
                for step in range(RADIUS):
                    (values,) = windows(by_row, first_col + step, (RADIUS + shift,))
                    put(slot, LON_AT + lon_slot + step * ROWS, values, near(first_col + step - own_col, there))
        return carry

    lax.fori_loop(0, bias_ref.shape[0], fill, 0, unroll=8)


LAST = (((1,), (1,)), ((), ()))
FACTOR = HEAD_DIM ** (-0.5)


def join_kernel(lon_west_ref, lon_east_ref, out_ref):
    out_ref[:, :SIDE] = lon_west_ref[...]
    out_ref[:, SIDE:] = lon_east_ref[...]


def over_pairs(width, body):
    return [body(pair, pl.ds(pair * PAIR, PAIR)) for pair in range(width // PAIR)]


def stacked(slot, at, own_ref, *refs):
    return jnp.concatenate([own_ref[:, at]] + [ref[slot, :, at] for ref in refs], axis=0)


def both_heads(block):
    first_head = lax.broadcasted_iota(jnp.int32, block.shape, 1) < HEAD_DIM
    zero = jnp.zeros_like(block)
    return jnp.concatenate([jnp.where(first_head, block, zero), jnp.where(first_head, zero, block)], axis=0)


def scaled(block):
    return both_heads(block * jnp.asarray(FACTOR, BF16))


def two_tables(table_ref, pair, rows):
    return jnp.concatenate([table_ref[2 * pair, rows], table_ref[2 * pair + 1, rows]], axis=1)


def times(left, right):
    return lax.dot_general(left, right, LAST, preferred_element_type=F32)


def column_sum(x):
    return jnp.sum(x, axis=0, keepdims=True)


def rounded_dot(probability, grad_prob):
    return column_sum(probability.astype(BF16).astype(F32) * grad_prob)


def score_gradient(probability, grad_prob, row_dot):
    return probability.astype(BF16), (probability * (grad_prob - row_dot)).astype(BF16)


def near_kernel(
    q_ref, g_ref, k_ref, v_ref, lon_west_ref, lon_east_ref, lat_even_ref, lat_odd_ref, corner_even_ref, table_ref,
    raised_ref, prob_ref, stats_ref,
):
    parts = (lon_west_ref, lon_east_ref, lat_even_ref, lat_odd_ref, corner_even_ref)

    def body(pair, at):
        scores = times(stacked(0, at, k_ref, *parts), scaled(q_ref[:, at])) + two_tables(table_ref, pair, pl.ds(0, EARLY))
        grad_prob = times(stacked(1, at, v_ref, *parts), both_heads(g_ref[:, at]))
        largest = jnp.max(scores, axis=0, keepdims=True)
        raised = jnp.exp(scores - largest)
        total = column_sum(raised)
        raised_ref[pair] = raised
        prob_ref[pair] = grad_prob
        stats_ref[pair, 0:1] = largest
        stats_ref[pair, 1:2] = total
        log_total = largest + jnp.log(total)
        stats_ref[pair, 2:3] = rounded_dot(raised * jnp.exp(largest - log_total), grad_prob)
        stats_ref[pair, 3:4] = log_total

    over_pairs(q_ref.shape[1], body)


def corner_kernel(
    q_ref, g_ref, corner_ref, table_ref, near_stats_ref, raised_ref, prob_ref, stats_ref, send_even_ref, send_odd_ref, lines_ref
):
    def score(pair, at):
        scores = times(corner_ref[0, :, at], scaled(q_ref[:, at])) + two_tables(table_ref, pair, pl.ds(EARLY, AROUND - EARLY))
        return scores, times(corner_ref[1, :, at], both_heads(g_ref[:, at]))

    scored = over_pairs(q_ref.shape[1], score)
    for pair, (scores, grad_prob) in enumerate(scored):
        near_largest = near_stats_ref[pair, 0:1]
        largest = jnp.maximum(near_largest, jnp.max(scores, axis=0, keepdims=True))
        raised = jnp.exp(scores - largest)
        shift = jnp.exp(near_largest - largest)
        total = near_stats_ref[pair, 1:2] * shift + column_sum(raised)
        log_total = largest + jnp.log(total)
        scale = jnp.exp(largest - log_total)
        near_scale = jnp.exp(near_largest - log_total)
        row_dot = near_stats_ref[pair, 2:3] * jnp.exp(near_stats_ref[pair, 3:4] - log_total)
        row_dot = row_dot + rounded_dot(raised * scale, grad_prob)
        raised_ref[pair] = raised
        prob_ref[pair] = grad_prob
        stats_ref[pair, 0:1] = near_scale
        stats_ref[pair, 1:2] = row_dot
        stats_ref[pair, 2:3] = scale
        for index, line in enumerate((log_total, row_dot)):
            for head in (0, 1):
                at = 4 * pair + 2 * index + head
                lines_ref[at : at + 1] = line[:, head * CELLS : (head + 1) * CELLS]
    lines = lines_ref[...]
    low_rows = pltpu.roll(lines, BAND, 1)
    lat_odd = is_odd("lat")
    send_even_ref[...] = jnp.where(lat_odd, lines, low_rows)
    odd_lines = jnp.where(lat_odd, low_rows, lines)
    send_odd_ref[...] = jnp.concatenate([odd_lines] * (send_odd_ref.shape[0] // lines.shape[0]), axis=0)


def near_gradient(raised_ref, prob_ref, stats_ref, pair, rows):
    return score_gradient(raised_ref[pair, rows] * stats_ref[pair, 0:1], prob_ref[pair, rows], stats_ref[pair, 1:2])


def band_lines(lines_refs, pair):
    def row(first):
        return jnp.concatenate([ref[line : line + 1] for ref in lines_refs for line in (first, first + 1)], axis=1)

    return row(4 * pair), row(4 * pair + 2)


def band_queries(queries_refs, slot, at, prepare):
    empty = jnp.zeros((CELLS - BAND, PAIR), BF16)
    return jnp.concatenate([prepare(jnp.concatenate([ref[slot, :, at], empty], axis=0)) for ref in queries_refs], axis=0)


def band_tables(table_ref, pair, rows):
    return jnp.concatenate([table_ref[slot, 2 * pair + head, rows] for slot in (0, 1) for head in (0, 1)], axis=1)


def side_scores_kernel(
    q_ref, g_ref, raised_ref, prob_ref, stats_ref, lon_west_ref, lon_east_ref, queries_even_ref, queries_odd_ref, table_ref,
    dlon_ref, scores_ref, prob_out_ref, band_q_ref, band_g_ref,
):
    queries_refs = (queries_even_ref, queries_odd_ref)

    def body(pair, at):
        keys, values = (
            jnp.concatenate([lon_west_ref[slot, :, at], lon_east_ref[slot, :, at]], axis=0) for slot in (0, 1)
        )
        queries = band_queries(queries_refs, 0, at, scaled)
        grads = band_queries(queries_refs, 1, at, both_heads)
        band_q_ref[pair] = queries
        band_g_ref[pair] = grads
        scores_ref[pair] = times(keys, queries) + band_tables(table_ref, pair, pl.ds(LON_AT, 2 * SIDE))
        prob_out_ref[pair] = times(values, grads)
        weights, dscore = near_gradient(raised_ref, prob_ref, stats_ref, pair, pl.ds(LON_AT, LAT_AT - LON_AT))
        dlon_ref[0, :, at] = jnp.dot(dscore, scaled(q_ref[:, at]), preferred_element_type=F32)
        dlon_ref[1, :, at] = jnp.dot(weights, both_heads(g_ref[:, at]), preferred_element_type=F32)

    over_pairs(q_ref.shape[1], body)


def side_terms(pair, at, lanes, scores_ref, prob_ref, lines_ref, band_q_ref, band_g_ref):
    log_total, row_dot = band_lines((lines_ref,), pair)
    weights, dscore = score_gradient(
        jnp.exp(scores_ref[pair, :, lanes] - log_total), prob_ref[pair, :, lanes], row_dot
    )
    return [
        jnp.dot(coefficients, other[pair, lanes], preferred_element_type=F32)
        for coefficients, other in ((dscore, band_q_ref), (weights, band_g_ref))
    ]


def side_even_kernel(dlon_ref, scores_ref, prob_ref, band_q_ref, band_g_ref, lines_ref, sum_ref):
    def body(pair, at):
        terms = side_terms(pair, at, pl.ds(0, 2 * CELLS), scores_ref, prob_ref, lines_ref, band_q_ref, band_g_ref)
        for slot, term in enumerate(terms):
            sum_ref[slot, :, at] = dlon_ref[slot, :, at] + term

    over_pairs(dlon_ref.shape[2], body)


def side_band_kernel(
    sum_ref, scores_ref, prob_ref, band_q_ref, band_g_ref, lines_ref, send_odd_ref, send_even_ref
):
    def body(pair, at):
        return side_terms(
            pair, at, pl.ds(2 * CELLS, 2 * CELLS), scores_ref, prob_ref, lines_ref, band_q_ref, band_g_ref
        )

    for pair, terms in enumerate(over_pairs(sum_ref.shape[2], body)):
        at = pl.ds(pair * PAIR, PAIR)
        for slot, term in enumerate(terms):
            total = (sum_ref[slot, :, at] + term).astype(BF16)
            send_odd_ref[slot, :, at] = total[:SIDE]
            send_even_ref[slot, :, at] = total[SIDE:]


def own_kernel(
    q_ref, g_ref, k_ref, v_ref, lon_west_ref, lon_east_ref, lat_even_ref, lat_odd_ref, corner_even_ref, corner_odd_ref,
    raised_ref, prob_ref, corner_raised_ref, corner_prob_ref, stats_ref, out_ref, dq_ref, own_ref,
):
    parts = (lon_west_ref, lon_east_ref, lat_even_ref, lat_odd_ref, corner_even_ref, corner_odd_ref)

    def per_query(cells, coefficients):
        turned = jnp.dot(cells.T, coefficients, preferred_element_type=F32)
        mine = jnp.concatenate([turned[:HEAD_DIM, :CELLS], turned[HEAD_DIM:, CELLS:]], axis=0)
        return mine.T

    def body(pair, at):
        nearby = near_gradient(raised_ref, prob_ref, stats_ref, pair, pl.ds(0, EARLY))
        far = score_gradient(
            corner_raised_ref[pair] * stats_ref[pair, 2:3], corner_prob_ref[pair], stats_ref[pair, 1:2]
        )
        weights, dscore = (jnp.concatenate(x, axis=0) for x in zip(nearby, far))
        own_ref[0, :, at] = jnp.dot(dscore[:LON_AT], scaled(q_ref[:, at]), preferred_element_type=F32)
        own_ref[1, :, at] = jnp.dot(weights[:LON_AT], both_heads(g_ref[:, at]), preferred_element_type=F32)
        out_ref[:, at] = per_query(stacked(1, at, v_ref, *parts), weights).astype(BF16)
        dq_ref[:, at] = (per_query(stacked(0, at, k_ref, *parts), dscore) * FACTOR).astype(BF16)

    over_pairs(q_ref.shape[1], body)


def own_band_kernel(
    k_ref, v_ref, band_q_ref, band_g_ref, table_ref, lines_even_ref, lines_odd_ref, own_ref, total_ref
):
    def score(pair, at):
        log_total, row_dot = band_lines((lines_even_ref, lines_odd_ref), pair)
        scores = times(k_ref[:, at], band_q_ref[pair]) + band_tables(table_ref, pair, pl.ds(OWN_AT, CELLS))
        return score_gradient(jnp.exp(scores - log_total), times(v_ref[:, at], band_g_ref[pair]), row_dot)

    scored = over_pairs(k_ref.shape[1], score)

    def finish(pair, at):
        weights, dscore = scored[pair]
        for slot, coefficients, other in ((0, dscore, band_q_ref), (1, weights, band_g_ref)):
            grad = jnp.dot(coefficients, other[pair], preferred_element_type=F32)
            total_ref[slot, :, at] = own_ref[slot, :, at] + grad

    over_pairs(k_ref.shape[1], finish)


def spread_matrix(first_col):
    shape = (CELLS, SIDE)
    cell = lax.broadcasted_iota(jnp.int32, shape, 0)
    place = lax.broadcasted_iota(jnp.int32, shape, 1)
    return (cell == (place % ROWS) * COLS + first_col + place // ROWS).astype(BF16)


def final_kernel(total_ref, side_east_ref, side_west_ref, dk_ref, dv_ref):
    spread = jnp.concatenate([spread_matrix(0), spread_matrix(COLS - RADIUS)], axis=1)
    for slot, out in ((0, dk_ref), (1, dv_ref)):
        sides = jnp.concatenate([side_east_ref[slot], side_west_ref[slot]], axis=0)
        out[...] = (total_ref[slot] + jnp.dot(spread, sides, preferred_element_type=F32)).astype(BF16)


def arr(shape, dtype):
    return jax.ShapeDtypeStruct(shape, dtype)


def call(kernel, name, operands, results, flops=0, **more):
    moved = sum(x.size * x.dtype.itemsize for x in operands)
    return pl.pallas_call(
        kernel,
        out_shape=results,
        compiler_params=pltpu.CompilerParams(vmem_limit_bytes=32 * 1024 * 1024),
        cost_estimate=pl.CostEstimate(flops=flops, bytes_accessed=moved, transcendentals=0),
        name=name,
        **more,
    )(*operands)


def shards(queries, key_cells, value_cells, grad_output, rel_bias):
    block = queries.shape
    heads = rel_bias.shape[0]
    feat = block[-1]
    pairs = feat // PAIR
    cells = arr((CELLS, feat), BF16)
    side, band, corner = (arr((2, rows, feat), BF16) for rows in (SIDE, BAND, 2 * SIDE))
    work = 2 * CELLS * feat
    barrier = lax.optimization_barrier

    def in_hbm(x):
        return pltpu.with_memory_space_constraint(x, pltpu.HBM)

    hbm, vmem = (pl.BlockSpec(memory_space=space) for space in (pltpu.HBM, pltpu.VMEM))
    arguments = [in_hbm(x) for x in (key_cells.reshape(CELLS, feat), value_cells.reshape(CELLS, feat), rel_bias)]
    lon_west, lon_east, k, v, rel_bias = call(
        pack_kernel, "pack", arguments, [side, side, cells, cells, arr(rel_bias.shape, F32)],
        in_specs=[hbm] * 3,
        scratch_shapes=[pltpu.SemaphoreType.DMA((3,))],
    )
    lon_west = ring_shift(lon_west, 1)
    lon_east = ring_shift(lon_east, -1)
    lat_even, lat_odd = call(rows_kernel, "rows", [k, v], [band, band])
    lat_even = pair_exchange(lat_even, "lat", 0, False)
    lat_odd = pair_exchange(lat_odd, "lat", 1, True)

    spread = [pltpu.VMEM((heads, TABLE), F32), pltpu.VMEM((2, heads, 8, TABLE), F32)]
    table, q, g = call(
        bias_kernel, "bias_table",
        [rel_bias, in_hbm(queries.reshape(CELLS, feat)), in_hbm(grad_output.reshape(CELLS, feat))],
        [arr((heads, AROUND, CELLS), F32), cells, cells], heads * AROUND * CELLS,
        in_specs=[vmem, hbm, hbm],
        scratch_shapes=[*spread, pltpu.SemaphoreType.DMA((2,))],
    )

    lon_west, lon_east, table = barrier((lon_west, lon_east, table))
    joined, = call(join_kernel, "join", [lon_west, lon_east], [corner], int(2e9))
    corner_even = pair_exchange(joined, "lat", 0, False)
    corner_odd = odd_rows_exchange(joined)

    def scored(rows):
        return [arr((pairs, rows, 2 * CELLS), F32)] * 2 + [arr((pairs, 8, 2 * CELLS), F32)]

    near = [k, v, lon_west, lon_east, lat_even, lat_odd]
    raised, prob, near_stats = call(near_kernel, "near", [q, g, *near, corner_even, table], scored(EARLY), 4 * work * EARLY)
    late_q, late_g, _ = barrier((q, g, joined))
    queries_even, queries_odd = call(rows_kernel, "query_rows", [late_q, late_g], [band, band])
    band_table, = call(
        band_bias_kernel, "band_table", [rel_bias, queries_odd], [arr((2, heads, LAT_AT, CELLS), F32)],
        2 * heads * LAT_AT * CELLS,
        scratch_shapes=spread,
    )
    table, band_table = barrier((table, band_table))
    queries_even = pair_exchange(queries_even, "lat", 0, False)
    queries_odd = odd_rows_exchange(queries_odd)
    lines = arr((4 * pairs, LANES), F32)
    corner_raised, corner_prob, stats, lines_even, lines_odd = call(
        corner_kernel, "corner", [q, g, corner_odd, table, near_stats],
        scored(AROUND - EARLY) + [lines, arr((2 * lines.shape[0], LANES), F32)], 4 * work * (AROUND - EARLY),
        scratch_shapes=[pltpu.VMEM(lines.shape, F32)],
    )
    lines_even = pair_exchange(lines_even, "lat", 0, False)
    lines_odd = pair_exchange(lines_odd, "lat", 1, True)
    band_scores = [arr((pairs, 2 * SIDE, 4 * CELLS), F32)] * 2
    masked = [arr((pairs, 4 * CELLS, PAIR), BF16)] * 2
    dlon, side_scores, side_prob, band_q, band_g = call(
        side_scores_kernel, "side_scores",
        [q, g, raised, prob, stats, lon_west, lon_east, queries_even, queries_odd, band_table],
        [arr(corner.shape, F32), *band_scores, *masked], 16 * work * SIDE,
    )
    dlon, = call(
        side_even_kernel, "side_even", [dlon, side_scores, side_prob, band_q, band_g, lines_even],
        [arr(corner.shape, F32)], 8 * work * SIDE,
    )
    lines_odd, dlon = barrier((lines_odd, dlon))
    send_west, send_east = call(
        side_band_kernel, "side_band", [dlon, side_scores, side_prob, band_q, band_g, lines_odd], [side, side],
        8 * work * SIDE,
    )
    side_east = ring_shift(send_east, 1)
    side_west = ring_shift(send_west, -1)
    out, dq, own = call(
        own_kernel, "own", [q, g, *near, corner_even, corner_odd, raised, prob, corner_raised, corner_prob, stats],
        [cells, cells, arr((2, CELLS, feat), F32)], 4 * work * AROUND,
    )
    total, = call(
        own_band_kernel, "own_band", [k, v, band_q, band_g, band_table, lines_even, lines_odd, own],
        [arr((2, CELLS, feat), F32)], 8 * work * CELLS,
    )
    dk, dv = call(final_kernel, "final", [total, side_east, side_west], [cells, cells])
    return tuple(x.reshape(block) for x in (out, dq, dk, dv))


def solution(mesh):
    spec = P("lat", "lon", None)
    return jax.shard_map(
        shards, mesh=mesh, in_specs=(spec, spec, spec, spec, P()), out_specs=(spec,) * 4, check_vma=False
    )
```
